32 devices in a mesh: dp: 16 (over z, x, core), tensor: 2 (over y).
Axes of the slice: x: 2, y: 2, z: 4, core: 2. Of those that a mesh axis runs over, the one named last changes fastest.
Arguments:
- layer_in: float32 [32768, 768], P(('dp', 'tensor')), may hold values from -6 to 6
- qkv_weight: bfloat16 [768, 2304], P(None, 'tensor'), may hold values from -0.21875 to 0.21875
- qkv_bias: float32 [2304], P('tensor'), may hold values from -2 to 2
- key_scorer: float32 [768], P('tensor'), may hold values from -2 to 2
- out_weight: bfloat16 [768, 768], P('tensor'), may hold values from -0.875 to 0.875
- out_bias: float32 [768], replicated, may hold values from -2 to 2
- fc_weight: bfloat16 [768, 3072], P(None, 'tensor'), may hold values from -0.21875 to 0.21875
- fc_bias: float32 [3072], P('tensor'), may hold values from -2 to 2
- proj_weight: bfloat16 [3072, 768], P('tensor'), may hold values from -0.109375 to 0.109375
- proj_bias: float32 [768], replicated, may hold values from -2 to 2
- norm1_gain: float32 [768], replicated, may hold values from 0.5 to 1.5
- norm1_shift: float32 [768], replicated, may hold values from -2 to 2
- norm2_gain: float32 [768], replicated, may hold values from 0.5 to 1.5
- norm2_shift: float32 [768], replicated, may hold values from -2 to 2
- key_index: int32 [32768, 64], P('dp'), may hold values from -1 to 2046, as said below
- key_count: int32 [32768], P('dp'), may hold values from 0 to 64, as said below
- out_grad: float32 [32768, 768], P(('dp', 'tensor')), may hold values from -18 to 18
Outputs:
- layer_out: float32 [32768, 768], P(('dp', 'tensor'))
- input_grad: float32 [32768, 768], P(('dp', 'tensor'))
- grad_qkv_weight: float32 [768, 2304], P(None, 'tensor')
- grad_qkv_bias: float32 [2304], P('tensor')
- grad_key_scorer: float32 [768], P('tensor')
- grad_out_weight: float32 [768, 768], P('tensor')
- grad_out_bias: float32 [768], replicated
- grad_fc_weight: float32 [768, 3072], P(None, 'tensor')
- grad_fc_bias: float32 [3072], P('tensor')
- grad_proj_weight: float32 [3072, 768], P('tensor')
- grad_proj_bias: float32 [768], replicated
- grad_norm1_gain: float32 [768], replicated
- grad_norm1_shift: float32 [768], replicated
- grad_norm2_gain: float32 [768], replicated
- grad_norm2_shift: float32 [768], replicated
The draws below stay inside these ranges and needn't reach their ends.
Inputs may be any that keep to these rules, and one draw needn't show every extreme that they name: `key_index`: for a token at position p of its sequence, slots 0 to min(64, p) - 1 hold distinct positions below p of the same sequence, slot 0 holding p - 1; the other slots hold -1. At position p, key_count lies between (min(64, p) + 1) // 2 and min(64, p), and equals min(64, p) at the last position of every sequence.
All inputs are finite; a program needn't handle non-finite values.
Results may differ from the reference program's by a relative error of at most 0.014.
Values may be sent and summed in bfloat16 or wider, within the bound.
No kernel may reach another device: no remote copies, remote signals or barrier semaphores. Data moves between devices by JAX's collectives and lax.ppermute only.
A program may use at most 256 MiB of HBM per device.

```python
import math
from functools import partial
import jax
import jax.numpy as jnp
from jax import lax

D = 768
H = 12
HD = 64
FF = 3072
TOPK = 64
WIN = 64
QBLK = 512
SEQ = 2048
TOKENS = 32768


def draw_key_index(key, part):
    key = jax.random.fold_in(key, 11)
    seq_total = TOKENS // SEQ
    key_pos = jnp.arange(SEQ, dtype=jnp.int32)

    def one_sequence(seq_key):
        ranking = jax.random.randint(seq_key, (SEQ, SEQ), 0, 1 << 17)
        ranked = ranking * SEQ + key_pos[None, :]
        ranked = jnp.where(key_pos[None, :] == key_pos[:, None] - 1, 1 << 30, ranked)
        ranked = jnp.where(key_pos[None, :] >= key_pos[:, None], -1, ranked)
        top_values, top_slots = lax.top_k(ranked, TOPK)
        return jnp.where(top_values >= 0, top_slots, -1).astype(jnp.int32)
    seq_keys = jax.random.split(key, seq_total)
    return lax.map(one_sequence, seq_keys).reshape(TOKENS, TOPK)


def draw_key_count(key, part):
    key = jax.random.fold_in(key, 23)
    position = jnp.arange(TOKENS, dtype=jnp.int32) % SEQ
    upper = jnp.minimum(position, TOPK)
    lower = (upper + 1) // 2
    drawn = jax.random.randint(key, (TOKENS,), lower, upper + 1)
    return jnp.where(position == SEQ - 1, upper, drawn).astype(jnp.int32)


def draw_out_grad(key, part):
    key = jax.random.fold_in(key, 37)
    row_place = jnp.arange(TOKENS, dtype=jnp.float32) / TOKENS
    row_scale = jnp.exp(row_place * math.log(3.0))[:, None]
    samples = jnp.clip(jax.random.normal(key, (TOKENS, D), jnp.float32), -6.0, 6.0)
    return samples * row_scale


def steps_of(key, dims, cuts, least, high):
    level, own = 1.0, jax.random.fold_in(key, 6)
    for axis_at, parts in cuts:
        heights = jnp.exp(jax.random.uniform(jax.random.fold_in(own, axis_at), (parts,), jnp.float32, least / len(cuts), high / len(cuts)))
        level = level * jnp.repeat(heights, dims[axis_at] // parts).reshape([-1 if axis == axis_at else 1 for axis in range(len(dims))])
    return level


def centred(own_key, shape, scale, bound, cuts=(), kind=jnp.bfloat16):
    values = jax.random.normal(own_key, shape, jnp.float32) * scale
    if len(cuts) > 0:
        values = steps_of(own_key, shape, cuts, -0.22, 0.18) * values
    return jnp.clip(values, min=-bound, max=bound).astype(kind)


def setup_inputs(seed: int = 0) -> dict:
    arg_keys = jax.random.split(jax.random.key(seed), 18)
    layer_in = centred(arg_keys[0], (TOKENS, D), 1.0, 6.0, ((0, 32),), jnp.float32)
    qkv_weight = centred(arg_keys[1], (D, 3 * D), D ** -0.5, 0.21875, ((1, 2),))
    qkv_bias = centred(arg_keys[2], (3 * D,), 0.3, 2.0, ((0, 2),), jnp.float32)
    key_scorer = centred(arg_keys[3], (D,), 0.3, 2.0, ((0, 2),), jnp.float32)
    out_weight = centred(arg_keys[4], (D, D), (D // 16) ** -0.5, 0.875, ((0, 2),))
    out_bias = centred(arg_keys[5], (D,), 0.3, 2.0, (), jnp.float32)
    fc_weight = centred(arg_keys[6], (D, FF), D ** -0.5, 0.21875, ((1, 2),))
    fc_bias = centred(arg_keys[7], (FF,), 0.3, 2.0, ((0, 2),), jnp.float32)
    proj_weight = centred(arg_keys[8], (FF, D), FF ** -0.5, 0.109375, ((0, 2),))
    proj_bias = centred(arg_keys[9], (D,), 0.3, 2.0, (), jnp.float32)
    norm1_gain = jnp.clip(1.0 + 0.1 * jax.random.normal(arg_keys[10], (D,), jnp.float32), 0.5, 1.5)
    norm1_shift = centred(arg_keys[11], (D,), 0.3, 2.0, (), jnp.float32)
    norm2_gain = jnp.clip(1.0 + 0.1 * jax.random.normal(arg_keys[12], (D,), jnp.float32), 0.5, 1.5)
    norm2_shift = centred(arg_keys[13], (D,), 0.3, 2.0, (), jnp.float32)
    key_index = draw_key_index(jax.random.fold_in(arg_keys[17], 71), 0)
    key_count = draw_key_count(jax.random.fold_in(arg_keys[17], 71), 0)
    out_grad = draw_out_grad(jax.random.fold_in(arg_keys[17], 71), 0)
    return {"layer_in": layer_in, "qkv_weight": qkv_weight, "qkv_bias": qkv_bias, "key_scorer": key_scorer, "out_weight": out_weight, "out_bias": out_bias, "fc_weight": fc_weight, "fc_bias": fc_bias, "proj_weight": proj_weight, "proj_bias": proj_bias, "norm1_gain": norm1_gain, "norm1_shift": norm1_shift, "norm2_gain": norm2_gain, "norm2_shift": norm2_shift, "key_index": key_index, "key_count": key_count, "out_grad": out_grad}


HIGHEST = lax.Precision.HIGHEST

@jax.custom_vjp
def low(v):
    return lax.optimization_barrier(v.astype(jnp.bfloat16)).astype(jnp.float32)

@jax.custom_vjp
def low_back(v):
    return v

def low_keep(v):
    return (low(v), None)

def low_pass(kept, grad):
    return (grad,)

def back_keep(v):
    return (v, None)

def back_low(kept, grad):
    return (low(grad),)
low.defvjp(low_keep, low_pass)
low_back.defvjp(back_keep, back_low)

def layer_norm(inputs, norm_gain, norm_shift):
    center = inputs - lax.optimization_barrier(jnp.mean(inputs, axis=-1, keepdims=True))
    variance = lax.optimization_barrier(jnp.mean(center * center, axis=-1, keepdims=True))
    return center * lax.rsqrt(variance + 1e-05) * norm_gain + norm_shift

def block_mask(index_rows, count_rows, first_pos, seq_len):
    row_total = index_rows.shape[0]
    query_pos = first_pos + jnp.arange(row_total, dtype=jnp.int32)
    key_pos = jnp.arange(seq_len, dtype=jnp.int32)
    window_hit = (key_pos[None, :] <= query_pos[:, None]) & (key_pos[None, :] > query_pos[:, None] - WIN)
    slot_ids = jnp.arange(index_rows.shape[1], dtype=jnp.int32)
    picked = jnp.where((slot_ids[None, :] < count_rows[:, None]) & (index_rows >= 0), index_rows, seq_len)
    chosen = jnp.any(picked[:, :, None] == key_pos[None, None, :], axis=1)
    return window_hit | chosen

def attend_block(query_blk, keys_all, values_all, key_gate, index_blk, count_blk, first_pos):
    scores = jnp.einsum('qhe,khe->hqk', query_blk, keys_all, precision=HIGHEST) * 0.125 + key_gate[:, None, :]
    allowed = block_mask(index_blk, count_blk, first_pos, keys_all.shape[0])
    scores = low_back(jnp.where(allowed[None], scores, -1e+30))
    row_peak = lax.optimization_barrier(jnp.max(scores, axis=-1, keepdims=True))
    weights = jnp.exp(scores - row_peak)
    probs = weights / lax.optimization_barrier(jnp.sum(weights, axis=-1, keepdims=True))
    return jnp.einsum('hqk,khe->qhe', low(probs), values_all, precision=HIGHEST)

def attend_sequence(sequence_args):
    queries, keys_all, values_all, key_gate, index_seq, count_seq = sequence_args
    seq_len = keys_all.shape[0]
    block_total = seq_len // QBLK
    firsts = jnp.arange(block_total, dtype=jnp.int32) * QBLK

    def one_block(block_args):
        query_blk, index_blk, count_blk, first_pos = block_args
        return attend_block(query_blk, keys_all, values_all, key_gate, index_blk, count_blk, first_pos)
    results = lax.map(jax.checkpoint(one_block), (queries.reshape(block_total, QBLK, H, HD), index_seq.reshape(block_total, QBLK, TOPK), count_seq.reshape(block_total, QBLK), firsts))
    return results.reshape(seq_len, H, HD)

def forward(layer_in, qkv_weight, qkv_bias, key_scorer, out_weight, out_bias, fc_weight, fc_bias, proj_weight, proj_bias, norm1_gain, norm1_shift, norm2_gain, norm2_shift, key_index, key_count):
    seq_total = TOKENS // SEQ
    normed_one = low(layer_norm(layer_in, norm1_gain, norm1_shift))
    joined_proj = low_back(jnp.dot(normed_one, qkv_weight, precision=HIGHEST)) + qkv_bias
    joined_proj = low(joined_proj).reshape(seq_total, SEQ, H, 3, HD)
    queries = joined_proj[:, :, :, 0]
    keys_all = joined_proj[:, :, :, 1]
    values_all = joined_proj[:, :, :, 2]
    gate_raw = jnp.einsum('nshe,he->nhs', keys_all, key_scorer.reshape(H, HD), precision=HIGHEST)
    key_gate = jax.nn.log_sigmoid(gate_raw)
    attended = lax.map(attend_sequence, (queries, keys_all, values_all, key_gate, key_index.reshape(seq_total, SEQ, TOPK), key_count.reshape(seq_total, SEQ)))
    attended = low(low_back(attended.reshape(TOKENS, D)))
    mixed = layer_in + low_back(jnp.dot(attended, out_weight, precision=HIGHEST)) + out_bias
    normed_two = low(layer_norm(mixed, norm2_gain, norm2_shift))
    hidden = low_back(jnp.dot(normed_two, fc_weight, precision=HIGHEST)) + fc_bias
    active = low(jax.nn.gelu(hidden, approximate=True))
    return mixed + low_back(jnp.dot(active, proj_weight, precision=HIGHEST)) + proj_bias

def reference(layer_in, qkv_weight, qkv_bias, key_scorer, out_weight, out_bias, fc_weight, fc_bias, proj_weight, proj_bias, norm1_gain, norm1_shift, norm2_gain, norm2_shift, key_index, key_count, out_grad):
    floats = (layer_in, qkv_weight.astype(jnp.float32), qkv_bias, key_scorer, out_weight.astype(jnp.float32), out_bias, fc_weight.astype(jnp.float32), fc_bias, proj_weight.astype(jnp.float32), proj_bias, norm1_gain, norm1_shift, norm2_gain, norm2_shift)
    layer_out, pullback = jax.vjp(partial(forward, key_index=key_index, key_count=key_count), *floats)
    grads = pullback(out_grad)
    return (layer_out, grads[0], grads[1], grads[2], grads[3], grads[4], grads[5], grads[6], grads[7], grads[8], grads[9], grads[10], grads[11], grads[12], grads[13])
```

```python
import functools
import math

import jax
import jax.numpy as jnp
from jax import lax
from jax.experimental import pallas as pl
from jax.experimental.pallas import tpu as pltpu
from jax.sharding import PartitionSpec as P

HD = 64
LANES = 128
WIN = 64
LOG2E = math.log2(math.e)
LN2 = math.log(2.0)
NEG = -1e30
QB = 512
KB = 512
ROWS = 512
VT = 80
NT = (((1,), (1,)), ((), ()))
NN = (((1,), (0,)), ((), ()))
TN = (((0,), (0,)), ((), ()))
F32 = jnp.float32
BF16 = jnp.bfloat16
MIB = 1024 * 1024


def dot(a, b, dims=NN):
    return lax.dot_general(a, b, dims, preferred_element_type=F32)


def split3(x):
    hi = x.astype(BF16).astype(F32)
    rest = x - hi
    mid = rest.astype(BF16).astype(F32)
    low = (rest - mid).astype(BF16).astype(F32)
    return hi, mid, low


def lane_ids(rows):
    return lax.broadcasted_iota(jnp.int32, (rows, LANES), 1)


def put3(base, lanes, first, parts):
    out = base
    for n, part in enumerate(parts):
        out = jnp.where(lanes == first + n, part, out)
    return out


def whole_block(array):
    return pl.BlockSpec(array.shape, lambda *_: (0,) * array.ndim)


def scorer_rows(key_scorer):
    return jnp.pad(key_scorer.reshape(-1, HD), ((0, 0), (0, LANES - HD)))


def bits_kernel(low_ref, flag_ref, bits_ref):
    width = bits_ref.shape[1]
    first = pl.program_id(0) * width
    lane = lax.broadcasted_iota(jnp.int32, (LANES, width), 0)
    pos = lax.broadcasted_iota(jnp.int32, (LANES, width), 1) + first
    back = (pos - lane) & (LANES - 1)
    at = pos - back
    bits = jnp.where((back < WIN) & (at >= 0), 1 << (jnp.maximum(at, 0) >> 7), 0)
    for slot in range(low_ref.shape[0]):
        hit = low_ref[slot : slot + 1, :] == lane
        bits = bits | jnp.where(hit, flag_ref[slot : slot + 1, :], 0)
    bits_ref[...] = bits


def allowed_bits(key_index, key_count):
    seq = key_index.shape[0]
    index = key_index.T
    slots = index.shape[0]
    slot = lax.broadcasted_iota(jnp.int32, index.shape, 0)
    used = (slot < key_count[None, :]) & (index >= 0)
    low = index & (LANES - 1)
    flag = jnp.where(used, 1 << (jnp.maximum(index, 0) >> 7), 0)
    width = 256
    spec = pl.BlockSpec((slots, width), lambda i: (0, i))
    return pl.pallas_call(
        bits_kernel,
        grid=(seq // width,),
        in_specs=[spec, spec],
        out_specs=pl.BlockSpec((LANES, width), lambda i: (0, i)),
        out_shape=jax.ShapeDtypeStruct((LANES, seq), jnp.int32),
        cost_estimate=pl.CostEstimate(
            flops=3 * slots * LANES * seq, bytes_accessed=8 * slots * seq, transcendentals=0
        ),
        name="allowed_bits",
    )(low, flag)


def fill_bias(bias_ref, bits_ref, q0, k0):
    depth, width = bias_ref.shape
    bits = bits_ref[:, pl.ds(q0, width)]
    for part in range(depth // LANES):
        shift = k0 // LANES + part
        seen = ((bits >> shift) & 1) == 1
        bias_ref[part * LANES : (part + 1) * LANES, :] = jnp.where(seen, 0.0, NEG)


def qkv_kernel(norm_ref, weight_ref, bias_ref, scorer_ref, qa_ref, ka_ref, va_ref, vt_ref, kt_ref):
    rows = norm_ref.shape[0]
    heads = qa_ref.shape[0]
    lanes = lane_ids(rows)
    real = lanes < HD
    ones = jnp.where((lanes >= HD) & (lanes < HD + 3), 1.0, 0.0)
    for pair in range(heads // 2):
        cols = slice(pair * 6 * HD, (pair + 1) * 6 * HD)
        raw = dot(norm_ref[...], weight_ref[:, cols]) + bias_ref[:, cols]
        raw = raw.astype(BF16).astype(F32)
        blocks = [raw[:, n * LANES : (n + 1) * LANES] for n in range(3)]
        turned = [pltpu.roll(block, HD, 1) for block in blocks]
        groups = (
            (blocks[0], turned[0], blocks[1]),
            (turned[1], blocks[2], turned[2]),
        )
        for side, (query, key, value) in enumerate(groups):
            head = pair * 2 + side
            raw_gate = jnp.sum(key * scorer_ref[head : head + 1, :], axis=1, keepdims=True)
            gate = jnp.minimum(raw_gate, 0.0) - jnp.log1p(jnp.exp(-jnp.abs(raw_gate)))
            key_plain = jnp.where(real, key, 0.0)
            value_ones = jnp.where(real, value, ones)
            qa_ref[head] = jnp.where(real, query * 0.125, ones).astype(BF16)
            ka_ref[head] = put3(key_plain, lanes, HD, split3(gate)).astype(BF16)
            va_ref[head] = value_ones.astype(BF16)
            vt_ref[head] = value_ones.T[:VT, :].astype(BF16)
            kt_ref[head] = key_plain.T[:HD, :].astype(BF16)


def qkv_heads(norm_all, weight, bias, scorer):
    seq, width = norm_all.shape
    heads = scorer.shape[0]
    cols = weight.shape[1]
    row_spec = pl.BlockSpec((heads, ROWS, LANES), lambda i: (0, i, 0))
    row_shape = jax.ShapeDtypeStruct((heads, seq, LANES), BF16)
    bias = bias.reshape(1, cols)
    return pl.pallas_call(
        qkv_kernel,
        grid=(seq // ROWS,),
        in_specs=[
            pl.BlockSpec((ROWS, width), lambda i: (i, 0)),
            whole_block(weight),
            whole_block(bias),
            whole_block(scorer),
        ],
        out_specs=[
            row_spec,
            row_spec,
            row_spec,
            pl.BlockSpec((heads, VT, ROWS), lambda i: (0, 0, i)),
            pl.BlockSpec((heads, HD, ROWS), lambda i: (0, 0, i)),
        ],
        out_shape=[
            row_shape,
            row_shape,
            row_shape,
            jax.ShapeDtypeStruct((heads, VT, seq), BF16),
            jax.ShapeDtypeStruct((heads, HD, seq), BF16),
        ],
        compiler_params=pltpu.CompilerParams(vmem_limit_bytes=40 * MIB),
        cost_estimate=pl.CostEstimate(
            flops=2 * seq * width * cols, bytes_accessed=20 * MIB, transcendentals=0
        ),
        name="qkv_heads",
    )(norm_all, weight, bias, scorer)


def attend_kernel(
    qa_ref, ka_ref, vt_ref, bits_ref, out_ref, log_ref, bias_ref, total_ref, peak_ref
):
    heads = qa_ref.shape[0]
    q0 = pl.multiple_of(pl.program_id(0) * QB, QB)
    total_ref[...] = jnp.zeros_like(total_ref)
    peak_ref[...] = jnp.full_like(peak_ref, NEG)

    def step(j, carry):
        k0 = pl.multiple_of(j * KB, KB)
        fill_bias(bias_ref, bits_ref, q0, k0)

        def scores_of(head):
            return dot(ka_ref[head, pl.ds(k0, KB), :], qa_ref[head], NT)

        ahead = scores_of(0)
        for head in range(heads):
            scores = ahead
            if head + 1 < heads:
                ahead = scores_of(head + 1)
            scores = scores * LOG2E + bias_ref[...]
            old = peak_ref[head]
            new = jnp.maximum(old, jnp.max(scores, axis=0, keepdims=True))
            weights = jnp.exp2(scores - new[0:1])
            shrink = jnp.exp2(old - new)
            peak_ref[head] = new
            part = dot(vt_ref[head, :, pl.ds(k0, KB)], weights.astype(BF16))
            total_ref[head] = total_ref[head] * shrink[0:1] + part
        return carry

    lax.fori_loop(0, (q0 + QB + KB - 1) // KB, step, 0)
    for pair in range(heads // 2):
        sides = []
        for head in (2 * pair, 2 * pair + 1):
            mass = total_ref[head, HD : HD + 1, :]
            sides.append(total_ref[head, 0:HD, :] / mass)
            log_ref[head] = peak_ref[head] + jnp.log(mass) * LOG2E
        both = jnp.concatenate(sides, axis=0).T
        out_ref[:, pair * LANES : (pair + 1) * LANES] = both.astype(BF16)


def attend(qa, ka, vt, bits):
    heads, seq, _ = qa.shape
    return pl.pallas_call(
        attend_kernel,
        grid=(seq // QB,),
        in_specs=[
            pl.BlockSpec((heads, QB, LANES), lambda i: (0, i, 0)),
            whole_block(ka),
            whole_block(vt),
            whole_block(bits),
        ],
        out_specs=[
            pl.BlockSpec((QB, heads * HD), lambda i: (i, 0)),
            pl.BlockSpec((heads, 8, QB), lambda i: (0, 0, i)),
        ],
        out_shape=[
            jax.ShapeDtypeStruct((seq, heads * HD), BF16),
            jax.ShapeDtypeStruct((heads, 8, seq), F32),
        ],
        scratch_shapes=[
            pltpu.VMEM((KB, QB), F32),
            pltpu.VMEM((heads, VT, QB), F32),
            pltpu.VMEM((heads, 8, QB), F32),
        ],
        compiler_params=pltpu.CompilerParams(vmem_limit_bytes=48 * MIB),
        cost_estimate=pl.CostEstimate(
            flops=heads * seq * seq * 256, bytes_accessed=12 * MIB, transcendentals=0
        ),
        name="attend",
    )(qa, ka, vt, bits)


def attend_back_kernel(
    qa_ref,
    ka_ref,
    kt_ref,
    va_ref,
    grad_ref,
    att_ref,
    log_ref,
    bits_ref,
    scorer_ref,
    keys_ref,
    joined_ref,
    bias_out_ref,
    scorer_out_ref,
    bias_ref,
    ga_ref,
    dq_ref,
    dk_ref,
    dv_ref,
):
    j = pl.program_id(0)
    heads, seq, _ = qa_ref.shape
    k0 = pl.multiple_of(j * KB, KB)

    @pl.when(j == 0)
    def _():
        dq_ref[...] = jnp.zeros_like(dq_ref)
        lanes = lane_ids(ROWS)

        def prepare(step, carry):
            rows = pl.ds(pl.multiple_of(step * ROWS, ROWS), ROWS)
            for pair in range(heads // 2):
                cols = slice(pair * LANES, (pair + 1) * LANES)
                grad = grad_ref[rows, cols].astype(F32)
                prod = grad * att_ref[rows, cols].astype(F32)
                turned = pltpu.roll(grad, HD, 1)
                for side, values in enumerate((grad, turned)):
                    mine = (lanes < HD) if side == 0 else (lanes >= HD)
                    inner = jnp.sum(jnp.where(mine, prod, 0.0), axis=1, keepdims=True)
                    plain = jnp.where(lanes < HD, values, 0.0)
                    filled = put3(plain, lanes, HD, split3(-inner))
                    ga_ref[pair * 2 + side, rows, :] = filled.astype(BF16)
            return carry

        lax.fori_loop(0, seq // ROWS, prepare, 0)

    mine = pl.ds(k0, KB)
    dk_ref[:, mine, :] = jnp.zeros((heads, KB, LANES), F32)
    dv_ref[:, mine, :] = jnp.zeros((heads, KB, LANES), F32)

    def step(i, carry):
        q0 = pl.multiple_of(i * QB, QB)
        queries = pl.ds(q0, QB)
        fill_bias(bias_ref, bits_ref, q0, k0)

        def first_of(head):
            qa = qa_ref[head, queries, :]
            ga = ga_ref[head, queries, :]
            return qa, ga, dot(ka_ref[head], qa, NT), dot(va_ref[head], ga, NT)

        ahead = first_of(0)
        for head in range(heads):
            qa, ga, scores, inner = ahead
            if head + 1 < heads:
                ahead = first_of(head + 1)
            scores = scores * LOG2E + bias_ref[...]
            probs = jnp.exp2(scores - log_ref[head, 0:1, queries])
            slopes = (probs * inner).astype(BF16)
            dv_ref[head, mine, :] += dot(probs.astype(BF16), ga)
            dk_ref[head, mine, :] += dot(slopes, qa)
            dq_ref[head, :, queries] += dot(kt_ref[head], slopes)
        return carry

    lax.fori_loop(k0 // QB, seq // QB, step, 0)

    @pl.when(j == pl.num_programs(0) - 1)
    def _():
        span = 256
        lanes = lane_ids(span)
        real = lanes < HD
        bias_out_ref[...] = jnp.zeros_like(bias_out_ref)
        scorer_out_ref[...] = jnp.zeros_like(scorer_out_ref)

        def finish(step, carry):
            r0 = pl.multiple_of(step * span, span)
            rows = pl.ds(r0, span)
            for pair in range(heads // 2):
                dq = dq_ref[2 * pair : 2 * pair + 2, :, rows].reshape(LANES, span).T * 0.125
                dks, dvs = [], []
                for head in (2 * pair, 2 * pair + 1):
                    scorer = scorer_ref[head : head + 1, :]
                    key = keys_ref[head, rows, :].astype(F32)
                    dk = dk_ref[head, rows, :]
                    raw_gate = jnp.sum(key * scorer, axis=1, keepdims=True)
                    slope = dk[:, HD : HD + 1] / (1.0 + jnp.exp(raw_gate))
                    scorer_out_ref[head : head + 1, :] += jnp.sum(slope * key, axis=0, keepdims=True)
                    dks.append(dk + slope * scorer)
                    dvs.append(dv_ref[head, rows, :])
                blocks = (
                    jnp.where(real, dq, pltpu.roll(dks[0], HD, 1)),
                    jnp.where(real, dvs[0], dq),
                    jnp.where(real, dks[1], pltpu.roll(dvs[1], HD, 1)),
                )
                for n, block in enumerate(blocks):
                    cols = slice((pair * 3 + n) * LANES, (pair * 3 + n + 1) * LANES)
                    bias_out_ref[:, cols] += jnp.sum(block, axis=0, keepdims=True)
                    joined_ref[rows, cols] = block.astype(BF16)
            return carry

        lax.fori_loop(0, seq // span, finish, 0)


def attend_back(qa, ka, kt, va, grad, att, logs, bits, scorer):
    heads, seq, _ = qa.shape
    cols = heads * 3 * HD
    key_spec = pl.BlockSpec((heads, KB, LANES), lambda j: (0, j, 0))
    joined, bias_out, scorer_out = pl.pallas_call(
        attend_back_kernel,
        grid=(seq // KB,),
        in_specs=[
            whole_block(qa),
            key_spec,
            pl.BlockSpec((heads, HD, KB), lambda j: (0, 0, j)),
            key_spec,
            whole_block(grad),
            whole_block(att),
            whole_block(logs),
            whole_block(bits),
            whole_block(scorer),
            whole_block(ka),
        ],
        out_specs=[
            pl.BlockSpec((seq, cols), lambda j: (0, 0)),
            pl.BlockSpec((1, cols), lambda j: (0, 0)),
            pl.BlockSpec((heads, LANES), lambda j: (0, 0)),
        ],
        out_shape=[
            jax.ShapeDtypeStruct((seq, cols), BF16),
            jax.ShapeDtypeStruct((1, cols), F32),
            jax.ShapeDtypeStruct((heads, LANES), F32),
        ],
        scratch_shapes=[
            pltpu.VMEM((KB, QB), F32),
            pltpu.VMEM((heads, seq, LANES), BF16),
            pltpu.VMEM((heads, HD, seq), F32),
            pltpu.VMEM((heads, seq, LANES), F32),
            pltpu.VMEM((heads, seq, LANES), F32),
        ],
        compiler_params=pltpu.CompilerParams(vmem_limit_bytes=60 * MIB),
        cost_estimate=pl.CostEstimate(
            flops=heads * seq * seq * 640, bytes_accessed=24 * MIB, transcendentals=0
        ),
        name="attend_back",
    )(qa, ka, kt, va, grad, att, logs, bits, scorer, ka)
    return joined, bias_out.reshape(cols), scorer_out[:, :HD].reshape(heads * HD)


def layer_norm(inputs, norm_gain, norm_shift):
    center = inputs - jnp.mean(inputs, axis=-1, keepdims=True)
    variance = jnp.mean(center * center, axis=-1, keepdims=True)
    return center * lax.rsqrt(variance + 1e-05) * norm_gain + norm_shift


def smooth_gelu(inputs):
    return jax.nn.gelu(inputs, approximate=True)


def scatter_rows(partial):
    return lax.psum_scatter(
        partial.astype(BF16), "tensor", scatter_dimension=0, tiled=True
    ).astype(F32)


def shards(
    layer_in,
    qkv_weight,
    qkv_bias,
    key_scorer,
    out_weight,
    out_bias,
    fc_weight,
    fc_bias,
    proj_weight,
    proj_bias,
    norm1_gain,
    norm1_shift,
    norm2_gain,
    norm2_shift,
    key_index,
    key_count,
    out_grad,
):
    bits = allowed_bits(key_index, key_count)
    scorer = scorer_rows(key_scorer)
    normed_one, norm1_back = jax.vjp(layer_norm, layer_in, norm1_gain, norm1_shift)
    normed_one_all = lax.all_gather(normed_one.astype(BF16), "tensor", axis=0, tiled=True)
    qa, ka, va, vt, kt = qkv_heads(normed_one_all, qkv_weight, qkv_bias, scorer)
    attended_low, logs = attend(qa, ka, vt, bits)
    mixed = layer_in + scatter_rows(dot(attended_low, out_weight)) + out_bias
    normed_two, norm2_back = jax.vjp(layer_norm, mixed, norm2_gain, norm2_shift)
    normed_two_all = lax.all_gather(normed_two.astype(BF16), "tensor", axis=0, tiled=True)
    hidden = dot(normed_two_all, fc_weight) + fc_bias
    active, gelu_back = jax.vjp(smooth_gelu, hidden)
    active_low = active.astype(BF16)
    layer_out = mixed + scatter_rows(dot(active_low, proj_weight)) + proj_bias
    grad_proj_bias = jnp.sum(out_grad, axis=0)
    grad_all = lax.all_gather(out_grad.astype(BF16), "tensor", axis=0, tiled=True)
    grad_proj_weight = dot(active_low, grad_all, TN)
    grad_active = dot(grad_all, proj_weight, NT)
    (grad_hidden,) = gelu_back(grad_active)
    grad_fc_bias = jnp.sum(grad_hidden, axis=0)
    grad_hidden_low = grad_hidden.astype(BF16)
    grad_fc_weight = dot(normed_two_all, grad_hidden_low, TN)
    grad_normed_two = scatter_rows(dot(grad_hidden_low, fc_weight, NT))
    grad_mixed_part, grad_norm2_gain, grad_norm2_shift = norm2_back(grad_normed_two)
    grad_mixed = out_grad + grad_mixed_part
    grad_out_bias = jnp.sum(grad_mixed, axis=0)
    grad_mixed_all = lax.all_gather(grad_mixed.astype(BF16), "tensor", axis=0, tiled=True)
    grad_out_weight = dot(attended_low, grad_mixed_all, TN)
    grad_attended = dot(grad_mixed_all, out_weight, NT).astype(BF16)
    joined_grad, grad_qkv_bias, grad_key_scorer = attend_back(
        qa, ka, kt, va, grad_attended, attended_low, logs, bits, scorer
    )
    grad_qkv_weight = dot(normed_one_all, joined_grad, TN)
    grad_normed_one = scatter_rows(dot(joined_grad, qkv_weight, NT))
    grad_in_part, grad_norm1_gain, grad_norm1_shift = norm1_back(grad_normed_one)
    input_grad = grad_mixed + grad_in_part
    (grad_out_weight, grad_fc_weight, grad_proj_weight) = lax.psum(
        tuple(g.astype(BF16) for g in (grad_out_weight, grad_fc_weight, grad_proj_weight)), "dp"
    )
    grad_qkv_weight = lax.psum(grad_qkv_weight.astype(BF16), "dp")
    (grad_qkv_bias, grad_key_scorer, grad_fc_bias) = lax.psum(
        (grad_qkv_bias, grad_key_scorer, grad_fc_bias), "dp"
    )
    (
        grad_out_bias,
        grad_proj_bias,
        grad_norm1_gain,
        grad_norm1_shift,
        grad_norm2_gain,
        grad_norm2_shift,
    ) = lax.psum(
        (
            grad_out_bias,
            grad_proj_bias,
            grad_norm1_gain,
            grad_norm1_shift,
            grad_norm2_gain,
            grad_norm2_shift,
        ),
        ("dp", "tensor"),
    )
    return (
        layer_out,
        input_grad,
        grad_qkv_weight.astype(F32),
        grad_qkv_bias,
        grad_key_scorer,
        grad_out_weight.astype(F32),
        grad_out_bias,
        grad_fc_weight.astype(F32),
        grad_fc_bias,
        grad_proj_weight.astype(F32),
        grad_proj_bias,
        grad_norm1_gain,
        grad_norm1_shift,
        grad_norm2_gain,
        grad_norm2_shift,
    )


def solution(mesh):
    rows = P(("dp", "tensor"), None)
    in_specs = (
        rows,
        P(None, "tensor"),
        P("tensor"),
        P("tensor"),
        P("tensor", None),
        P(),
        P(None, "tensor"),
        P("tensor"),
        P("tensor", None),
        P(),
        P(),
        P(),
        P(),
        P(),
        P("dp", None),
        P("dp"),
        rows,
    )
    out_specs = (
        rows,
        rows,
        P(None, "tensor"),
        P("tensor"),
        P("tensor"),
        P("tensor", None),
        P(),
        P(None, "tensor"),
        P("tensor"),
        P("tensor", None),
        P(),
        P(),
        P(),
        P(),
        P(),
    )
    return jax.shard_map(shards, mesh=mesh, in_specs=in_specs, out_specs=out_specs, check_vma=False)
```

```python
import functools
import math

import jax
import jax.numpy as jnp
from jax import lax
from jax.experimental import pallas as pl
from jax.experimental.pallas import tpu as pltpu
from jax.sharding import PartitionSpec as P

HD = 64
LANES = 128
WIN = 64
LOG2E = math.log2(math.e)
LN2 = math.log(2.0)
NEG = -1e30
QB = 512
KB = 512
ROWS = 512
VT = 80
NT = (((1,), (1,)), ((), ()))
NN = (((1,), (0,)), ((), ()))
TN = (((0,), (0,)), ((), ()))
F32 = jnp.float32
BF16 = jnp.bfloat16
MIB = 1024 * 1024


def dot(a, b, dims=NN):
    return lax.dot_general(a, b, dims, preferred_element_type=F32)


def split3(x):
    hi = x.astype(BF16).astype(F32)
    rest = x - hi
    mid = rest.astype(BF16).astype(F32)
    low = (rest - mid).astype(BF16).astype(F32)
    return hi, mid, low


def lane_ids(rows):
    return lax.broadcasted_iota(jnp.int32, (rows, LANES), 1)


def put3(base, lanes, first, parts):
    out = base
    for n, part in enumerate(parts):
        out = jnp.where(lanes == first + n, part, out)
    return out


def whole_block(array):
    return pl.BlockSpec(array.shape, lambda *_: (0,) * array.ndim)


def scorer_rows(key_scorer):
    return jnp.pad(key_scorer.reshape(-1, HD), ((0, 0), (0, LANES - HD)))


def bits_kernel(low_ref, flag_ref, bits_ref):
    width = bits_ref.shape[1]
    first = pl.program_id(0) * width
    lane = lax.broadcasted_iota(jnp.int32, (LANES, width), 0)
    pos = lax.broadcasted_iota(jnp.int32, (LANES, width), 1) + first
    back = (pos - lane) & (LANES - 1)
    at = pos - back
    bits = jnp.where((back < WIN) & (at >= 0), 1 << (jnp.maximum(at, 0) >> 7), 0)
    for slot in range(low_ref.shape[0]):
        hit = low_ref[slot : slot + 1, :] == lane
        bits = bits | jnp.where(hit, flag_ref[slot : slot + 1, :], 0)
    bits_ref[...] = bits


def allowed_bits(key_index, key_count):
    seq = key_index.shape[0]
    index = key_index.T
    slots = index.shape[0]
    slot = lax.broadcasted_iota(jnp.int32, index.shape, 0)
    used = (slot < key_count[None, :]) & (index >= 0)
    low = index & (LANES - 1)
    flag = jnp.where(used, 1 << (jnp.maximum(index, 0) >> 7), 0)
    width = 256
    spec = pl.BlockSpec((slots, width), lambda i: (0, i))
    return pl.pallas_call(
        bits_kernel,
        grid=(seq // width,),
        in_specs=[spec, spec],
        out_specs=pl.BlockSpec((LANES, width), lambda i: (0, i)),
        out_shape=jax.ShapeDtypeStruct((LANES, seq), jnp.int32),
        cost_estimate=pl.CostEstimate(
            flops=3 * slots * LANES * seq, bytes_accessed=8 * slots * seq, transcendentals=0
        ),
        name="allowed_bits",
    )(low, flag)


def fill_bias(bias_ref, bits_ref, q0, k0):
    depth, width = bias_ref.shape
    bits = bits_ref[:, pl.ds(q0, width)]
    for part in range(depth // LANES):
        shift = k0 // LANES + part
        seen = ((bits >> shift) & 1) == 1
        bias_ref[part * LANES : (part + 1) * LANES, :] = jnp.where(seen, 0.0, NEG)


def qkv_kernel(
    at_ref, norm_ref, weight_ref, bias_ref, scorer_ref, qa_ref, ka_ref, va_ref, vt_ref, kt_ref
):
    rows = norm_ref.shape[0]
    heads = qa_ref.shape[0]
    lanes = lane_ids(rows)
    real = lanes < HD
    ones = jnp.where((lanes >= HD) & (lanes < HD + 3), 1.0, 0.0)
    for pair in range(heads // 2):
        cols = slice(pair * 6 * HD, (pair + 1) * 6 * HD)
        raw = dot(norm_ref[...], weight_ref[:, cols]) + bias_ref[:, cols]
        raw = raw.astype(BF16).astype(F32)
        blocks = [raw[:, n * LANES : (n + 1) * LANES] for n in range(3)]
        turned = [pltpu.roll(block, HD, 1) for block in blocks]
        groups = (
            (blocks[0], turned[0], blocks[1]),
            (turned[1], blocks[2], turned[2]),
        )
        for side, (query, key, value) in enumerate(groups):
            head = pair * 2 + side
            raw_gate = jnp.sum(key * scorer_ref[head : head + 1, :], axis=1, keepdims=True)
            gate = jnp.minimum(raw_gate, 0.0) - jnp.log1p(jnp.exp(-jnp.abs(raw_gate)))
            key_plain = jnp.where(real, key, 0.0)
            value_ones = jnp.where(real, value, ones)
            qa_ref[head] = jnp.where(real, query * 0.125, ones).astype(BF16)
            ka_ref[head] = put3(key_plain, lanes, HD, split3(gate)).astype(BF16)
            va_ref[head] = value_ones.astype(BF16)
            vt_ref[head] = value_ones.T[:VT, :].astype(BF16)
            kt_ref[head] = key_plain.T[:HD, :].astype(BF16)


def qkv_kernel_again(at_ref, norm_ref, weight_ref, bias_ref, scorer_ref, *rest):
    qkv_kernel(at_ref, norm_ref, weight_ref, bias_ref, scorer_ref, *rest[5:])


def qkv_heads(norm_rows, weight, bias, scorer, block, seq, earlier=None):
    rows, width = norm_rows.shape
    heads = scorer.shape[0]
    cols = weight.shape[1]
    row_shape = jax.ShapeDtypeStruct((heads, seq, LANES), BF16)
    row_spec = pl.BlockSpec((heads, ROWS, LANES), lambda i, at: (0, at[0] + i, 0))
    bias = bias.reshape(1, cols)
    tall = [
        jax.ShapeDtypeStruct((heads, VT, seq), BF16),
        jax.ShapeDtypeStruct((heads, HD, seq), BF16),
    ]
    kernel = qkv_kernel
    inputs = [norm_rows, weight, bias, scorer]
    in_specs = [
        pl.BlockSpec((ROWS, width), lambda i, at: (i, 0)),
        whole_block(weight),
        whole_block(bias),
        whole_block(scorer),
    ]
    aliases = {}
    if earlier is not None:
        aliases = {len(inputs) + 1 + n: n for n in range(len(earlier))}
        inputs += list(earlier)
        in_specs += [pl.BlockSpec(memory_space=pl.ANY)] * len(earlier)
        kernel = qkv_kernel_again
    return pl.pallas_call(
        kernel,
        grid_spec=pltpu.PrefetchScalarGridSpec(
            num_scalar_prefetch=1,
            grid=(rows // ROWS,),
            in_specs=in_specs,
            out_specs=[
                row_spec,
                row_spec,
                row_spec,
                pl.BlockSpec((heads, VT, ROWS), lambda i, at: (0, 0, at[0] + i)),
                pl.BlockSpec((heads, HD, ROWS), lambda i, at: (0, 0, at[0] + i)),
            ],
        ),
        out_shape=[row_shape, row_shape, row_shape] + tall,
        input_output_aliases=aliases,
        compiler_params=pltpu.CompilerParams(vmem_limit_bytes=40 * MIB),
        cost_estimate=pl.CostEstimate(
            flops=4 * rows * width * cols, bytes_accessed=10 * MIB, transcendentals=0
        ),
        name="qkv_heads",
    )(block, *inputs)


def attend_kernel(
    at_ref, qa_ref, ka_ref, vt_ref, bits_ref, out_ref, log_ref, bias_ref, total_ref, peak_ref
):
    heads = qa_ref.shape[0]
    q0 = pl.multiple_of((at_ref[0] + pl.program_id(0)) * QB, QB)
    total_ref[...] = jnp.zeros_like(total_ref)
    peak_ref[...] = jnp.full_like(peak_ref, NEG)

    def step(j, carry):
        k0 = pl.multiple_of(j * KB, KB)
        fill_bias(bias_ref, bits_ref, q0, k0)

        def scores_of(head):
            return dot(ka_ref[head, pl.ds(k0, KB), :], qa_ref[head], NT)

        ahead = scores_of(0)
        for head in range(heads):
            scores = ahead
            if head + 1 < heads:
                ahead = scores_of(head + 1)
            scores = scores * LOG2E + bias_ref[...]
            old = peak_ref[head]
            new = jnp.maximum(old, jnp.max(scores, axis=0, keepdims=True))
            weights = jnp.exp2(scores - new[0:1])
            shrink = jnp.exp2(old - new)
            peak_ref[head] = new
            part = dot(vt_ref[head, :, pl.ds(k0, KB)], weights.astype(BF16))
            total_ref[head] = total_ref[head] * shrink[0:1] + part
        return carry

    lax.fori_loop(0, (q0 + QB + KB - 1) // KB, step, 0)
    for pair in range(heads // 2):
        sides = []
        for head in (2 * pair, 2 * pair + 1):
            mass = total_ref[head, HD : HD + 1, :]
            sides.append(total_ref[head, 0:HD, :] / mass)
            log_ref[head] = peak_ref[head] + jnp.log(mass) * LOG2E
        both = jnp.concatenate(sides, axis=0).T
        out_ref[:, pair * LANES : (pair + 1) * LANES] = both.astype(BF16)


def attend(qa, ka, vt, bits, block, count):
    heads, seq, _ = qa.shape
    return pl.pallas_call(
        attend_kernel,
        grid_spec=pltpu.PrefetchScalarGridSpec(
            num_scalar_prefetch=1,
            grid=(count // QB,),
            in_specs=[
                pl.BlockSpec((heads, QB, LANES), lambda i, at: (0, at[0] + i, 0)),
                whole_block(ka),
                whole_block(vt),
                whole_block(bits),
            ],
            out_specs=[
                pl.BlockSpec((QB, heads * HD), lambda i, at: (i, 0)),
                pl.BlockSpec((heads, 8, QB), lambda i, at: (0, 0, i)),
            ],
            scratch_shapes=[
                pltpu.VMEM((KB, QB), F32),
                pltpu.VMEM((heads, VT, QB), F32),
                pltpu.VMEM((heads, 8, QB), F32),
            ],
        ),
        out_shape=[
            jax.ShapeDtypeStruct((count, heads * HD), BF16),
            jax.ShapeDtypeStruct((heads, 8, count), F32),
        ],
        compiler_params=pltpu.CompilerParams(vmem_limit_bytes=48 * MIB),
        cost_estimate=pl.CostEstimate(
            flops=heads * seq * count * 384, bytes_accessed=12 * MIB, transcendentals=0
        ),
        name="attend",
    )(block, qa, ka, vt, bits)


def attend_back_kernel(
    qa_ref,
    ka_ref,
    kt_ref,
    va_ref,
    grad_ref,
    att_ref,
    log_ref,
    bits_ref,
    scorer_ref,
    keys_ref,
    joined_ref,
    bias_out_ref,
    scorer_out_ref,
    bias_ref,
    ga_ref,
    dq_ref,
    dk_ref,
    dv_ref,
):
    j = pl.program_id(0)
    heads, seq, _ = qa_ref.shape
    k0 = pl.multiple_of(j * KB, KB)

    @pl.when(j == 0)
    def _():
        dq_ref[...] = jnp.zeros_like(dq_ref)
        lanes = lane_ids(ROWS)

        def prepare(step, carry):
            rows = pl.ds(pl.multiple_of(step * ROWS, ROWS), ROWS)
            for pair in range(heads // 2):
                cols = slice(pair * LANES, (pair + 1) * LANES)
                grad = grad_ref[rows, cols].astype(F32)
                prod = grad * att_ref[rows, cols].astype(F32)
                turned = pltpu.roll(grad, HD, 1)
                for side, values in enumerate((grad, turned)):
                    mine = (lanes < HD) if side == 0 else (lanes >= HD)
                    inner = jnp.sum(jnp.where(mine, prod, 0.0), axis=1, keepdims=True)
                    plain = jnp.where(lanes < HD, values, 0.0)
                    filled = put3(plain, lanes, HD, split3(-inner))
                    ga_ref[pair * 2 + side, rows, :] = filled.astype(BF16)
            return carry

        lax.fori_loop(0, seq // ROWS, prepare, 0)

    mine = pl.ds(k0, KB)
    dk_ref[:, mine, :] = jnp.zeros((heads, KB, LANES), F32)
    dv_ref[:, mine, :] = jnp.zeros((heads, KB, LANES), F32)

    def step(i, carry):
        q0 = pl.multiple_of(i * QB, QB)
        queries = pl.ds(q0, QB)
        fill_bias(bias_ref, bits_ref, q0, k0)

        def first_of(head):
            qa = qa_ref[head, queries, :]
            ga = ga_ref[head, queries, :]
            return qa, ga, dot(ka_ref[head], qa, NT), dot(va_ref[head], ga, NT)

        ahead = first_of(0)
        for head in range(heads):
            qa, ga, scores, inner = ahead
            if head + 1 < heads:
                ahead = first_of(head + 1)
            scores = scores * LOG2E + bias_ref[...]
            probs = jnp.exp2(scores - log_ref[head, 0:1, queries])
            slopes = (probs * inner).astype(BF16)
            dv_ref[head, mine, :] += dot(probs.astype(BF16), ga)
            dk_ref[head, mine, :] += dot(slopes, qa)
            dq_ref[head, :, queries] += dot(kt_ref[head], slopes)
        return carry

    lax.fori_loop(k0 // QB, seq // QB, step, 0)

    @pl.when(j == pl.num_programs(0) - 1)
    def _():
        span = 256
        lanes = lane_ids(span)
        real = lanes < HD
        bias_out_ref[...] = jnp.zeros_like(bias_out_ref)
        scorer_out_ref[...] = jnp.zeros_like(scorer_out_ref)

        def finish(step, carry):
            r0 = pl.multiple_of(step * span, span)
            rows = pl.ds(r0, span)
            for pair in range(heads // 2):
                dq = dq_ref[2 * pair : 2 * pair + 2, :, rows].reshape(LANES, span).T * 0.125
                dks, dvs = [], []
                for head in (2 * pair, 2 * pair + 1):
                    scorer = scorer_ref[head : head + 1, :]
                    key = keys_ref[head, rows, :].astype(F32)
                    dk = dk_ref[head, rows, :]
                    raw_gate = jnp.sum(key * scorer, axis=1, keepdims=True)
                    slope = dk[:, HD : HD + 1] / (1.0 + jnp.exp(raw_gate))
                    scorer_out_ref[head : head + 1, :] += jnp.sum(slope * key, axis=0, keepdims=True)
                    dks.append(dk + slope * scorer)
                    dvs.append(dv_ref[head, rows, :])
                blocks = (
                    jnp.where(real, dq, pltpu.roll(dks[0], HD, 1)),
                    jnp.where(real, dvs[0], dq),
                    jnp.where(real, dks[1], pltpu.roll(dvs[1], HD, 1)),
                )
                for n, block in enumerate(blocks):
                    cols = slice((pair * 3 + n) * LANES, (pair * 3 + n + 1) * LANES)
                    bias_out_ref[:, cols] += jnp.sum(block, axis=0, keepdims=True)
                    joined_ref[rows, cols] = block.astype(BF16)
            return carry

        lax.fori_loop(0, seq // span, finish, 0)


def attend_back(qa, ka, kt, va, grad, att, logs, bits, scorer):
    heads, seq, _ = qa.shape
    cols = heads * 3 * HD
    key_spec = pl.BlockSpec((heads, KB, LANES), lambda j: (0, j, 0))
    joined, bias_out, scorer_out = pl.pallas_call(
        attend_back_kernel,
        grid=(seq // KB,),
        in_specs=[
            whole_block(qa),
            key_spec,
            pl.BlockSpec((heads, HD, KB), lambda j: (0, 0, j)),
            key_spec,
            whole_block(grad),
            whole_block(att),
            whole_block(logs),
            whole_block(bits),
            whole_block(scorer),
            whole_block(ka),
        ],
        out_specs=[
            pl.BlockSpec((seq, cols), lambda j: (0, 0)),
            pl.BlockSpec((1, cols), lambda j: (0, 0)),
            pl.BlockSpec((heads, LANES), lambda j: (0, 0)),
        ],
        out_shape=[
            jax.ShapeDtypeStruct((seq, cols), BF16),
            jax.ShapeDtypeStruct((1, cols), F32),
            jax.ShapeDtypeStruct((heads, LANES), F32),
        ],
        scratch_shapes=[
            pltpu.VMEM((KB, QB), F32),
            pltpu.VMEM((heads, seq, LANES), BF16),
            pltpu.VMEM((heads, HD, seq), F32),
            pltpu.VMEM((heads, seq, LANES), F32),
            pltpu.VMEM((heads, seq, LANES), F32),
        ],
        compiler_params=pltpu.CompilerParams(vmem_limit_bytes=60 * MIB),
        cost_estimate=pl.CostEstimate(
            flops=heads * seq * seq * 640, bytes_accessed=24 * MIB, transcendentals=0
        ),
        name="attend_back",
    )(qa, ka, kt, va, grad, att, logs, bits, scorer, ka)
    return joined, bias_out.reshape(cols), scorer_out[:, :HD].reshape(heads * HD)


def layer_norm(inputs, norm_gain, norm_shift):
    center = inputs - jnp.mean(inputs, axis=-1, keepdims=True)
    variance = jnp.mean(center * center, axis=-1, keepdims=True)
    return center * lax.rsqrt(variance + 1e-05) * norm_gain + norm_shift


def smooth_gelu(inputs):
    return jax.nn.gelu(inputs, approximate=True)


def flip_bit(values, bit):
    total = lax.axis_size("dp")
    return lax.ppermute(values, "dp", [(n, n ^ (1 << bit)) for n in range(total)])


def flip_core(values):
    return flip_bit(values, 0)


def flip_tensor(values):
    return lax.ppermute(values, "tensor", [(0, 1), (1, 0)])


def rows_at(values, start, count):
    return lax.dynamic_slice_in_dim(values, start, count, 0)


def my_bit(bit):
    return (lax.axis_index("dp") >> bit) & 1


def add_low(one, two):
    return (one.astype(F32) + two.astype(F32)).astype(BF16)


def halve(values, bit):
    half = values.shape[0] // 2
    mine = my_bit(bit)
    return add_low(
        rows_at(values, mine * half, half),
        flip_bit(rows_at(values, (1 - mine) * half, half), bit),
    )


def both_sides(own, other, mine):
    return jnp.where(
        mine == 0,
        jnp.concatenate([own, other], axis=0),
        jnp.concatenate([other, own], axis=0),
    )


def double(values, bit):
    return both_sides(values, flip_bit(values, bit), my_bit(bit))


def sum_over_dp(values):
    count = lax.axis_size("dp").bit_length() - 1
    rest = list(range(1, count))
    orders = (rest, rest[1:] + rest[:1])
    rows, cols = values.shape
    pieces = 2 << count
    mine = halve(values.reshape(pieces, rows // pieces, cols), 0)
    half = pieces // 4
    parts = [mine[:half], mine[half:]]
    for n in range(len(rest)):
        parts = [halve(part, order[n]) for part, order in zip(parts, orders)]
    for n in reversed(range(len(rest))):
        parts = [double(part, order[n]) for part, order in zip(parts, orders)]
    return double(jnp.concatenate(parts, axis=0), 0).reshape(rows, cols)


def sum_over_all(values):
    values = values + flip_tensor(values)
    for bit in range(lax.axis_size("dp").bit_length() - 1):
        values = values + flip_bit(values, bit)
    return values


def side_rows(own, other, side):
    half = own.shape[0]
    out = jnp.zeros((2 * half,) + own.shape[1:], own.dtype)
    out = lax.dynamic_update_slice_in_dim(out, own, side * half, 0)
    return lax.dynamic_update_slice_in_dim(out, other, (1 - side) * half, 0)


def in_half(vector, side):
    out = jnp.zeros((2 * vector.shape[0],), vector.dtype)
    return lax.dynamic_update_slice_in_dim(out, vector, side * vector.shape[0], 0)


def shards(
    layer_in,
    qkv_weight,
    qkv_bias,
    key_scorer,
    out_weight,
    out_bias,
    fc_weight,
    fc_bias,
    proj_weight,
    proj_bias,
    norm1_gain,
    norm1_shift,
    norm2_gain,
    norm2_shift,
    key_index,
    key_count,
    out_grad,
):
    side = lax.axis_index("tensor")
    own_rows = layer_in.shape[0]
    seq = key_index.shape[0]
    blocks_here = own_rows // QB
    own_at = (side * blocks_here).reshape(1).astype(jnp.int32)
    peer_at = ((1 - side) * blocks_here).reshape(1).astype(jnp.int32)

    normed_one, norm1_back = jax.vjp(layer_norm, layer_in, norm1_gain, norm1_shift)
    normed_one_low = normed_one.astype(BF16)
    normed_one_peer = flip_tensor(normed_one_low)
    bits = allowed_bits(key_index, key_count)
    scorer = scorer_rows(key_scorer)
    _, grad_low, out_weight_later = lax.optimization_barrier(
        (normed_one_peer, out_grad.astype(BF16), out_weight)
    )
    out_peer = flip_tensor(out_weight_later)
    grad_low_peer = flip_tensor(grad_low)

    parts = qkv_heads(normed_one_low, qkv_weight, qkv_bias, scorer, own_at, seq)
    parts = qkv_heads(normed_one_peer, qkv_weight, qkv_bias, scorer, peer_at, seq, parts)
    qa, ka, va, vt, kt = parts
    normed_one_all = side_rows(normed_one_low, normed_one_peer, side)

    att_send, logs_send = attend(qa, ka, vt, bits, peer_at, own_rows)
    att_peer = flip_tensor(att_send)
    att_own, logs_own = attend(qa, ka, vt, bits, own_at, own_rows)
    attended = side_rows(att_own, att_send, side)
    logs = jnp.where(
        side == 0,
        jnp.concatenate([logs_own, logs_send], axis=2),
        jnp.concatenate([logs_send, logs_own], axis=2),
    )
    mixed = layer_in + (dot(att_own, out_weight) + dot(att_peer, out_peer)) + out_bias

    normed_two, norm2_back = jax.vjp(layer_norm, mixed, norm2_gain, norm2_shift)
    normed_two_low = normed_two.astype(BF16)
    normed_two_peer = flip_tensor(normed_two_low)

    def feed_forward(norm_rows, grad_rows):
        hidden = dot(norm_rows, fc_weight) + fc_bias
        active, gelu_back = jax.vjp(smooth_gelu, hidden)
        (grad_hidden,) = gelu_back(dot(grad_rows, proj_weight, NT))
        grad_hidden_low = grad_hidden.astype(BF16)
        return (
            active.astype(BF16),
            grad_hidden_low,
            dot(grad_hidden_low, fc_weight, NT),
            jnp.sum(grad_hidden, axis=0),
        )

    active_own, slope_own, back_own, fc_sum_own = feed_forward(normed_two_low, grad_low)
    active_peer, slope_peer, back_peer, fc_sum_peer = feed_forward(normed_two_peer, grad_low_peer)
    back_other = flip_tensor(back_peer.astype(BF16))
    grad_fc_bias = fc_sum_own + fc_sum_peer
    grad_fc_weight = dot(normed_two_low, slope_own, TN) + dot(normed_two_peer, slope_peer, TN)
    grad_proj_weight = dot(active_own, grad_low, TN) + dot(active_peer, grad_low_peer, TN)
    grad_fc_weight, grad_proj_weight = lax.psum(
        (grad_fc_weight.astype(BF16), grad_proj_weight.astype(BF16)), "dp"
    )
    grad_normed_two = back_own + back_other.astype(F32)
    grad_mixed_part, grad_norm2_gain, grad_norm2_shift = norm2_back(grad_normed_two)
    grad_mixed = out_grad + grad_mixed_part
    grad_mixed_low = grad_mixed.astype(BF16)
    grad_att_peer = flip_tensor(dot(grad_mixed_low, out_peer, NT).astype(BF16))
    grad_att_own = dot(grad_mixed_low, out_weight, NT).astype(BF16)
    grad_attended = side_rows(grad_att_own, grad_att_peer, side)

    proj_own = dot(active_own, proj_weight)
    proj_other = flip_tensor(dot(active_peer, proj_weight).astype(BF16))
    layer_out = mixed + (proj_own + proj_other.astype(F32)) + proj_bias
    grad_out_turned = add_low(
        dot(grad_mixed_low, att_own, TN),
        flip_tensor(dot(grad_mixed_low, att_peer, TN).astype(BF16)),
    )

    joined_grad, grad_qkv_bias, grad_key_scorer = attend_back(
        qa, ka, kt, va, grad_attended, attended, logs, bits, scorer
    )
    grad_one_send = dot(rows_at(joined_grad, (1 - side) * own_rows, own_rows), qkv_weight, NT)
    grad_one_other = flip_tensor(grad_one_send.astype(BF16))
    grad_qkv_weight = dot(normed_one_all, joined_grad, TN).astype(BF16)
    last = sum_over_dp(jnp.concatenate([grad_qkv_weight, grad_out_turned], axis=1))
    joined_cols = qkv_weight.shape[1]
    grad_qkv_weight = last[:, :joined_cols]
    grad_out_weight = last[:, joined_cols:].T
    grad_one_own = dot(rows_at(joined_grad, side * own_rows, own_rows), qkv_weight, NT)
    grad_normed_one = grad_one_own + grad_one_other.astype(F32)
    grad_in_part, grad_norm1_gain, grad_norm1_shift = norm1_back(grad_normed_one)
    input_grad = grad_mixed + grad_in_part

    sums = [
        jnp.sum(grad_mixed, axis=0),
        jnp.sum(out_grad, axis=0),
        grad_norm1_gain,
        grad_norm1_shift,
        grad_norm2_gain,
        grad_norm2_shift,
        in_half(grad_qkv_bias, side),
        in_half(grad_key_scorer, side),
        in_half(grad_fc_bias, side),
    ]
    packed = sum_over_all(jnp.concatenate(sums).reshape(-1, LANES)).reshape(-1)
    ends = []
    at = 0
    for part in sums:
        ends.append(packed[at : at + part.shape[0]])
        at += part.shape[0]

    def mine_of(vector):
        half = vector.shape[0] // 2
        return lax.dynamic_slice_in_dim(vector, side * half, half, 0)

    return (
        layer_out,
        input_grad,
        grad_qkv_weight.astype(F32),
        mine_of(ends[6]),
        mine_of(ends[7]),
        grad_out_weight.astype(F32),
        ends[0],
        grad_fc_weight.astype(F32),
        mine_of(ends[8]),
        grad_proj_weight.astype(F32),
        ends[1],
        ends[2],
        ends[3],
        ends[4],
        ends[5],
    )


def solution(mesh):
    rows = P(("dp", "tensor"), None)
    in_specs = (
        rows,
        P(None, "tensor"),
        P("tensor"),
        P("tensor"),
        P("tensor", None),
        P(),
        P(None, "tensor"),
        P("tensor"),
        P("tensor", None),
        P(),
        P(),
        P(),
        P(),
        P(),
        P("dp", None),
        P("dp"),
        rows,
    )
    out_specs = (
        rows,
        rows,
        P(None, "tensor"),
        P("tensor"),
        P("tensor"),
        P("tensor", None),
        P(),
        P(None, "tensor"),
        P("tensor"),
        P("tensor", None),
        P(),
        P(),
        P(),
        P(),
        P(),
    )
    return jax.shard_map(shards, mesh=mesh, in_specs=in_specs, out_specs=out_specs, check_vma=False)
```

```python
import functools
import math

import jax
import jax.numpy as jnp
from jax import lax
from jax.experimental import pallas as pl
from jax.experimental.pallas import tpu as pltpu
from jax.sharding import PartitionSpec as P

HD = 64
LANES = 128
WIN = 64
LOG2E = math.log2(math.e)
LN2 = math.log(2.0)
NEG = -1e30
QB = 512
KB = 512
ROWS = 512
VT = 80
NT = (((1,), (1,)), ((), ()))
NN = (((1,), (0,)), ((), ()))
TN = (((0,), (0,)), ((), ()))
F32 = jnp.float32
BF16 = jnp.bfloat16
MIB = 1024 * 1024


def dot(a, b, dims=NN):
    return lax.dot_general(a, b, dims, preferred_element_type=F32)


def split3(x):
    hi = x.astype(BF16).astype(F32)
    rest = x - hi
    mid = rest.astype(BF16).astype(F32)
    low = (rest - mid).astype(BF16).astype(F32)
    return hi, mid, low


def lane_ids(rows):
    return lax.broadcasted_iota(jnp.int32, (rows, LANES), 1)


def put3(base, lanes, first, parts):
    out = base
    for n, part in enumerate(parts):
        out = jnp.where(lanes == first + n, part, out)
    return out


def whole_block(array):
    return pl.BlockSpec(
        array.shape, lambda *_: (0,) * array.ndim, pipeline_mode=pl.Buffered(1)
    )


def scorer_rows(key_scorer):
    return jnp.pad(key_scorer.reshape(-1, HD), ((0, 0), (0, LANES - HD)))


def bits_kernel(low_ref, flag_ref, bits_ref):
    width = bits_ref.shape[1]
    first = pl.program_id(0) * width
    lane = lax.broadcasted_iota(jnp.int32, (LANES, width), 0)
    pos = lax.broadcasted_iota(jnp.int32, (LANES, width), 1) + first
    back = (pos - lane) & (LANES - 1)
    at = pos - back
    bits = jnp.where((back < WIN) & (at >= 0), 1 << (jnp.maximum(at, 0) >> 7), 0)
    for slot in range(low_ref.shape[0]):
        hit = low_ref[slot : slot + 1, :] == lane
        bits = bits | jnp.where(hit, flag_ref[slot : slot + 1, :], 0)
    bits_ref[...] = bits


def allowed_bits(key_index, key_count):
    seq = key_index.shape[0]
    index = key_index.T
    slots = index.shape[0]
    slot = lax.broadcasted_iota(jnp.int32, index.shape, 0)
    used = (slot < key_count[None, :]) & (index >= 0)
    low = index & (LANES - 1)
    flag = jnp.where(used, 1 << (jnp.maximum(index, 0) >> 7), 0)
    width = 256
    spec = pl.BlockSpec((slots, width), lambda i: (0, i))
    return pl.pallas_call(
        bits_kernel,
        grid=(seq // width,),
        in_specs=[spec, spec],
        out_specs=pl.BlockSpec((LANES, width), lambda i: (0, i)),
        out_shape=jax.ShapeDtypeStruct((LANES, seq), jnp.int32),
        cost_estimate=pl.CostEstimate(
            flops=3 * slots * LANES * seq, bytes_accessed=8 * slots * seq, transcendentals=0
        ),
        name="allowed_bits",
    )(low, flag)


def fill_bias(bias_ref, bits_ref, q0, k0):
    depth, width = bias_ref.shape
    bits = bits_ref[:, pl.ds(q0, width)]
    for part in range(depth // LANES):
        shift = k0 // LANES + part
        seen = ((bits >> shift) & 1) == 1
        bias_ref[part * LANES : (part + 1) * LANES, :] = jnp.where(seen, 0.0, NEG)


def qkv_kernel(
    norm_ref, weight_ref, bias_ref, scorer_ref, qa_ref, ka_ref, va_ref, vt_ref, kt_ref
):
    rows = norm_ref.shape[0]
    heads = qa_ref.shape[0]
    lanes = lane_ids(rows)
    real = lanes < HD
    ones = jnp.where((lanes >= HD) & (lanes < HD + 3), 1.0, 0.0)
    for pair in range(heads // 2):
        cols = slice(pair * 6 * HD, (pair + 1) * 6 * HD)
        raw = dot(norm_ref[...], weight_ref[:, cols]) + bias_ref[:, cols]
        raw = raw.astype(BF16).astype(F32)
        blocks = [raw[:, n * LANES : (n + 1) * LANES] for n in range(3)]
        turned = [pltpu.roll(block, HD, 1) for block in blocks]
        groups = (
            (blocks[0], turned[0], blocks[1]),
            (turned[1], blocks[2], turned[2]),
        )
        for side, (query, key, value) in enumerate(groups):
            head = pair * 2 + side
            raw_gate = jnp.sum(key * scorer_ref[head : head + 1, :], axis=1, keepdims=True)
            gate = jnp.minimum(raw_gate, 0.0) - jnp.log1p(jnp.exp(-jnp.abs(raw_gate)))
            key_plain = jnp.where(real, key, 0.0)
            value_ones = jnp.where(real, value, ones)
            qa_ref[head] = jnp.where(real, query * 0.125, ones).astype(BF16)
            ka_ref[head] = put3(key_plain, lanes, HD, split3(gate)).astype(BF16)
            va_ref[head] = value_ones.astype(BF16)
            vt_ref[head] = value_ones.T[:VT, :].astype(BF16)
            kt_ref[head] = key_plain.T[:HD, :].astype(BF16)


def qkv_heads(norm_rows, weight, bias, scorer):
    rows, width = norm_rows.shape
    heads = scorer.shape[0]
    cols = weight.shape[1]
    row_shape = jax.ShapeDtypeStruct((heads, rows, LANES), BF16)
    row_block = pl.BlockSpec((heads, ROWS, LANES), lambda i: (0, i, 0))
    bias = bias.reshape(1, cols)
    return pl.pallas_call(
        qkv_kernel,
        grid=(rows // ROWS,),
        in_specs=[
            pl.BlockSpec((ROWS, width), lambda i: (i, 0)),
            whole_block(weight),
            whole_block(bias),
            whole_block(scorer),
        ],
        out_specs=[
            row_block,
            row_block,
            row_block,
            pl.BlockSpec((heads, VT, ROWS), lambda i: (0, 0, i)),
            pl.BlockSpec((heads, HD, ROWS), lambda i: (0, 0, i)),
        ],
        out_shape=[
            row_shape,
            row_shape,
            row_shape,
            jax.ShapeDtypeStruct((heads, VT, rows), BF16),
            jax.ShapeDtypeStruct((heads, HD, rows), BF16),
        ],
        compiler_params=pltpu.CompilerParams(vmem_limit_bytes=20 * MIB),
        cost_estimate=pl.CostEstimate(
            flops=4 * rows * width * cols, bytes_accessed=10 * MIB, transcendentals=0
        ),
        name="qkv_heads",
    )(norm_rows, weight, bias, scorer)


def attend_block(
    place, q_block, k0, qa_ref, ka_ref, vt_ref, bits_ref, bias_ref, total_ref, peak_ref, corner
):
    heads = qa_ref.shape[0]
    depth, first = corner
    queries = slice(first, QB)
    bias = bias_ref.at[0:depth, queries]
    keys = pl.ds(k0, depth)
    fill_bias(bias, bits_ref, q_block * QB + first, place * KB + k0)

    def scores_of(head):
        return dot(ka_ref[head, keys, :], qa_ref[head, queries, :], NT)

    ahead = scores_of(0)
    for head in range(heads):
        scores = ahead
        if head + 1 < heads:
            ahead = scores_of(head + 1)
        scores = scores * LOG2E + bias[...]
        old = peak_ref[head, :, queries]
        new = jnp.maximum(old, jnp.max(scores, axis=0, keepdims=True))
        weights = jnp.exp2(scores - new[0:1])
        shrink = jnp.exp2(old - new)
        peak_ref[head, :, queries] = new
        part = dot(vt_ref[head, :, keys], weights.astype(BF16))
        total_ref[head, :, queries] = total_ref[head, :, queries] * shrink[0:1] + part


def attend_blocks(count, place, q_block, *refs):
    def step(j, carry):
        k0 = pl.multiple_of(j * KB, KB)
        attend_block(place, q_block, k0, *refs, (KB, 0))
        return carry

    lax.fori_loop(0, count, step, 0)


def attend_diagonal(n, place, q_block, *refs):
    half = KB // 2
    k0 = pl.multiple_of(n * KB, KB)
    attend_block(place, q_block, k0, *refs, (half, 0))
    attend_block(place, q_block, pl.multiple_of(k0 + half, half), *refs, (half, half))


def attend_open(total_ref, peak_ref):
    total_ref[...] = jnp.zeros_like(total_ref)
    peak_ref[...] = jnp.full_like(peak_ref, NEG)


def attend_end(total_ref, peak_ref, out_ref, log_ref):
    heads = total_ref.shape[0]
    for pair in range(heads // 2):
        sides = []
        for head in (2 * pair, 2 * pair + 1):
            mass = total_ref[head, HD : HD + 1, :]
            sides.append(total_ref[head, 0:HD, :] / mass)
            log_ref[head] = peak_ref[head] + jnp.log(mass) * LOG2E
        both = jnp.concatenate(sides, axis=0).T
        out_ref[:, pair * LANES : (pair + 1) * LANES] = both.astype(BF16)


def attend_start_kernel(
    places_ref, qa_ref, ka_ref, vt_ref, bits_ref, total_ref, peak_ref, bias_ref
):
    own = places_ref[0]
    n = pl.program_id(0)
    refs = (qa_ref, ka_ref, vt_ref, bits_ref, bias_ref, total_ref, peak_ref)
    attend_open(total_ref, peak_ref)
    attend_blocks(n, own, own + n, *refs)
    attend_diagonal(n, own, own + n, *refs)


def attend_finish_kernel(
    n,
    places_ref,
    qa_ref,
    ka_ref,
    vt_ref,
    bits_ref,
    total_in_ref,
    peak_in_ref,
    out_ref,
    log_ref,
    bias_ref,
    total_ref,
    peak_ref,
):
    own, peer, later = places_ref[0], places_ref[1], places_ref[2]
    refs = (qa_ref, ka_ref, vt_ref, bits_ref, bias_ref, total_ref, peak_ref)
    total_ref[...] = total_in_ref[...]
    peak_ref[...] = peak_in_ref[...]
    attend_blocks(later * (ka_ref.shape[1] // KB), peer, own + n, *refs)
    attend_end(total_ref, peak_ref, out_ref, log_ref)


def attend_other_kernel(
    n,
    places_ref,
    qa_ref,
    ka_ref,
    vt_ref,
    ka_own_ref,
    vt_own_ref,
    bits_ref,
    out_ref,
    log_ref,
    bias_ref,
    total_ref,
    peak_ref,
):
    own, peer, later = places_ref[0], places_ref[1], places_ref[2]
    block = peer + n
    tail = (bits_ref, bias_ref, total_ref, peak_ref)
    attend_open(total_ref, peak_ref)
    for at in range(n):
        attend_block(peer, block, at * KB, qa_ref, ka_ref, vt_ref, *tail, (KB, 0))
    attend_diagonal(n, peer, block, qa_ref, ka_ref, vt_ref, *tail)
    earlier = (1 - later) * (ka_own_ref.shape[1] // KB)
    attend_blocks(earlier, own, block, qa_ref, ka_own_ref, vt_own_ref, *tail)
    attend_end(total_ref, peak_ref, out_ref, log_ref)


def attend_call(kernel, name, places, qa, others, count, first, state=(), keep=False):
    heads = qa.shape[0]
    total_spec = pl.BlockSpec((heads, VT, QB), lambda i, _: (0, 0, first + i))
    peak_spec = pl.BlockSpec((heads, 8, QB), lambda i, _: (0, 0, first + i))
    log_spec = pl.BlockSpec((heads, 8, QB), lambda i, _: (0, 0, i))
    total_shape = jax.ShapeDtypeStruct((heads, VT, count * QB), F32)
    peak_shape = jax.ShapeDtypeStruct((heads, 8, count * QB), F32)
    scratch = [
        pltpu.VMEM((KB, QB), F32),
        pltpu.VMEM((heads, VT, QB), F32),
        pltpu.VMEM((heads, 8, QB), F32),
    ]
    if keep:
        out_specs, out_shape = [total_spec, peak_spec], [total_shape, peak_shape]
        scratch = scratch[:1]
    else:
        out_specs = [pl.BlockSpec((QB, heads * HD), lambda i, _: (i, 0)), log_spec]
        out_shape = [jax.ShapeDtypeStruct((count * QB, heads * HD), BF16), peak_shape]
    return pl.pallas_call(
        kernel,
        grid_spec=pltpu.PrefetchScalarGridSpec(
            num_scalar_prefetch=1,
            grid=(count,),
            in_specs=[pl.BlockSpec((heads, QB, LANES), lambda i, _: (0, first + i, 0))]
            + [whole_block(array) for array in others]
            + ([total_spec, peak_spec] if state else []),
            out_specs=out_specs,
            scratch_shapes=scratch,
        ),
        out_shape=out_shape,
        compiler_params=pltpu.CompilerParams(vmem_limit_bytes=24 * MIB),
        cost_estimate=pl.CostEstimate(
            flops=2 * count * heads * QB * KB * 2048, bytes_accessed=8 * MIB, transcendentals=0
        ),
        name=name,
    )(places, qa, *others, *state)


def in_vmem():
    return pl.BlockSpec(memory_space=pltpu.VMEM)


def attend_back_kernel(
    own_queries,
    places_ref,
    qa_ref,
    ka_refs,
    kt_refs,
    va_refs,
    grad_refs,
    att_refs,
    log_refs,
    bits_ref,
    dq_ref,
    dk_refs,
    dv_refs,
    bias_ref,
    ga_ref,
):
    heads, rows, _ = qa_ref.shape
    blocks = rows // QB
    lanes = lane_ids(ROWS)
    dq_ref[...] = jnp.zeros_like(dq_ref)
    if own_queries:
        for ref in tuple(dk_refs) + tuple(dv_refs):
            ref[...] = jnp.zeros_like(ref)

    for n in range(len(grad_refs)):
        rows_n = slice(n * ROWS, (n + 1) * ROWS)
        for pair in range(heads // 2):
            cols = slice(pair * LANES, (pair + 1) * LANES)
            grad = grad_refs[n][:, cols].astype(F32)
            prod = grad * att_refs[n][:, cols].astype(F32)
            turned = pltpu.roll(grad, HD, 1)
            for side, values in enumerate((grad, turned)):
                mine = (lanes < HD) if side == 0 else (lanes >= HD)
                inner = jnp.sum(jnp.where(mine, prod, 0.0), axis=1, keepdims=True)
                plain = jnp.where(lanes < HD, values, 0.0)
                filled = put3(plain, lanes, HD, split3(-inner))
                ga_ref[pair * 2 + side, rows_n, :] = filled.astype(BF16)

    q_place, k_places = places_ref[0], (places_ref[0], places_ref[1])
    later = places_ref[2]
    if not own_queries:
        q_place, k_places = k_places[1], (k_places[1], k_places[0])
        later = 1 - later

    def tile(piece, j, n, i, corner):
        depth, first = corner
        width = QB - first
        k1 = pl.multiple_of(j * KB + first, KB // 2)
        q1 = pl.multiple_of(i * QB + first, QB // 2)
        keys = pl.ds(k1, depth)
        queries = pl.ds(q1, width)
        bias = bias_ref.at[0:depth, 0:width]
        fill_bias(bias, bits_ref, q_place * QB + q1, k_places[piece] * KB + k1)
        ka_ref, kt_ref, va_ref = ka_refs[piece], kt_refs[piece], va_refs[piece]
        dk_ref, dv_ref = dk_refs[piece], dv_refs[piece]

        def first_of(head):
            qa = qa_ref[head, queries, :]
            ga = ga_ref[head, queries, :]
            return (
                qa,
                ga,
                dot(ka_ref[head, keys, :], qa, NT),
                dot(va_ref[head, keys, :], ga, NT),
            )

        ahead = first_of(0)
        for head in range(heads):
            qa, ga, scores, inner = ahead
            if head + 1 < heads:
                ahead = first_of(head + 1)
            scores = scores * LOG2E + bias[...]
            if isinstance(n, int):
                logs = log_refs[n][head, 0:1, first:QB]
            else:
                logs = jnp.where(n == 0, log_refs[0][head, 0:1, :], log_refs[1][head, 0:1, :])
            probs = jnp.exp2(scores - logs)
            slopes = (probs * inner).astype(BF16)
            dv_ref[head, keys, :] += dot(probs.astype(BF16), ga)
            dk_ref[head, keys, :] += dot(slopes, qa)
            dq_ref[head, :, queries] += dot(kt_ref[head, :, keys], slopes)

    half = KB // 2
    for n in range(blocks):
        tile(0, n, n, n, (half, 0))
        tile(0, n, n, n, (half, half))
        for j in range(n):
            tile(0, j, n, n, (KB, 0))

    def step(at, carry):
        i = at & (blocks - 1)
        tile(1, at // blocks, i, i, (KB, 0))
        return carry

    lax.fori_loop(0, later * (blocks * blocks), step, 0)


def attend_back(own_queries, places, qa, keys, grads, atts, logs, bits, sums=None):
    heads, rows, _ = qa.shape
    count = len(grads)
    inputs = [places, qa]
    for kind in range(3):
        inputs += [keys[0][kind], keys[1][kind]]
    inputs += list(grads) + list(atts) + list(logs) + [bits]
    given = len(inputs)
    aliases = {}
    if sums is not None:
        aliases = {given + n: 1 + n for n in range(4)}
        inputs += list(sums)
    big = jax.ShapeDtypeStruct((heads, rows, LANES), F32)

    def kernel(*refs):
        places_ref, qa_ref = refs[:2]
        pairs = [refs[2 + 2 * n : 4 + 2 * n] for n in range(3)]
        lists = [refs[8 + n * count : 8 + (n + 1) * count] for n in range(3)]
        bits_ref = refs[8 + 3 * count]
        dq_ref, dk0, dk1, dv0, dv1, bias_ref, ga_ref = refs[len(inputs) :]
        attend_back_kernel(
            own_queries,
            places_ref,
            qa_ref,
            *pairs,
            *lists,
            bits_ref,
            dq_ref,
            (dk0, dk1),
            (dv0, dv1),
            bias_ref,
            ga_ref,
        )

    return pl.pallas_call(
        kernel,
        in_specs=[pl.BlockSpec(memory_space=pltpu.SMEM)] + [in_vmem()] * (len(inputs) - 1),
        out_specs=[in_vmem()] * 5,
        out_shape=[jax.ShapeDtypeStruct((heads, HD, rows), F32)] + [big] * 4,
        scratch_shapes=[pltpu.VMEM((KB, QB), F32), pltpu.VMEM((heads, rows, LANES), BF16)],
        input_output_aliases=aliases,
        compiler_params=pltpu.CompilerParams(vmem_limit_bytes=16 * MIB),
        cost_estimate=pl.CostEstimate(flops=1000000, bytes_accessed=MIB, transcendentals=0),
        name="attend_back",
    )(*inputs)


def join_kernel(
    dq_own_ref,
    dq_peer_ref,
    dk_own_ref,
    dk_peer_ref,
    dv_own_ref,
    dv_peer_ref,
    ka_own_ref,
    ka_peer_ref,
    norm_own_ref,
    norm_peer_ref,
    weight_ref,
    scorer_ref,
    one_own_ref,
    one_peer_ref,
    joined_ref,
    bias_out_ref,
    scorer_out_ref,
    plain_ref,
    times_ref,
):
    heads, rows, _ = dk_own_ref.shape
    span = 256
    lanes = lane_ids(span)
    real = lanes < HD
    for ref in (bias_out_ref, scorer_out_ref, plain_ref, times_ref):
        ref[...] = jnp.zeros_like(ref)

    def piece(first, dq_ref, dk_ref, dv_ref, ka_ref, norm_ref, one_ref):
        def step(at, carry):
            here = pl.ds(pl.multiple_of(at * span, span), span)
            there = pl.ds(pl.multiple_of(at * span + first, span), span)
            for pair in range(heads // 2):
                dq = dq_ref[2 * pair : 2 * pair + 2, :, here].reshape(LANES, span).T * 0.125
                dks, dvs = [], []
                for head in (2 * pair, 2 * pair + 1):
                    scorer = scorer_ref[head : head + 1, :]
                    key = ka_ref[head, here, :].astype(F32)
                    dk = dk_ref[head, here, :]
                    raw_gate = jnp.sum(key * scorer, axis=1, keepdims=True)
                    slope = dk[:, HD : HD + 1] / (1.0 + jnp.exp(raw_gate))
                    scorer_out_ref[head : head + 1, :] += sum_rows(slope * key)
                    dks.append(dk + slope * scorer)
                    dvs.append(dv_ref[head, here, :])
                blocks = (
                    jnp.where(real, dq, pltpu.roll(dks[0], HD, 1)),
                    jnp.where(real, dvs[0], dq),
                    jnp.where(real, dks[1], pltpu.roll(dvs[1], HD, 1)),
                )
                for n, block in enumerate(blocks):
                    cols = slice((pair * 3 + n) * LANES, (pair * 3 + n + 1) * LANES)
                    bias_out_ref[:, cols] += sum_rows(block)
                    joined_ref[there, cols] = block.astype(BF16)
            back = dot(joined_ref[there, :], weight_ref[...], NT)
            one_ref[here, :] = back.astype(one_ref.dtype)
            plain_ref[...] += sum_rows(back)
            times_ref[...] += sum_rows(back * norm_ref[here, :].astype(F32))
            return carry

        lax.fori_loop(0, rows // span, step, 0)

    piece(rows, dq_peer_ref, dk_peer_ref, dv_peer_ref, ka_peer_ref, norm_peer_ref, one_peer_ref)
    piece(0, dq_own_ref, dk_own_ref, dv_own_ref, ka_own_ref, norm_own_ref, one_own_ref)


def join(dqs, dks, dvs, kas, norms, weight, scorer):
    heads = dks[0].shape[0]
    rows, width = norms[0].shape
    cols = weight.shape[1]
    inputs = (*dqs, *dks, *dvs, *kas, *norms, weight, scorer)
    vector = jax.ShapeDtypeStruct((1, width), F32)
    return pl.pallas_call(
        join_kernel,
        in_specs=[in_vmem()] * len(inputs),
        out_specs=[in_vmem()] * 7,
        out_shape=[
            jax.ShapeDtypeStruct((rows, width), F32),
            jax.ShapeDtypeStruct((rows, width), BF16),
            jax.ShapeDtypeStruct((2 * rows, cols), BF16),
            jax.ShapeDtypeStruct((1, cols), F32),
            jax.ShapeDtypeStruct((heads, LANES), F32),
            vector,
            vector,
        ],
        compiler_params=pltpu.CompilerParams(vmem_limit_bytes=20 * MIB),
        cost_estimate=pl.CostEstimate(flops=1000000, bytes_accessed=MIB, transcendentals=0),
        name="join",
    )(*inputs)


SPAN = 256


def normalize(values):
    center = values - jnp.mean(values, axis=-1, keepdims=True)
    scale = lax.rsqrt(jnp.mean(center * center, axis=-1, keepdims=True) + 1e-05)
    return center * scale, scale


def norm_back(slope, hat, scale):
    means = jnp.mean(slope, axis=-1, keepdims=True)
    inner = jnp.mean(slope * hat, axis=-1, keepdims=True)
    return (slope - means - hat * inner) * scale


def row_spec(width, span=SPAN, skip=0):
    return pl.BlockSpec((span, width), lambda i, *_: (i + skip, 0))


def sum_rows(values):
    return jnp.sum(values, axis=0, keepdims=True)


def start_at_zero(*refs):
    @pl.when(pl.program_id(0) == 0)
    def _():
        for ref in refs:
            ref[...] = jnp.zeros_like(ref)


def rows_call(
    kernel, name, rows, inputs, in_specs, outs, flops, span=SPAN, scalars=(), earlier=()
):
    aliases = {}
    body = kernel
    if earlier:
        first = len(scalars) + len(inputs)
        aliases = {first + n: at for n, (at, _) in enumerate(earlier)}
        skip_from, skip_count = first, len(earlier)
        inputs = tuple(inputs) + tuple(array for _, array in earlier)
        in_specs = list(in_specs) + [pl.BlockSpec(memory_space=pl.ANY)] * len(earlier)

        def body(*refs):
            kernel(*refs[:skip_from], *refs[skip_from + skip_count :])

    return pl.pallas_call(
        body,
        grid_spec=pltpu.PrefetchScalarGridSpec(
            num_scalar_prefetch=len(scalars),
            grid=(rows // span,),
            in_specs=in_specs,
            out_specs=[
                pl.BlockSpec((1, width), lambda i, *_: (0, 0))
                if one
                else row_spec(width, span, start // span)
                for one, width, _, _, start in outs
            ],
        ),
        out_shape=[
            jax.ShapeDtypeStruct((1 if one else total, width), kind)
            for one, width, kind, total, _ in outs
        ],
        input_output_aliases=aliases,
        compiler_params=pltpu.CompilerParams(vmem_limit_bytes=24 * MIB),
        cost_estimate=pl.CostEstimate(
            flops=flops, bytes_accessed=8 * rows * 768, transcendentals=0
        ),
        name=name,
    )(*scalars, *inputs)


def norm_one_kernel(in_ref, grad_ref, gain_ref, shift_ref, out_ref, low_ref):
    hat, _ = normalize(in_ref[...])
    out_ref[...] = (hat * gain_ref[...] + shift_ref[...]).astype(BF16)
    low_ref[...] = grad_ref[...].astype(BF16)


def norm_one(layer_in, out_grad, gain, shift):
    rows, width = layer_in.shape
    vector = pl.BlockSpec((1, width), lambda i: (0, 0))
    return rows_call(
        norm_one_kernel,
        "norm_one",
        rows,
        (layer_in, out_grad, gain.reshape(1, width), shift.reshape(1, width)),
        [row_spec(width), row_spec(width), vector, vector],
        [(False, width, BF16, rows, 0), (False, width, BF16, rows, 0)],
        rows * width * 8,
    )


def mix_kernel(
    in_ref, own_ref, peer_ref, w_own_ref, w_peer_ref, bias_ref, gain_ref, shift_ref, mixed_ref, norm_ref
):
    part = dot(own_ref[...], w_own_ref[...]) + dot(peer_ref[...], w_peer_ref[...])
    mixed = in_ref[...] + part + bias_ref[...]
    mixed_ref[...] = mixed
    hat, _ = normalize(mixed)
    norm_ref[...] = (hat * gain_ref[...] + shift_ref[...]).astype(BF16)


def mix(layer_in, own, peer, w_own, w_peer, bias, gain, shift, start, earlier):
    total, width = layer_in.shape
    rows, depth = peer.shape
    skip = start // SPAN
    vector = pl.BlockSpec((1, width), lambda i: (0, 0))
    return rows_call(
        mix_kernel,
        "mix",
        rows,
        (layer_in, own, peer, w_own, w_peer)
        + tuple(v.reshape(1, width) for v in (bias, gain, shift)),
        [
            row_spec(width, skip=skip),
            row_spec(depth),
            row_spec(depth),
            whole_block(w_own),
            whole_block(w_peer),
        ]
        + [vector] * 3,
        [(False, width, F32, total, start), (False, width, BF16, rows, 0)],
        rows * width * depth * 4,
        earlier=earlier,
    )


def feed_kernel(
    norm_ref, grad_ref, fc_ref, bias_ref, proj_ref, active_ref, slope_ref, back_ref, sum_ref
):
    start_at_zero(sum_ref)
    units = fc_ref.shape[1]
    step = 512
    total = None
    for at in range(0, units, step):
        cols = slice(at, at + step)
        hidden = dot(norm_ref[...], fc_ref[:, cols]) + bias_ref[:, cols]
        grad = dot(grad_ref[...], proj_ref[cols, :], NT)
        square = hidden * hidden
        bend = jnp.tanh(hidden * (0.7978845608 + 0.7978845608 * 0.044715 * square))
        half = 0.5 + 0.5 * bend
        active_ref[:, cols] = (hidden * half).astype(BF16)
        inner = 0.7978845608 + 3.0 * 0.7978845608 * 0.044715 * square
        slope = grad * (half + 0.5 * hidden * (1.0 - bend * bend) * inner)
        low = slope.astype(BF16)
        slope_ref[:, cols] = low
        sum_ref[:, cols] += sum_rows(slope)
        part = dot(low, fc_ref[:, cols], NT)
        total = part if total is None else total + part
    back_ref[...] = total.astype(back_ref.dtype)


def feed(norm_rows, grad_rows, grad_start, fc, bias, proj, back_kind, start, total, earlier):
    rows, width = norm_rows.shape
    units = fc.shape[1]
    bias = bias.reshape(1, units)
    return rows_call(
        feed_kernel,
        "feed",
        rows,
        (norm_rows, grad_rows, fc, bias, proj),
        [
            row_spec(width),
            row_spec(width, skip=grad_start // SPAN),
            whole_block(fc),
            whole_block(bias),
            whole_block(proj),
        ],
        [
            (False, units, BF16, total, start),
            (False, units, BF16, total, start),
            (False, width, back_kind, rows, 0),
            (True, units, F32, 1, 0),
        ],
        rows * width * units * 6,
        earlier=earlier,
    )


def mix_back_kernel(
    mixed_ref,
    own_ref,
    other_ref,
    grad_ref,
    gain_ref,
    w_own_ref,
    w_peer_ref,
    out_ref,
    low_ref,
    att_own_ref,
    att_peer_ref,
    gain_out_ref,
    shift_out_ref,
    mixed_out_ref,
    grad_out_ref,
):
    start_at_zero(gain_out_ref, shift_out_ref, mixed_out_ref, grad_out_ref)
    hat, scale = normalize(mixed_ref[...])
    slope = own_ref[...] + other_ref[...].astype(F32)
    gain_out_ref[...] += sum_rows(slope * hat)
    shift_out_ref[...] += sum_rows(slope)
    grad = grad_ref[...]
    grad_out_ref[...] += sum_rows(grad)
    out = grad + norm_back(slope * gain_ref[...], hat, scale)
    mixed_out_ref[...] += sum_rows(out)
    out_ref[...] = out
    low = out.astype(BF16)
    low_ref[...] = low
    att_own_ref[...] = dot(low, w_own_ref[...], NT).astype(BF16)
    att_peer_ref[...] = dot(low, w_peer_ref[...], NT).astype(BF16)


def mix_back(mixed, own, other, grad, gain, w_own, w_peer, start, earlier):
    total, width = mixed.shape
    rows = other.shape[0]
    depth = w_own.shape[0]
    gain = gain.reshape(1, width)
    wide = row_spec(width)
    later = row_spec(width, skip=start // SPAN)
    return rows_call(
        mix_back_kernel,
        "mix_back",
        rows,
        (mixed, own, other, grad, gain, w_own, w_peer),
        [later, wide, wide, later, whole_block(gain), whole_block(w_own), whole_block(w_peer)],
        [
            (False, width, F32, total, start),
            (False, width, BF16, total, start),
            (False, depth, BF16, rows, 0),
            (False, depth, BF16, rows, 0),
            (True, width, F32, 1, 0),
            (True, width, F32, 1, 0),
            (True, width, F32, 1, 0),
            (True, width, F32, 1, 0),
        ],
        rows * width * depth * 4,
        earlier=earlier,
    )


def norm_one_back_kernel(in_ref, own_ref, other_ref, grad_ref, gain_ref, out_ref):
    hat, scale = normalize(in_ref[...])
    slope = (own_ref[...] + other_ref[...].astype(F32)) * gain_ref[...]
    out_ref[...] = grad_ref[...] + norm_back(slope, hat, scale)


def norm_one_back(layer_in, own, other, grad, gain, start, earlier):
    total, width = layer_in.shape
    rows = other.shape[0]
    gain = gain.reshape(1, width)
    later = row_spec(width, skip=start // SPAN)
    (out,) = rows_call(
        norm_one_back_kernel,
        "norm_one_back",
        rows,
        (layer_in, own, other, grad, gain),
        [later, later, row_spec(width), later, whole_block(gain)],
        [(False, width, F32, total, start)],
        rows * width * 20,
        earlier=earlier,
    )
    return out


def flip_bit(values, bit):
    total = lax.axis_size("dp")
    return lax.ppermute(values, "dp", [(n, n ^ (1 << bit)) for n in range(total)])


def flip_core(values):
    return flip_bit(values, 0)


def flip_tensor(values):
    return lax.ppermute(values, "tensor", [(0, 1), (1, 0)])


def rows_at(values, start, count):
    return lax.dynamic_slice_in_dim(values, start, count, 0)


def my_bit(bit):
    return (lax.axis_index("dp") >> bit) & 1


def add_low(one, two):
    return (one.astype(F32) + two.astype(F32)).astype(BF16)


def halve(values, bit):
    half = values.shape[0] // 2
    mine = my_bit(bit)
    return add_low(
        rows_at(values, mine * half, half),
        flip_bit(rows_at(values, (1 - mine) * half, half), bit),
    )


def both_sides(own, other, mine):
    return jnp.where(
        mine == 0,
        jnp.concatenate([own, other], axis=0),
        jnp.concatenate([other, own], axis=0),
    )


def double(values, bit):
    return both_sides(values, flip_bit(values, bit), my_bit(bit))


def ladder_orders():
    rest = list(range(1, lax.axis_size("dp").bit_length() - 1))
    return rest, rest[1:] + rest[:1]


def scatter_over_dp(values, beside):
    orders = ladder_orders()
    rows, cols = values.shape
    pieces = 2 * lax.axis_size("dp")
    mine = halve(values.reshape(pieces, rows // pieces, cols), 0)
    half = pieces // 4
    parts = [mine[:half], mine[half:]]
    for n in range(len(orders[0])):
        parts = [halve(part, order[n]) for part, order in zip(parts, orders)]
        if n == 0:
            parts, beside = lax.optimization_barrier((parts, beside))
    return parts, beside


def gather_over_dp(parts):
    orders = ladder_orders()
    for n in reversed(range(len(orders[0]))):
        parts = [double(part, order[n]) for part, order in zip(parts, orders)]
    whole = double(jnp.concatenate(parts, axis=0), 0)
    return whole.reshape(-1, whole.shape[-1])


def sum_over_all(values):
    values = values + flip_tensor(values)
    for bit in range(lax.axis_size("dp").bit_length() - 1):
        values = values + flip_bit(values, bit)
    return values


def in_half(vector, side):
    out = jnp.zeros((2 * vector.shape[0],), vector.dtype)
    return lax.dynamic_update_slice_in_dim(out, vector, side * vector.shape[0], 0)


def shards(
    layer_in,
    qkv_weight,
    qkv_bias,
    key_scorer,
    out_weight,
    out_bias,
    fc_weight,
    fc_bias,
    proj_weight,
    proj_bias,
    norm1_gain,
    norm1_shift,
    norm2_gain,
    norm2_shift,
    key_index,
    key_count,
    out_grad,
):
    side = lax.axis_index("tensor")
    own_rows = layer_in.shape[0]
    seq = key_index.shape[0]
    half = own_rows // 2
    blocks = own_rows // QB
    places = jnp.stack([side * blocks, (1 - side) * blocks, side]).astype(jnp.int32)

    starts = (0, half)
    norm_own, grad_low = norm_one(layer_in, out_grad, norm1_gain, norm1_shift)
    norm_peer = flip_tensor(norm_own)
    bits = allowed_bits(key_index, key_count)
    scorer = scorer_rows(key_scorer)
    bits, out_later = lax.optimization_barrier((bits, out_weight))
    out_peer = flip_tensor(out_later)

    own = qkv_heads(norm_own, qkv_weight, qkv_bias, scorer)
    own, grad_first = lax.optimization_barrier((own, grad_low[:half]))
    grad_peers = [flip_tensor(grad_first)]
    qa_own, ka_own, va_own, vt_own, kt_own = own
    state = attend_call(
        attend_start_kernel, "attend_start", places, qa_own, (ka_own, vt_own, bits), blocks, 0, (), True
    )
    state, norm_peer = lax.optimization_barrier((state, norm_peer))
    peer = qkv_heads(norm_peer, qkv_weight, qkv_bias, scorer)
    peer, grad_second = lax.optimization_barrier((peer, grad_low[half:]))
    grad_peers.append(flip_tensor(grad_second))
    qa_peer, ka_peer, va_peer, vt_peer, kt_peer = peer
    att_owns, logs_owns, att_sends, logs_sends, att_peers = [], [], [], [], []
    for n in range(blocks):
        att_send, logs_send = attend_call(
            functools.partial(attend_other_kernel, n),
            "attend_other",
            places,
            qa_peer,
            (ka_peer, vt_peer, ka_own, vt_own, bits),
            1,
            n,
        )
        att_own, logs_own = attend_call(
            functools.partial(attend_finish_kernel, n),
            "attend_finish",
            places,
            qa_own,
            (ka_peer, vt_peer, bits),
            1,
            n,
            state,
        )
        att_send, att_own, qa_peer, qa_own = lax.optimization_barrier(
            (att_send, att_own, qa_peer, qa_own)
        )
        if n == 0:
            att_send, grad_peers[0] = lax.optimization_barrier((att_send, grad_peers[0]))
        att_owns.append(att_own)
        logs_owns.append(logs_own)
        att_sends.append(att_send)
        logs_sends.append(logs_send)
        att_peers.append(flip_tensor(att_send))

    mixed = None
    normed, normed_peers = [], []
    for n, at in enumerate(starts):
        mixed, low = mix(
            layer_in,
            att_owns[n],
            att_peers[n],
            out_weight,
            out_peer,
            out_bias,
            norm2_gain,
            norm2_shift,
            at,
            () if mixed is None else ((0, mixed),),
        )
        normed.append(low)
        normed_peers.append(flip_tensor(low))
    active = slopes = None
    backs, back_others, fc_sums = [], [], []
    for n, rows in enumerate(normed + normed_peers):
        active, slopes, back, fc_sum = feed(
            rows,
            grad_low if n < 2 else grad_peers[n - 2],
            n * half if n < 2 else 0,
            fc_weight,
            fc_bias,
            proj_weight,
            F32 if n < 2 else BF16,
            n * half,
            seq,
            () if active is None else ((0, active), (1, slopes)),
        )
        fc_sums.append(fc_sum)
        if n < 2:
            backs.append(back)
        else:
            back_others.append(flip_tensor(back))
    grad_fc_bias = sum(fc_sums[1:], fc_sums[0]).reshape(-1)
    grad_fc_weight = dot(jnp.concatenate(normed + normed_peers, axis=0), slopes, TN)
    grad_proj_weight = dot(active, jnp.concatenate([grad_low] + grad_peers, axis=0), TN)
    proj_own = dot(active[:own_rows], proj_weight).astype(BF16)
    proj_send = dot(active[own_rows:], proj_weight).astype(BF16)
    grad_fc_weight = grad_fc_weight.astype(BF16)
    grad_proj_weight = grad_proj_weight.astype(BF16)
    mixed, grad_fc_weight, grad_proj_weight = lax.optimization_barrier(
        (mixed, grad_fc_weight, grad_proj_weight)
    )
    grad_mixed = grad_mixed_low = None
    grad_att_owns, grad_att_peers, row_sums = [], [], []
    for n, at in enumerate(starts):
        grad_mixed, grad_mixed_low, grad_att_own, grad_att_send, *some = mix_back(
            mixed,
            backs[n],
            back_others[n],
            out_grad,
            norm2_gain,
            out_weight,
            out_peer,
            at,
            ()
            if grad_mixed is None
            else ((0, grad_mixed), (1, grad_mixed_low)),
        )
        row_sums.append(some)
        grad_att_owns.append(grad_att_own)
        grad_att_peers.append(flip_tensor(grad_att_send))
    grad_norm2_gain, grad_norm2_shift, grad_out_bias, grad_proj_bias = (
        one + two for one, two in zip(*row_sums)
    )

    out_send = dot(grad_mixed_low, jnp.concatenate(att_peers, axis=0), TN).astype(BF16)
    out_keep = dot(grad_mixed_low, jnp.concatenate(att_owns, axis=0), TN)
    grad_fc_weight, grad_proj_weight = lax.psum((grad_fc_weight, grad_proj_weight), "dp")
    own_keys, peer_keys = (ka_own, kt_own, va_own), (ka_peer, kt_peer, va_peer)
    _, proj_send, out_send = lax.optimization_barrier((grad_att_send, proj_send, out_send))
    proj_other = flip_tensor(proj_send)
    out_other = flip_tensor(out_send)
    norm_all = jnp.concatenate([norm_own, norm_peer], axis=0)
    qa_own, proj_send, proj_own, out_send, out_keep, norm_all = lax.optimization_barrier(
        (qa_own, proj_send, proj_own, out_send, out_keep, norm_all)
    )
    dq_own, *key_sums = attend_back(
        True, places, qa_own, (own_keys, peer_keys), grad_att_owns, att_owns, logs_owns, bits
    )
    swapped = (key_sums[1], key_sums[0], key_sums[3], key_sums[2])
    dq_peer, *key_sums = attend_back(
        False,
        places,
        qa_peer,
        (peer_keys, own_keys),
        grad_att_peers,
        att_sends,
        logs_sends,
        bits,
        swapped,
    )
    key_sums, proj_other, out_other = lax.optimization_barrier((key_sums, proj_other, out_other))
    dk_peer, dk_own, dv_peer, dv_own = key_sums
    one_own, one_send, joined, grad_qkv_bias, grad_key_scorer, plain_sum, times_sum = join(
        (dq_own, dq_peer),
        (dk_own, dk_peer),
        (dv_own, dv_peer),
        (ka_own, ka_peer),
        (norm_own, norm_peer),
        qkv_weight,
        scorer,
    )
    grad_key_scorer = grad_key_scorer[:, :HD].reshape(-1)
    grad_qkv_bias = grad_qkv_bias.reshape(-1)
    one_other = flip_tensor(one_send)
    grad_qkv_weight = dot(norm_all, joined, TN).astype(BF16)
    layer_out = mixed + (proj_own.astype(F32) + proj_other.astype(F32)) + proj_bias
    grad_out_turned = add_low(out_keep, out_other)
    scattered, (grad_fc_weight, grad_proj_weight) = scatter_over_dp(
        jnp.concatenate([grad_qkv_weight, grad_out_turned], axis=1),
        (grad_fc_weight, grad_proj_weight),
    )
    scattered, one_other = lax.optimization_barrier((scattered, one_other))
    last = gather_over_dp(scattered)
    joined_cols = qkv_weight.shape[1]
    grad_qkv_weight = last[:, :joined_cols]
    grad_out_weight = last[:, joined_cols:].T
    input_grad = norm_one_back(layer_in, one_own, one_other, grad_mixed, norm1_gain, 0, ())

    sums = [
        grad_out_bias,
        grad_proj_bias,
        times_sum,
        plain_sum,
        grad_norm2_gain,
        grad_norm2_shift,
        in_half(grad_qkv_bias, side),
        in_half(grad_key_scorer, side),
        in_half(grad_fc_bias, side),
    ]
    sums = [part.reshape(-1) for part in sums]
    packed = sum_over_all(jnp.concatenate(sums).reshape(-1, LANES)).reshape(-1)
    ends = []
    at = 0
    for part in sums:
        ends.append(packed[at : at + part.shape[0]])
        at += part.shape[0]
    grad_norm1_shift = ends[3]
    grad_norm1_gain = (ends[2] - norm1_shift * ends[3]) / norm1_gain

    def mine_of(vector):
        half = vector.shape[0] // 2
        return lax.dynamic_slice_in_dim(vector, side * half, half, 0)

    return (
        layer_out,
        input_grad,
        grad_qkv_weight.astype(F32),
        mine_of(ends[6]),
        mine_of(ends[7]),
        grad_out_weight.astype(F32),
        ends[0],
        grad_fc_weight.astype(F32),
        mine_of(ends[8]),
        grad_proj_weight.astype(F32),
        ends[1],
        grad_norm1_gain,
        grad_norm1_shift,
        ends[4],
        ends[5],
    )


def solution(mesh):
    rows = P(("dp", "tensor"), None)
    in_specs = (
        rows,
        P(None, "tensor"),
        P("tensor"),
        P("tensor"),
        P("tensor", None),
        P(),
        P(None, "tensor"),
        P("tensor"),
        P("tensor", None),
        P(),
        P(),
        P(),
        P(),
        P(),
        P("dp", None),
        P("dp"),
        rows,
    )
    out_specs = (
        rows,
        rows,
        P(None, "tensor"),
        P("tensor"),
        P("tensor"),
        P("tensor", None),
        P(),
        P(None, "tensor"),
        P("tensor"),
        P("tensor", None),
        P(),
        P(),
        P(),
        P(),
        P(),
    )
    return jax.shard_map(shards, mesh=mesh, in_specs=in_specs, out_specs=out_specs, check_vma=False)
```

```python
import functools
import math

import jax
import jax.numpy as jnp
from jax import lax
from jax.experimental import pallas as pl
from jax.experimental.pallas import tpu as pltpu
from jax.sharding import PartitionSpec as P

HD = 64
LANES = 128
WIN = 64
LOG2E = math.log2(math.e)
LN2 = math.log(2.0)
NEG = -1e30
QB = 512
KB = 512
ROWS = 512
VT = 80
NT = (((1,), (1,)), ((), ()))
NN = (((1,), (0,)), ((), ()))
TN = (((0,), (0,)), ((), ()))
F32 = jnp.float32
BF16 = jnp.bfloat16
MIB = 1024 * 1024
SMALL = pl.CostEstimate(flops=1000, bytes_accessed=1000, transcendentals=0)


def dot(a, b, dims=NN):
    return lax.dot_general(a, b, dims, preferred_element_type=F32)


def split3(x):
    hi = x.astype(BF16).astype(F32)
    rest = x - hi
    mid = rest.astype(BF16).astype(F32)
    low = (rest - mid).astype(BF16).astype(F32)
    return hi, mid, low


def lane_ids(rows):
    return lax.broadcasted_iota(jnp.int32, (rows, LANES), 1)


def put3(base, lanes, first, parts):
    out = base
    for n, part in enumerate(parts):
        out = jnp.where(lanes == first + n, part, out)
    return out


def whole_block(array):
    return pl.BlockSpec(memory_space=pltpu.VMEM)


def scorer_rows(key_scorer):
    return jnp.pad(key_scorer.reshape(-1, HD), ((0, 0), (0, LANES - HD)))


def bits_kernel(low_ref, flag_ref, bits_ref):
    width = bits_ref.shape[1]
    first = pl.program_id(0) * width
    lane = lax.broadcasted_iota(jnp.int32, (LANES, width), 0)
    pos = lax.broadcasted_iota(jnp.int32, (LANES, width), 1) + first
    back = (pos - lane) & (LANES - 1)
    at = pos - back
    bits = jnp.where((back < WIN) & (at >= 0), 1 << (jnp.maximum(at, 0) >> 7), 0)
    for slot in range(low_ref.shape[0]):
        hit = low_ref[slot : slot + 1, :] == lane
        bits = bits | jnp.where(hit, flag_ref[slot : slot + 1, :], 0)
    bits_ref[...] = bits


def allowed_bits(key_index, key_count):
    seq = key_index.shape[0]
    index = key_index.T
    slots = index.shape[0]
    slot = lax.broadcasted_iota(jnp.int32, index.shape, 0)
    used = (slot < key_count[None, :]) & (index >= 0)
    low = index & (LANES - 1)
    flag = jnp.where(used, 1 << (jnp.maximum(index, 0) >> 7), 0)
    width = 256
    spec = pl.BlockSpec((slots, width), lambda i: (0, i))
    return pl.pallas_call(
        bits_kernel,
        grid=(seq // width,),
        in_specs=[spec, spec],
        out_specs=pl.BlockSpec((LANES, width), lambda i: (0, i)),
        out_shape=jax.ShapeDtypeStruct((LANES, seq), jnp.int32),
        cost_estimate=SMALL,
        name="allowed_bits",
    )(low, flag)


def fill_bias(bias_ref, bits_ref, q0, k0):
    depth, width = bias_ref.shape
    bits = bits_ref[:, pl.ds(q0, width)]
    for part in range(depth // LANES):
        shift = k0 // LANES + part
        seen = ((bits >> shift) & 1) == 1
        bias_ref[part * LANES : (part + 1) * LANES, :] = jnp.where(seen, 0.0, NEG)


def qkv_kernel(
    norm_ref, weight_ref, bias_ref, scorer_ref, qa_ref, ka_ref, va_ref, vt_ref, kt_ref
):
    rows = norm_ref.shape[0]
    heads = qa_ref.shape[0]
    lanes = lane_ids(rows)
    real = lanes < HD
    ones = jnp.where((lanes >= HD) & (lanes < HD + 3), 1.0, 0.0)
    for pair in range(heads // 2):
        cols = slice(pair * 6 * HD, (pair + 1) * 6 * HD)
        raw = dot(norm_ref[...], weight_ref[:, cols]) + bias_ref[:, cols]
        raw = raw.astype(BF16).astype(F32)
        blocks = [raw[:, n * LANES : (n + 1) * LANES] for n in range(3)]
        turned = [pltpu.roll(block, HD, 1) for block in blocks]
        groups = (
            (blocks[0], turned[0], blocks[1]),
            (turned[1], blocks[2], turned[2]),
        )
        for side, (query, key, value) in enumerate(groups):
            head = pair * 2 + side
            raw_gate = jnp.sum(key * scorer_ref[head : head + 1, :], axis=1, keepdims=True)
            gate = jnp.minimum(raw_gate, 0.0) - jnp.log1p(jnp.exp(-jnp.abs(raw_gate)))
            key_plain = jnp.where(real, key, 0.0)
            value_ones = jnp.where(real, value, ones)
            qa_ref[head] = jnp.where(real, query * 0.125, ones).astype(BF16)
            ka_ref[head] = put3(key_plain, lanes, HD, split3(gate)).astype(BF16)
            va_ref[head] = value_ones.astype(BF16)
            vt_ref[head] = value_ones.T[:VT, :].astype(BF16)
            kt_ref[head] = key_plain.T[:HD, :].astype(BF16)


def qkv_heads(norm_rows, weight, bias, scorer):
    rows, width = norm_rows.shape
    heads = scorer.shape[0]
    cols = weight.shape[1]
    row_shape = jax.ShapeDtypeStruct((heads, rows, LANES), BF16)
    row_block = pl.BlockSpec((heads, ROWS, LANES), lambda i: (0, i, 0))
    bias = bias.reshape(1, cols)
    return pl.pallas_call(
        qkv_kernel,
        grid=(rows // ROWS,),
        in_specs=[
            pl.BlockSpec((ROWS, width), lambda i: (i, 0)),
            whole_block(weight),
            whole_block(bias),
            whole_block(scorer),
        ],
        out_specs=[
            row_block,
            row_block,
            row_block,
            pl.BlockSpec((heads, VT, ROWS), lambda i: (0, 0, i)),
            pl.BlockSpec((heads, HD, ROWS), lambda i: (0, 0, i)),
        ],
        out_shape=[
            row_shape,
            row_shape,
            row_shape,
            jax.ShapeDtypeStruct((heads, VT, rows), BF16),
            jax.ShapeDtypeStruct((heads, HD, rows), BF16),
        ],
        compiler_params=pltpu.CompilerParams(vmem_limit_bytes=14 * MIB),
        cost_estimate=SMALL,
        name="qkv_heads",
    )(norm_rows, weight, bias, scorer)


def attend_block(
    place, q_block, k0, qa_ref, ka_ref, vt_ref, bits_ref, bias_ref, total_ref, peak_ref, corner
):
    heads = qa_ref.shape[0]
    depth, first = corner
    queries = slice(first, QB)
    bias = bias_ref.at[0:depth, queries]
    keys = pl.ds(k0, depth)
    fill_bias(bias, bits_ref, q_block * QB + first, place * KB + k0)

    def scores_of(head):
        return dot(ka_ref[head, keys, :], qa_ref[head, queries, :], NT)

    ahead = scores_of(0)
    for head in range(heads):
        scores = ahead
        if head + 1 < heads:
            ahead = scores_of(head + 1)
        scores = scores * LOG2E + bias[...]
        old = peak_ref[head, :, queries]
        new = jnp.maximum(old, jnp.max(scores, axis=0, keepdims=True))
        weights = jnp.exp2(scores - new[0:1])
        shrink = jnp.exp2(old - new)
        peak_ref[head, :, queries] = new
        part = dot(vt_ref[head, :, keys], weights.astype(BF16))
        total_ref[head, :, queries] = total_ref[head, :, queries] * shrink[0:1] + part


def attend_blocks(count, place, q_block, *refs):
    def step(j, carry):
        k0 = pl.multiple_of(j * KB, KB)
        attend_block(place, q_block, k0, *refs, (KB, 0))
        return carry

    lax.fori_loop(0, count, step, 0)


def attend_diagonal(n, place, q_block, *refs):
    half = KB // 2
    k0 = pl.multiple_of(n * KB, KB)
    attend_block(place, q_block, k0, *refs, (half, 0))
    attend_block(place, q_block, pl.multiple_of(k0 + half, half), *refs, (half, half))


def attend_open(total_ref, peak_ref):
    total_ref[...] = jnp.zeros_like(total_ref)
    peak_ref[...] = jnp.full_like(peak_ref, NEG)


def attend_end(total_ref, peak_ref, out_ref, log_ref):
    heads = total_ref.shape[0]
    for pair in range(heads // 2):
        sides = []
        for head in (2 * pair, 2 * pair + 1):
            mass = total_ref[head, HD : HD + 1, :]
            sides.append(total_ref[head, 0:HD, :] / mass)
            log_ref[head] = peak_ref[head] + jnp.log(mass) * LOG2E
        both = jnp.concatenate(sides, axis=0).T
        out_ref[:, pair * LANES : (pair + 1) * LANES] = both.astype(BF16)


def attend_start_kernel(
    places_ref, qa_ref, ka_ref, vt_ref, bits_ref, total_ref, peak_ref, bias_ref
):
    own = places_ref[0]
    n = pl.program_id(0)
    refs = (qa_ref, ka_ref, vt_ref, bits_ref, bias_ref, total_ref, peak_ref)
    attend_open(total_ref, peak_ref)
    attend_blocks(n, own, own + n, *refs)
    attend_diagonal(n, own, own + n, *refs)


def attend_finish_kernel(
    n,
    places_ref,
    qa_ref,
    ka_ref,
    vt_ref,
    bits_ref,
    total_in_ref,
    peak_in_ref,
    out_ref,
    log_ref,
    bias_ref,
    total_ref,
    peak_ref,
):
    own, peer, later = places_ref[0], places_ref[1], places_ref[2]
    refs = (qa_ref, ka_ref, vt_ref, bits_ref, bias_ref, total_ref, peak_ref)
    total_ref[...] = total_in_ref[...]
    peak_ref[...] = peak_in_ref[...]
    attend_blocks(later * (ka_ref.shape[1] // KB), peer, own + n, *refs)
    attend_end(total_ref, peak_ref, out_ref, log_ref)


def attend_other_kernel(
    n,
    places_ref,
    qa_ref,
    ka_ref,
    vt_ref,
    ka_own_ref,
    vt_own_ref,
    bits_ref,
    out_ref,
    log_ref,
    bias_ref,
    total_ref,
    peak_ref,
):
    own, peer, later = places_ref[0], places_ref[1], places_ref[2]
    block = peer + n
    tail = (bits_ref, bias_ref, total_ref, peak_ref)
    attend_open(total_ref, peak_ref)
    for at in range(n):
        attend_block(peer, block, at * KB, qa_ref, ka_ref, vt_ref, *tail, (KB, 0))
    attend_diagonal(n, peer, block, qa_ref, ka_ref, vt_ref, *tail)
    earlier = (1 - later) * (ka_own_ref.shape[1] // KB)
    attend_blocks(earlier, own, block, qa_ref, ka_own_ref, vt_own_ref, *tail)
    attend_end(total_ref, peak_ref, out_ref, log_ref)


def attend_call(kernel, name, places, qa, others, count, first, state=(), keep=False):
    heads = qa.shape[0]
    total_spec = pl.BlockSpec((heads, VT, QB), lambda i, _: (0, 0, first + i))
    peak_spec = pl.BlockSpec((heads, 8, QB), lambda i, _: (0, 0, first + i))
    log_spec = pl.BlockSpec((heads, 8, QB), lambda i, _: (0, 0, i))
    total_shape = jax.ShapeDtypeStruct((heads, VT, count * QB), F32)
    peak_shape = jax.ShapeDtypeStruct((heads, 8, count * QB), F32)
    scratch = [
        pltpu.VMEM((KB, QB), F32),
        pltpu.VMEM((heads, VT, QB), F32),
        pltpu.VMEM((heads, 8, QB), F32),
    ]
    if keep:
        out_specs, out_shape = [total_spec, peak_spec], [total_shape, peak_shape]
        scratch = scratch[:1]
    else:
        out_specs = [pl.BlockSpec((QB, heads * HD), lambda i, _: (i, 0)), log_spec]
        out_shape = [jax.ShapeDtypeStruct((count * QB, heads * HD), BF16), peak_shape]
    return pl.pallas_call(
        kernel,
        grid_spec=pltpu.PrefetchScalarGridSpec(
            num_scalar_prefetch=1,
            grid=(count,),
            in_specs=[pl.BlockSpec((heads, QB, LANES), lambda i, _: (0, first + i, 0))]
            + [whole_block(array) for array in others]
            + ([total_spec, peak_spec] if state else []),
            out_specs=out_specs,
            scratch_shapes=scratch,
        ),
        out_shape=out_shape,
        compiler_params=pltpu.CompilerParams(vmem_limit_bytes=16 * MIB),
        cost_estimate=SMALL,
        name=name,
    )(places, qa, *others, *state)


def in_vmem():
    return pl.BlockSpec(memory_space=pltpu.VMEM)


def attend_back_kernel(
    own_queries,
    places_ref,
    qa_ref,
    ka_refs,
    kt_refs,
    va_refs,
    grad_refs,
    att_refs,
    log_refs,
    bits_ref,
    dq_ref,
    dk_refs,
    dv_refs,
    bias_ref,
    ga_ref,
):
    heads, rows, _ = qa_ref.shape
    blocks = rows // QB
    lanes = lane_ids(ROWS)
    dq_ref[...] = jnp.zeros_like(dq_ref)
    if own_queries:
        for ref in tuple(dk_refs) + tuple(dv_refs):
            ref[...] = jnp.zeros_like(ref)

    for n in range(len(grad_refs)):
        rows_n = slice(n * ROWS, (n + 1) * ROWS)
        for pair in range(heads // 2):
            cols = slice(pair * LANES, (pair + 1) * LANES)
            grad = grad_refs[n][:, cols].astype(F32)
            prod = grad * att_refs[n][:, cols].astype(F32)
            turned = pltpu.roll(grad, HD, 1)
            for side, values in enumerate((grad, turned)):
                mine = (lanes < HD) if side == 0 else (lanes >= HD)
                inner = jnp.sum(jnp.where(mine, prod, 0.0), axis=1, keepdims=True)
                plain = jnp.where(lanes < HD, values, 0.0)
                filled = put3(plain, lanes, HD, split3(-inner))
                ga_ref[pair * 2 + side, rows_n, :] = filled.astype(BF16)

    q_place, k_places = places_ref[0], (places_ref[0], places_ref[1])
    later = places_ref[2]
    if not own_queries:
        q_place, k_places = k_places[1], (k_places[1], k_places[0])
        later = 1 - later

    def tile(piece, j, n, i, corner):
        depth, first = corner
        width = QB - first
        k1 = pl.multiple_of(j * KB + first, KB // 2)
        q1 = pl.multiple_of(i * QB + first, QB // 2)
        keys = pl.ds(k1, depth)
        queries = pl.ds(q1, width)
        bias = bias_ref.at[0:depth, 0:width]
        fill_bias(bias, bits_ref, q_place * QB + q1, k_places[piece] * KB + k1)
        ka_ref, kt_ref, va_ref = ka_refs[piece], kt_refs[piece], va_refs[piece]
        dk_ref, dv_ref = dk_refs[piece], dv_refs[piece]

        def first_of(head):
            qa = qa_ref[head, queries, :]
            ga = ga_ref[head, queries, :]
            return (
                qa,
                ga,
                dot(ka_ref[head, keys, :], qa, NT),
                dot(va_ref[head, keys, :], ga, NT),
            )

        ahead = first_of(0)
        for head in range(heads):
            qa, ga, scores, inner = ahead
            if head + 1 < heads:
                ahead = first_of(head + 1)
            scores = scores * LOG2E + bias[...]
            if isinstance(n, int):
                logs = log_refs[n][head, 0:1, first:QB]
            else:
                logs = jnp.where(n == 0, log_refs[0][head, 0:1, :], log_refs[1][head, 0:1, :])
            probs = jnp.exp2(scores - logs)
            slopes = (probs * inner).astype(BF16)
            dv_ref[head, keys, :] += dot(probs.astype(BF16), ga)
            dk_ref[head, keys, :] += dot(slopes, qa)
            dq_ref[head, :, queries] += dot(kt_ref[head, :, keys], slopes)

    half = KB // 2
    for n in range(blocks):
        tile(0, n, n, n, (half, 0))
        tile(0, n, n, n, (half, half))
        for j in range(n):
            tile(0, j, n, n, (KB, 0))

    def step(at, carry):
        i = at & (blocks - 1)
        tile(1, at // blocks, i, i, (KB, 0))
        return carry

    lax.fori_loop(0, later * (blocks * blocks), step, 0)


def join_piece(first, scorer_ref, dq_ref, dk_ref, dv_ref, ka_ref, joined_ref, bias_out_ref, scorer_out_ref):
    heads, rows, _ = dk_ref.shape
    span = 256
    lanes = lane_ids(span)
    real = lanes < HD

    def step(at, carry):
        here = pl.ds(pl.multiple_of(at * span, span), span)
        there = pl.ds(pl.multiple_of(at * span + first, span), span)
        for pair in range(heads // 2):
            dq = dq_ref[2 * pair : 2 * pair + 2, :, here].reshape(LANES, span).T * 0.125
            dks, dvs = [], []
            for head in (2 * pair, 2 * pair + 1):
                scorer = scorer_ref[head : head + 1, :]
                key = ka_ref[head, here, :].astype(F32)
                dk = dk_ref[head, here, :]
                raw_gate = jnp.sum(key * scorer, axis=1, keepdims=True)
                slope = dk[:, HD : HD + 1] / (1.0 + jnp.exp(raw_gate))
                scorer_out_ref[head : head + 1, :] += sum_rows(slope * key)
                dks.append(dk + slope * scorer)
                dvs.append(dv_ref[head, here, :])
            blocks = (
                jnp.where(real, dq, pltpu.roll(dks[0], HD, 1)),
                jnp.where(real, dvs[0], dq),
                jnp.where(real, dks[1], pltpu.roll(dvs[1], HD, 1)),
            )
            for n, block in enumerate(blocks):
                cols = slice((pair * 3 + n) * LANES, (pair * 3 + n + 1) * LANES)
                bias_out_ref[:, cols] += sum_rows(block)
                joined_ref[there, cols] = block.astype(BF16)
        return carry

    lax.fori_loop(0, rows // span, step, 0)


def attend_back(own_queries, places, qa, keys, grads, atts, logs, bits, sums=None):
    heads, rows, _ = qa.shape
    count = len(grads)
    inputs = [places, qa]
    for kind in range(3):
        inputs += [keys[0][kind], keys[1][kind]]
    inputs += list(grads) + list(atts) + list(logs) + [bits]
    given = len(inputs)
    aliases = {}
    dq_shape = jax.ShapeDtypeStruct((heads, HD, rows), F32)
    sum_shapes = [jax.ShapeDtypeStruct((heads, rows, LANES), F32)] * 4
    out_shape = [dq_shape] + sum_shapes
    scratch = [pltpu.VMEM((KB, QB), F32), pltpu.VMEM((heads, rows, LANES), BF16)]
    if not own_queries:
        aliases = {given + n: n for n in range(4)}
        inputs += list(sums)
        cols = 3 * HD * heads
        out_shape = sum_shapes + [
            jax.ShapeDtypeStruct((2 * rows, cols), BF16),
            jax.ShapeDtypeStruct((1, cols), F32),
            jax.ShapeDtypeStruct((heads, LANES), F32),
        ]
        scratch.append(pltpu.VMEM((heads, HD, rows), F32))

    def kernel(*refs):
        places_ref, qa_ref = refs[:2]
        pairs = [refs[2 + 2 * n : 4 + 2 * n] for n in range(3)]
        lists = [refs[8 + n * count : 8 + (n + 1) * count] for n in range(3)]
        bits_ref = refs[8 + 3 * count]
        outs = refs[len(inputs) :]
        if own_queries:
            dq_ref, dk0, dk1, dv0, dv1, bias_ref, ga_ref = outs
        else:
            dk0, dk1, dv0, dv1, joined_ref, bias_out_ref, scorer_out_ref = outs[:7]
            bias_ref, ga_ref, dq_ref = outs[7:]
        attend_back_kernel(
            own_queries,
            places_ref,
            qa_ref,
            *pairs,
            *lists,
            bits_ref,
            dq_ref,
            (dk0, dk1),
            (dv0, dv1),
            bias_ref,
            ga_ref,
        )
        if not own_queries:
            dq_own_ref, scorer_ref = refs[given + 4 : given + 6]
            bias_out_ref[...] = jnp.zeros_like(bias_out_ref)
            scorer_out_ref[...] = jnp.zeros_like(scorer_out_ref)
            ends = (joined_ref, bias_out_ref, scorer_out_ref)
            join_piece(rows, scorer_ref, dq_ref, dk0, dv0, pairs[0][0], *ends)
            join_piece(0, scorer_ref, dq_own_ref, dk1, dv1, pairs[0][1], *ends)

    return pl.pallas_call(
        kernel,
        in_specs=[pl.BlockSpec(memory_space=pltpu.SMEM)] + [in_vmem()] * (len(inputs) - 1),
        out_specs=[in_vmem()] * len(out_shape),
        out_shape=out_shape,
        scratch_shapes=scratch,
        input_output_aliases=aliases,
        compiler_params=pltpu.CompilerParams(vmem_limit_bytes=16 * MIB),
        cost_estimate=SMALL,
        name="attend_back",
    )(*inputs)


def turned_product(parts, others, name, tile=256, chunks=1):
    across = parts[0].shape[1]
    width = others[0].shape[1]
    lengths = [part.shape[0] for part in parts]
    sizes = [other.shape[0] for other in others]
    cuts = sorted({sum(lengths[:n]) for n in range(len(lengths) + 1)} | {sum(sizes[:n]) for n in range(len(sizes) + 1)})

    def rows_of(refs, counts, start, stop):
        base = 0
        for ref, count in zip(refs, counts):
            if base <= start < base + count:
                return ref[start - base : stop - base, :]
            base += count

    def kernel(*refs):
        out_refs = refs[-chunks:]
        lefts, rights = refs[: len(parts)], refs[len(parts) : -chunks]
        total = None
        for start, stop in zip(cuts[:-1], cuts[1:]):
            left = rows_of(lefts, lengths, start, stop)
            part = dot(left, rows_of(rights, sizes, start, stop), TN)
            total = part if total is None else total + part
        value = total.astype(BF16)
        if chunks == 1:
            out_refs[0][...] = value
            return
        for n, ref in enumerate(out_refs):

            @pl.when(pl.program_id(0) == n)
            def _():
                ref[...] = value

    out = pl.pallas_call(
        kernel,
        grid=(across // tile,),
        in_specs=[pl.BlockSpec((n, tile), lambda i: (0, i)) for n in lengths]
        + [whole_block(other) for other in others],
        out_specs=[pl.BlockSpec((tile, width), lambda i: (i if chunks == 1 else 0, 0))] * chunks,
        out_shape=[jax.ShapeDtypeStruct((across // chunks, width), BF16)] * chunks,
        compiler_params=pltpu.CompilerParams(vmem_limit_bytes=20 * MIB),
        cost_estimate=SMALL,
        name=name,
    )(*parts, *others)
    return out[0] if chunks == 1 else out


def choose(refs, at):
    value = refs[0][...]
    for n in range(1, len(refs)):
        value = jnp.where(at == n, refs[n][...], value)
    return value


def chunk_spec(array):
    return pl.BlockSpec(array.shape, lambda i: (0, 0))


def product(rows, weight, dims, first, count, kind, name, chunks=1):
    depth = rows.shape[1]
    width = weight.shape[1] if dims == NN else weight.shape[0]
    span = count // max(chunks, 2)
    shape = (count // chunks, width)

    def kernel(rows_ref, weight_ref, *out_refs):
        value = dot(rows_ref[...], weight_ref[...], dims).astype(kind)
        if chunks == 1:
            out_refs[0][...] = value
            return
        for n, ref in enumerate(out_refs):

            @pl.when(pl.program_id(0) == n)
            def _():
                ref[...] = value

    return pl.pallas_call(
        kernel,
        grid=(count // span,),
        in_specs=[
            pl.BlockSpec((span, depth), lambda i: (first // span + i, 0)),
            whole_block(weight),
        ],
        out_specs=[pl.BlockSpec((span, width), lambda i: (i if chunks == 1 else 0, 0))] * chunks,
        out_shape=[jax.ShapeDtypeStruct(shape, kind)] * chunks,
        compiler_params=pltpu.CompilerParams(vmem_limit_bytes=16 * MIB),
        cost_estimate=SMALL,
        name=name,
    )(rows, weight)


def end_kernel(mixed_ref, active_ref, weight_ref, bias_ref, *refs):
    other = choose(refs[:-1], pl.program_id(0)).astype(F32)
    own = dot(active_ref[...], weight_ref[...])
    refs[-1][...] = mixed_ref[...] + (own + other) + bias_ref[...]


def layer_end(mixed, active, weight, bias, others, start, earlier):
    total, width = mixed.shape
    span, units = others[0].shape[0], weight.shape[0]
    bias = bias.reshape(1, width)
    (out,) = rows_call(
        end_kernel,
        "layer_end",
        span * len(others),
        (mixed, active, weight, bias, *others),
        [
            row_spec(width, span, start // span),
            row_spec(units, span, start // span),
            whole_block(weight),
            whole_block(bias),
        ]
        + [chunk_spec(other) for other in others],
        [(False, width, F32, total, start)],
        0,
        span=span,
        earlier=earlier,
    )
    return out


def pack_kernel(side_ref, weight_ref, joined_ref, bias_ref, scorer_ref, *refs):
    fulls, (fc_ref, out_ref) = refs[:-2], refs[-2:]
    width = fulls[0].shape[1]
    weight = weight_ref[...]
    ones = jnp.ones((8, weight.shape[1]), BF16)
    wide = weight.astype(F32) * joined_ref[...].astype(F32)
    times = sum(dot(ones, part.astype(BF16), NT) for part in split3(wide))
    rows = jnp.broadcast_to(bias_ref[...], (8, weight.shape[1]))
    plain = sum(dot(part.astype(BF16), weight, NT) for part in split3(rows))
    out_ref[...] = jnp.zeros_like(out_ref)
    at = 0
    for value in [times[0:1], plain[0:1]] + [ref[...] for ref in fulls]:
        out_ref[:, at : at + width] = value
        at += width
    heads = scorer_ref.shape[0]
    real = lane_ids(1) < HD
    pairs = []
    for pair in range(heads // 2):
        one, two = scorer_ref[2 * pair : 2 * pair + 1, :], scorer_ref[2 * pair + 1 : 2 * pair + 2, :]
        pairs.append(jnp.where(real, one, pltpu.roll(two, HD, 1)))
    halves = [bias_ref[...]] + pairs + [fc_ref[...]]
    total = sum(half.shape[1] for half in halves)
    for side in range(2):

        @pl.when(side_ref[2] == side)
        def _():
            start = at + side * total
            for half in halves:
                out_ref[:, start : start + half.shape[1]] = half
                start += half.shape[1]


def pack(places, weight, joined, bias, scorer, fulls, fc):
    inputs = (places, weight, joined, bias, scorer, *fulls, fc)
    heads = scorer.shape[0]
    total = (2 + len(fulls)) * weight.shape[0] + 2 * (
        bias.shape[1] + heads * HD + fc.shape[1]
    )
    return pl.pallas_call(
        pack_kernel,
        in_specs=[pl.BlockSpec(memory_space=pltpu.SMEM)] + [in_vmem()] * (len(inputs) - 1),
        out_specs=in_vmem(),
        out_shape=jax.ShapeDtypeStruct((1, total), F32),
        compiler_params=pltpu.CompilerParams(vmem_limit_bytes=16 * MIB),
        cost_estimate=SMALL,
        name="pack",
    )(*inputs)


SPAN = 256


def normalize(values):
    center = values - jnp.mean(values, axis=-1, keepdims=True)
    scale = lax.rsqrt(jnp.mean(center * center, axis=-1, keepdims=True) + 1e-05)
    return center * scale, scale


def norm_back(slope, hat, scale):
    means = jnp.mean(slope, axis=-1, keepdims=True)
    inner = jnp.mean(slope * hat, axis=-1, keepdims=True)
    return (slope - means - hat * inner) * scale


def row_spec(width, span=SPAN, skip=0):
    return pl.BlockSpec((span, width), lambda i, *_: (i + skip, 0))


def sum_rows(values):
    return jnp.sum(values, axis=0, keepdims=True)


def start_at_zero(*refs):
    @pl.when(pl.program_id(0) == 0)
    def _():
        for ref in refs:
            ref[...] = jnp.zeros_like(ref)


def rows_call(
    kernel, name, rows, inputs, in_specs, outs, flops, span=SPAN, earlier=(), limit=16
):
    aliases = {}
    body = kernel
    if earlier:
        first = len(inputs)
        aliases = {first + n: at for n, (at, _) in enumerate(earlier)}
        skip_from, skip_count = first, len(earlier)
        inputs = tuple(inputs) + tuple(array for _, array in earlier)
        in_specs = list(in_specs) + [pl.BlockSpec(memory_space=pl.ANY)] * len(earlier)

        def body(*refs):
            kernel(*refs[:skip_from], *refs[skip_from + skip_count :])

    return pl.pallas_call(
        body,
        grid=(rows // span,),
        in_specs=in_specs,
        out_specs=[
            pl.BlockSpec((1, width), lambda i, *_: (0, 0))
            if one
            else row_spec(width, span, start // span)
            for one, width, _, _, start in outs
        ],
        out_shape=[
            jax.ShapeDtypeStruct((1 if one else total, width), kind)
            for one, width, kind, total, _ in outs
        ],
        input_output_aliases=aliases,
        compiler_params=pltpu.CompilerParams(vmem_limit_bytes=limit * MIB),
        cost_estimate=SMALL,
        name=name,
    )(*inputs)


def norm_one_kernel(in_ref, gain_ref, shift_ref, out_ref):
    hat, _ = normalize(in_ref[...])
    gain = gain_ref[...].reshape(1, gain_ref.shape[0])
    shift = shift_ref[...].reshape(1, shift_ref.shape[0])
    out_ref[...] = (hat * gain + shift).astype(BF16)


def norm_one(layer_in, gain, shift):
    rows, width = layer_in.shape
    (out,) = rows_call(
        norm_one_kernel,
        "norm_one",
        rows,
        (layer_in, gain, shift),
        [row_spec(width), in_vmem(), in_vmem()],
        [(False, width, BF16, rows, 0)],
        rows * width * 8,
        limit=60,
    )
    return out


def narrow_kernel(first_ref, second_ref, out_first_ref, out_second_ref):
    out_first_ref[...] = first_ref[...].astype(BF16)
    out_second_ref[...] = second_ref[...].astype(BF16)


def narrow_halves(values):
    rows, width = values.shape
    half = rows // 2
    return rows_call(
        narrow_kernel,
        "narrow",
        half,
        (values, values),
        [row_spec(width), row_spec(width, skip=half // SPAN)],
        [(False, width, BF16, half, 0)] * 2,
        rows * width,
        limit=60,
    )


def mix_kernel(
    in_ref, own_ref, peer_ref, w_own_ref, w_peer_ref, bias_ref, gain_ref, shift_ref, mixed_ref, norm_ref
):
    part = dot(own_ref[...], w_own_ref[...]) + dot(peer_ref[...], w_peer_ref[...])
    mixed = in_ref[...] + part + bias_ref[...]
    mixed_ref[...] = mixed
    hat, _ = normalize(mixed)
    norm_ref[...] = (hat * gain_ref[...] + shift_ref[...]).astype(BF16)


def mix(layer_in, own, peer, w_own, w_peer, bias, gain, shift, start, earlier):
    total, width = layer_in.shape
    rows, depth = peer.shape
    skip = start // SPAN
    vector = pl.BlockSpec((1, width), lambda i: (0, 0))
    return rows_call(
        mix_kernel,
        "mix",
        rows,
        (layer_in, own, peer, w_own, w_peer)
        + tuple(v.reshape(1, width) for v in (bias, gain, shift)),
        [
            row_spec(width, skip=skip),
            row_spec(depth),
            row_spec(depth),
            whole_block(w_own),
            whole_block(w_peer),
        ]
        + [vector] * 3,
        [(False, width, F32, total, start), (False, width, BF16, rows, 0)],
        rows * width * depth * 4,
        earlier=earlier,
        limit=60,
    )


def feed_kernel(
    norm_ref, grad_ref, fc_ref, bias_ref, proj_ref, active_ref, slope_ref, back_ref, sum_ref
):
    start_at_zero(sum_ref)
    units = fc_ref.shape[1]
    step = 512
    total = None
    for at in range(0, units, step):
        cols = slice(at, at + step)
        hidden = dot(norm_ref[...], fc_ref[:, cols]) + bias_ref[:, cols]
        grad = dot(grad_ref[...], proj_ref[cols, :], NT)
        square = hidden * hidden
        bend = jnp.tanh(hidden * (0.7978845608 + 0.7978845608 * 0.044715 * square))
        half = 0.5 + 0.5 * bend
        active_ref[:, cols] = (hidden * half).astype(BF16)
        inner = 0.7978845608 + 3.0 * 0.7978845608 * 0.044715 * square
        slope = grad * (half + 0.5 * hidden * (1.0 - bend * bend) * inner)
        low = slope.astype(BF16)
        slope_ref[:, cols] = low
        sum_ref[:, cols] += sum_rows(slope)
        part = dot(low, fc_ref[:, cols], NT)
        total = part if total is None else total + part
    back_ref[...] = total.astype(back_ref.dtype)


def feed(norm_rows, grad_rows, fc, bias, proj, back_kind, start, total, earlier):
    rows, width = norm_rows.shape
    units = fc.shape[1]
    bias = bias.reshape(1, units)
    return rows_call(
        feed_kernel,
        "feed",
        rows,
        (norm_rows, grad_rows, fc, bias, proj),
        [
            row_spec(width),
            row_spec(width),
            whole_block(fc),
            whole_block(bias),
            whole_block(proj),
        ],
        [
            (False, units, BF16, total, start),
            (False, units, BF16, total, start),
            (False, width, back_kind, rows, 0),
            (True, units, F32, 1, 0),
        ],
        rows * width * units * 6,
        earlier=earlier,
    )


def mix_back_kernel(
    mixed_ref,
    own_ref,
    other_ref,
    grad_ref,
    gain_ref,
    w_own_ref,
    w_peer_ref,
    out_ref,
    low_ref,
    att_own_ref,
    att_peer_ref,
    gain_out_ref,
    shift_out_ref,
    mixed_out_ref,
    grad_out_ref,
):
    start_at_zero(gain_out_ref, shift_out_ref, mixed_out_ref, grad_out_ref)
    hat, scale = normalize(mixed_ref[...])
    slope = own_ref[...] + other_ref[...].astype(F32)
    gain_out_ref[...] += sum_rows(slope * hat)
    shift_out_ref[...] += sum_rows(slope)
    grad = grad_ref[...]
    grad_out_ref[...] += sum_rows(grad)
    out = grad + norm_back(slope * gain_ref[...], hat, scale)
    mixed_out_ref[...] += sum_rows(out)
    out_ref[...] = out
    low = out.astype(BF16)
    low_ref[...] = low
    att_own_ref[...] = dot(low, w_own_ref[...], NT).astype(BF16)
    att_peer_ref[...] = dot(low, w_peer_ref[...], NT).astype(BF16)


def mix_back(mixed, own, other, grad, gain, w_own, w_peer, start, earlier):
    total, width = mixed.shape
    rows = other.shape[0]
    depth = w_own.shape[0]
    gain = gain.reshape(1, width)
    wide = row_spec(width)
    later = row_spec(width, skip=start // SPAN)
    return rows_call(
        mix_back_kernel,
        "mix_back",
        rows,
        (mixed, own, other, grad, gain, w_own, w_peer),
        [later, wide, wide, later, whole_block(gain), whole_block(w_own), whole_block(w_peer)],
        [
            (False, width, F32, total, start),
            (False, width, BF16, total, start),
            (False, depth, BF16, rows, 0),
            (False, depth, BF16, rows, 0),
            (True, width, F32, 1, 0),
            (True, width, F32, 1, 0),
            (True, width, F32, 1, 0),
            (True, width, F32, 1, 0),
        ],
        rows * width * depth * 4,
        earlier=earlier,
        limit=60,
    )


def norm_one_back_kernel(in_ref, own_ref, grad_ref, gain_ref, *refs):
    hat, scale = normalize(in_ref[...])
    other = choose(refs[:-1], pl.program_id(0)).astype(F32)
    slope = (own_ref[...] + other) * gain_ref[...]
    refs[-1][...] = grad_ref[...] + norm_back(slope, hat, scale)


def norm_one_back(layer_in, own, grad, gain, others):
    rows, width = layer_in.shape
    span = others[0].shape[0]
    gain = gain.reshape(1, width)
    return pl.pallas_call(
        norm_one_back_kernel,
        grid=(rows // span,),
        in_specs=[row_spec(width, span)] * 3
        + [whole_block(gain)]
        + [chunk_spec(other) for other in others],
        out_specs=row_spec(width, span),
        out_shape=jax.ShapeDtypeStruct((rows, width), F32),
        compiler_params=pltpu.CompilerParams(vmem_limit_bytes=16 * MIB),
        cost_estimate=SMALL,
        name="norm_one_back",
    )(layer_in, own, grad, gain, *others)


def flip_bit(values, bit):
    total = lax.axis_size("dp")
    return lax.ppermute(values, "dp", [(n, n ^ (1 << bit)) for n in range(total)])


def flip_core(values):
    return flip_bit(values, 0)


def flip_tensor(values):
    return lax.ppermute(values, "tensor", [(0, 1), (1, 0)])


def small_call(kernel, name, bits, inputs, outs):
    return pl.pallas_call(
        kernel,
        in_specs=[pl.BlockSpec(memory_space=pltpu.SMEM)] + [in_vmem()] * len(inputs),
        out_specs=[in_vmem()] * len(outs),
        out_shape=[jax.ShapeDtypeStruct(shape, kind) for shape, kind in outs],
        compiler_params=pltpu.CompilerParams(vmem_limit_bytes=16 * MIB),
        cost_estimate=SMALL,
        name=name,
    )(bits, *inputs)


def added(one_ref, two_ref, at, count):
    here = pl.ds(at, count)
    return (one_ref[here].astype(F32) + two_ref[here].astype(F32)).astype(BF16)


def stack_kernel(bits_ref, joined_ref, keep_ref, *refs):
    other_refs, (mine_ref, send_ref) = refs[:-2], refs[-2:]
    width = mine_ref.shape[1]
    rest = joined_ref.shape[1] - width
    step = other_refs[0].shape[0]

    def place(first, second):
        first[...] = joined_ref[:, 0:width]
        second[:, 0:rest] = joined_ref[:, width:]
        for n, other_ref in enumerate(other_refs):
            here = slice(n * step, (n + 1) * step)
            out = keep_ref[here, :].astype(F32) + other_ref[...].astype(F32)
            second[here, rest:] = out.astype(BF16)

    @pl.when(bits_ref[0] == 0)
    def _():
        place(mine_ref, send_ref)

    @pl.when(bits_ref[0] == 1)
    def _():
        place(send_ref, mine_ref)


def split_kernel(places, bits_ref, mine_ref, got_ref, *outs):
    step = mine_ref.shape[0] // (2 * len(places))
    for n, bit in enumerate(places):
        mine = bits_ref[bit]
        base = 2 * n * step
        outs[2 * n][...] = added(mine_ref, got_ref, base + mine * step, step)
        outs[2 * n + 1][...] = added(mine_ref, got_ref, base + (1 - mine) * step, step)


def split_sum(places, bits, mine, got):
    pieces, rows, cols = mine.shape
    shape = ((pieces // (2 * len(places)), rows, cols), BF16)
    return small_call(
        functools.partial(split_kernel, places), "split_sum", bits, (mine, got), [shape] * (2 * len(places))
    )


def add_kernel(bits_ref, mine_ref, got_ref, out_ref):
    out_ref[...] = added(mine_ref, got_ref, 0, mine_ref.shape[0])


def merge_kernel(places, bits_ref, *refs):
    out_ref = refs[-1]
    step = refs[0].shape[0]
    for n, bit in enumerate(places):
        mine = bits_ref[bit]
        base = 2 * n * step
        out_ref[pl.ds(base + mine * step, step)] = refs[2 * n][...]
        out_ref[pl.ds(base + (1 - mine) * step, step)] = refs[2 * n + 1][...]


def merge(places, bits, *inputs):
    pieces, rows, cols = inputs[0].shape
    shape = ((2 * len(places) * pieces, rows, cols), BF16)
    (out,) = small_call(
        functools.partial(merge_kernel, places), "merge", bits, inputs, [shape]
    )
    return out


def unstack_kernel(bits_ref, mine_ref, got_ref, joined_ref, out_ref):
    width = mine_ref.shape[1]
    rest = joined_ref.shape[1] - width

    def place(first, second):
        joined_ref[:, 0:width] = first[...].astype(F32)
        joined_ref[:, width:] = second[:, 0:rest].astype(F32)
        out_ref[...] = second[:, rest:].astype(F32).T

    @pl.when(bits_ref[0] == 0)
    def _():
        place(mine_ref, got_ref)

    @pl.when(bits_ref[0] == 1)
    def _():
        place(got_ref, mine_ref)


def ladder(joined, out_keep, out_others, small, sends, early, late):
    total = lax.axis_size("dp")
    count = total.bit_length() - 1
    bits = (lax.axis_index("dp") >> jnp.arange(count, dtype=jnp.int32)) & 1
    rows, cols = joined.shape
    width = (cols + out_keep.shape[1]) // 2
    rest = list(range(1, count))
    orders = (rest, rest[1:] + rest[:1])
    state = {"step": 0, "small": small, "sends": list(sends), "sent": [], "made": {}}
    flips = [functools.partial(flip_bit, bit=bit) for bit in range(count)] + [flip_tensor]
    first = 2

    def together(values):
        at = state["step"]
        state["step"] += 1
        beside = []
        sums, chunk = first <= at < first + len(flips), first <= at < first + len(sends)
        if sums:
            beside.append(state["small"] + flips[at - first](state["small"]))
        if chunk:
            beside.append(flip_tensor(state["sends"][at - first]))
        if at in early:
            beside.append(early[at](state["made"]))
        values, beside = lax.optimization_barrier((values, beside))
        if sums:
            state["small"] = beside.pop(0)
        if chunk:
            state["sent"].append(beside.pop(0))
        if at in early:
            state["made"][at] = beside.pop(0)
        return values

    mine, send = small_call(
        stack_kernel, "stack", bits, (joined, out_keep, *out_others), [((rows, width), BF16)] * 2
    )
    cut = (total, rows // total, width)
    mine, got = together((mine.reshape(cut), flip_core(send.reshape(cut))))
    level = split_sum((orders[0][0], orders[1][0]), bits, mine, got)
    parts = [(level[0], level[1]), (level[2], level[3])]
    for n in range(len(rest)):
        both = together([(parts[p][0], flip_bit(parts[p][1], orders[p][n])) for p in range(2)])
        for p, (mine, got) in enumerate(both):
            if n + 1 < len(rest):
                parts[p] = split_sum((orders[p][n + 1],), bits, mine, got)
            else:
                (parts[p],) = small_call(add_kernel, "add_last", bits, (mine, got), [(mine.shape, BF16)])
    for n in reversed(range(len(rest))):
        both = together([(parts[p], flip_bit(parts[p], orders[p][n])) for p in range(2)])
        if n > 0:
            parts = [merge((orders[p][n],), bits, *both[p]) for p in range(2)]
    mine = merge((orders[0][0], orders[1][0]), bits, *both[0], *both[1])
    last = late(state["sent"])
    (mine, got), last = lax.optimization_barrier(((mine, flip_core(mine)), last))
    outs = [((rows, cols), F32), ((out_keep.shape[1], rows), F32)]
    grads = small_call(
        unstack_kernel, "unstack", bits, (mine.reshape(rows, width), got.reshape(rows, width)), outs
    )
    return grads, state["small"], state["made"], last


def shards(
    layer_in,
    qkv_weight,
    qkv_bias,
    key_scorer,
    out_weight,
    out_bias,
    fc_weight,
    fc_bias,
    proj_weight,
    proj_bias,
    norm1_gain,
    norm1_shift,
    norm2_gain,
    norm2_shift,
    key_index,
    key_count,
    out_grad,
):
    side = lax.axis_index("tensor")
    own_rows, width = layer_in.shape
    seq = key_index.shape[0]
    half = own_rows // 2
    blocks = own_rows // QB
    places = jnp.stack([side * blocks, (1 - side) * blocks, side]).astype(jnp.int32)

    starts = (0, half)
    norm_own = norm_one(layer_in, norm1_gain, norm1_shift)
    norm_peer = flip_tensor(norm_own)
    bits = allowed_bits(key_index, key_count)
    grad_lows = narrow_halves(out_grad)
    scorer = scorer_rows(key_scorer)
    bits, out_later = lax.optimization_barrier((bits, out_weight))
    out_peer = flip_tensor(out_later)

    own = qkv_heads(norm_own, qkv_weight, qkv_bias, scorer)
    own, *grad_laters = lax.optimization_barrier((own, *grad_lows))
    grad_peers = [flip_tensor(low) for low in grad_laters]
    qa_own, ka_own, va_own, vt_own, kt_own = own
    state = attend_call(
        attend_start_kernel, "attend_start", places, qa_own, (ka_own, vt_own, bits), blocks, 0, (), True
    )
    state, norm_peer = lax.optimization_barrier((state, norm_peer))
    peer = qkv_heads(norm_peer, qkv_weight, qkv_bias, scorer)
    qa_peer, ka_peer, va_peer, vt_peer, kt_peer = peer
    att_owns, logs_owns, att_sends, logs_sends, att_peers = [], [], [], [], []
    for n in range(blocks):
        att_send, logs_send = attend_call(
            functools.partial(attend_other_kernel, n),
            "attend_other",
            places,
            qa_peer,
            (ka_peer, vt_peer, ka_own, vt_own, bits),
            1,
            n,
        )
        att_own, logs_own = attend_call(
            functools.partial(attend_finish_kernel, n),
            "attend_finish",
            places,
            qa_own,
            (ka_peer, vt_peer, bits),
            1,
            n,
            state,
        )
        att_send, att_own, qa_peer, qa_own = lax.optimization_barrier(
            (att_send, att_own, qa_peer, qa_own)
        )
        if n == 0:
            att_send, *grad_peers = lax.optimization_barrier((att_send, *grad_peers))
        att_owns.append(att_own)
        logs_owns.append(logs_own)
        att_sends.append(att_send)
        logs_sends.append(logs_send)
        att_peers.append(flip_tensor(att_send))

    mixed = None
    normed, normed_peers = [], []
    grad_lows = list(grad_lows)
    for n, at in enumerate(starts):
        mixed, low = mix(
            layer_in,
            att_owns[n],
            att_peers[n],
            out_weight,
            out_peer,
            out_bias,
            norm2_gain,
            norm2_shift,
            at,
            () if mixed is None else ((0, mixed),),
        )
        normed.append(low)
        normed_peers.append(flip_tensor(low))
    active = slopes = None
    backs, back_others, fc_sums = [], [], []
    for n, rows in enumerate(normed + normed_peers):
        active, slopes, back, fc_sum = feed(
            rows,
            (grad_lows + grad_peers)[n],
            fc_weight,
            fc_bias,
            proj_weight,
            F32 if n < 2 else BF16,
            n * half,
            seq,
            () if active is None else ((0, active), (1, slopes)),
        )
        fc_sums.append(fc_sum)
        if n < 2:
            backs.append(back)
        else:
            back_others.append(flip_tensor(back))
    grad_fc_bias = sum(fc_sums[1:], fc_sums[0])
    grad_fc_weight = turned_product(normed + normed_peers, [slopes], "fc_slope")
    grad_proj_weight = turned_product([active], grad_lows + grad_peers, "proj_slope")
    proj_sends = product(active, proj_weight, NN, own_rows, own_rows, BF16, "proj_send", 4)
    mixed, grad_fc_weight, grad_proj_weight = lax.optimization_barrier(
        (mixed, grad_fc_weight, grad_proj_weight)
    )
    grad_mixed = grad_mixed_low = None
    grad_att_owns, grad_att_peers, row_sums = [], [], []
    for n, at in enumerate(starts):
        grad_mixed, grad_mixed_low, grad_att_own, grad_att_send, *some = mix_back(
            mixed,
            backs[n],
            back_others[n],
            out_grad,
            norm2_gain,
            out_weight,
            out_peer,
            at,
            ()
            if grad_mixed is None
            else ((0, grad_mixed), (1, grad_mixed_low)),
        )
        row_sums.append(some)
        grad_att_owns.append(grad_att_own)
        grad_att_peers.append(flip_tensor(grad_att_send))
    grad_norm2_gain, grad_norm2_shift, grad_out_bias, grad_proj_bias = (
        one + two for one, two in zip(*row_sums)
    )

    out_sends = turned_product([grad_mixed_low], att_peers, "out_slope", width // 2, 2)
    out_keep = turned_product([grad_mixed_low], att_owns, "out_slope")
    grad_fc_weight, grad_proj_weight = lax.psum((grad_fc_weight, grad_proj_weight), "dp")
    own_keys, peer_keys = (ka_own, kt_own, va_own), (ka_peer, kt_peer, va_peer)
    out_others = [flip_tensor(rows) for rows in out_sends]
    qa_own, proj_sends, out_sends, out_keep = lax.optimization_barrier(
        (qa_own, proj_sends, out_sends, out_keep)
    )
    proj_others = [flip_tensor(rows) for rows in proj_sends]
    dq_own, *key_sums = attend_back(
        True, places, qa_own, (own_keys, peer_keys), grad_att_owns, att_owns, logs_owns, bits
    )
    swapped = (key_sums[1], key_sums[0], key_sums[3], key_sums[2])
    *_, joined, grad_qkv_bias, grad_key_scorer = attend_back(
        False,
        places,
        qa_peer,
        (peer_keys, own_keys),
        grad_att_peers,
        att_sends,
        logs_sends,
        bits,
        swapped + (dq_own, scorer),
    )
    joined, out_others, proj_others = lax.optimization_barrier((joined, out_others, proj_others))
    grad_qkv_weight = turned_product([norm_own, norm_peer], [joined], "qkv_slope")
    one_sends = product(joined, qkv_weight, NT, own_rows, own_rows, BF16, "one_send", 4)
    (one_own,) = product(joined, qkv_weight, NT, 0, own_rows, F32, "one_own")
    layer_half = layer_end(mixed, active, proj_weight, proj_bias, proj_others[:2], 0, ())
    packed = pack(
        places,
        qkv_weight,
        grad_qkv_weight,
        grad_qkv_bias,
        grad_key_scorer,
        (grad_norm2_gain, grad_norm2_shift, grad_out_bias, grad_proj_bias),
        grad_fc_bias,
    )

    def end_of_norm_one(sent):
        return norm_one_back(layer_in, one_own, grad_mixed, norm1_gain, sent)

    grads, packed, made, input_grad = ladder(
        grad_qkv_weight,
        out_keep,
        out_others,
        packed,
        one_sends,
        {
            0: lambda made: (grad_fc_weight, grad_proj_weight),
            2: lambda made: one_own,
            3: lambda made: layer_half,
            4: lambda made: layer_end(
                mixed, active, proj_weight, proj_bias, proj_others[2:], half, ((0, made[3]),)
            ),
            5: lambda made: made[0][0].astype(F32),
            6: lambda made: made[0][1].astype(F32),
        },
        end_of_norm_one,
    )
    grad_qkv_weight, grad_out_weight = grads
    layer_out, grad_fc_weight, grad_proj_weight = made[4], made[5], made[6]
    joined_cols = qkv_weight.shape[1]

    full = [packed[0, n * width : (n + 1) * width] for n in range(6)]
    grad_norm1_gain = (full[0] - norm1_shift * full[1]) / norm1_gain
    sizes = (joined_cols, key_scorer.shape[0], fc_bias.shape[0])
    halves = lax.dynamic_slice_in_dim(packed[0], 6 * width + side * sum(sizes), sum(sizes), 0)
    ends = (sizes[0], sizes[0] + sizes[1])
    return (
        layer_out,
        input_grad,
        grad_qkv_weight,
        halves[: ends[0]],
        halves[ends[0] : ends[1]],
        grad_out_weight,
        full[4],
        grad_fc_weight,
        halves[ends[1] :],
        grad_proj_weight,
        full[5],
        grad_norm1_gain,
        full[1],
        full[2],
        full[3],
    )


def solution(mesh):
    rows = P(("dp", "tensor"), None)
    in_specs = (
        rows,
        P(None, "tensor"),
        P("tensor"),
        P("tensor"),
        P("tensor", None),
        P(),
        P(None, "tensor"),
        P("tensor"),
        P("tensor", None),
        P(),
        P(),
        P(),
        P(),
        P(),
        P("dp", None),
        P("dp"),
        rows,
    )
    out_specs = (
        rows,
        rows,
        P(None, "tensor"),
        P("tensor"),
        P("tensor"),
        P("tensor", None),
        P(),
        P(None, "tensor"),
        P("tensor"),
        P("tensor", None),
        P(),
        P(),
        P(),
        P(),
        P(),
    )
    return jax.shard_map(shards, mesh=mesh, in_specs=in_specs, out_specs=out_specs, check_vma=False)
```

```python
import functools
import math

import jax
import jax.numpy as jnp
from jax import lax
from jax.experimental import pallas as pl
from jax.experimental.pallas import tpu as pltpu
from jax.sharding import PartitionSpec as P

HD = 64
LANES = 128
WIN = 64
LOG2E = math.log2(math.e)
LN2 = math.log(2.0)
NEG = -1e30
QB = 512
KB = 512
ROWS = 512
VT = 80
NT = (((1,), (1,)), ((), ()))
NN = (((1,), (0,)), ((), ()))
TN = (((0,), (0,)), ((), ()))
F32 = jnp.float32
BF16 = jnp.bfloat16
MIB = 1024 * 1024
SMALL = pl.CostEstimate(flops=1000, bytes_accessed=1000, transcendentals=0)


def dot(a, b, dims=NN):
    return lax.dot_general(a, b, dims, preferred_element_type=F32)


def split3(x):
    hi = x.astype(BF16).astype(F32)
    rest = x - hi
    mid = rest.astype(BF16).astype(F32)
    low = (rest - mid).astype(BF16).astype(F32)
    return hi, mid, low


def lane_ids(rows):
    return lax.broadcasted_iota(jnp.int32, (rows, LANES), 1)


def put3(base, lanes, first, parts):
    out = base
    for n, part in enumerate(parts):
        out = jnp.where(lanes == first + n, part, out)
    return out


def whole_block(array):
    return pl.BlockSpec(memory_space=pltpu.VMEM)


def scorer_rows(key_scorer):
    return jnp.pad(key_scorer.reshape(-1, HD), ((0, 0), (0, LANES - HD)))


def bits_kernel(low_ref, flag_ref, bits_ref):
    width = bits_ref.shape[1]
    first = pl.program_id(0) * width
    lane = lax.broadcasted_iota(jnp.int32, (LANES, width), 0)
    pos = lax.broadcasted_iota(jnp.int32, (LANES, width), 1) + first
    back = (pos - lane) & (LANES - 1)
    at = pos - back
    bits = jnp.where((back < WIN) & (at >= 0), 1 << (jnp.maximum(at, 0) >> 7), 0)
    for slot in range(low_ref.shape[0]):
        hit = low_ref[slot : slot + 1, :] == lane
        bits = bits | jnp.where(hit, flag_ref[slot : slot + 1, :], 0)
    bits_ref[...] = bits


def allowed_bits(key_index, key_count):
    seq = key_index.shape[0]
    index = key_index.T
    slots = index.shape[0]
    slot = lax.broadcasted_iota(jnp.int32, index.shape, 0)
    used = (slot < key_count[None, :]) & (index >= 0)
    low = index & (LANES - 1)
    flag = jnp.where(used, 1 << (jnp.maximum(index, 0) >> 7), 0)
    width = 256
    spec = pl.BlockSpec((slots, width), lambda i: (0, i))
    return pl.pallas_call(
        bits_kernel,
        grid=(seq // width,),
        in_specs=[spec, spec],
        out_specs=pl.BlockSpec((LANES, width), lambda i: (0, i)),
        out_shape=jax.ShapeDtypeStruct((LANES, seq), jnp.int32),
        cost_estimate=SMALL,
        name="allowed_bits",
    )(low, flag)


def fill_bias(bias_ref, bits_ref, q0, k0):
    depth, width = bias_ref.shape
    bits = bits_ref[:, pl.ds(q0, width)]
    for part in range(depth // LANES):
        shift = k0 // LANES + part
        seen = ((bits >> shift) & 1) == 1
        bias_ref[part * LANES : (part + 1) * LANES, :] = jnp.where(seen, 0.0, NEG)


def qkv_kernel(weight_ref, bias_ref, scorer_ref, *refs):
    norm_refs, (qa_ref, ka_ref, va_ref, vt_ref, kt_ref) = refs[:-5], refs[-5:]
    norm = choose(norm_refs, pl.program_id(0))
    rows = norm.shape[0]
    heads = qa_ref.shape[0]
    lanes = lane_ids(rows)
    real = lanes < HD
    ones = jnp.where((lanes >= HD) & (lanes < HD + 3), 1.0, 0.0)
    for pair in range(heads // 2):
        cols = slice(pair * 6 * HD, (pair + 1) * 6 * HD)
        raw = dot(norm, weight_ref[:, cols]) + bias_ref[:, cols]
        raw = raw.astype(BF16).astype(F32)
        blocks = [raw[:, n * LANES : (n + 1) * LANES] for n in range(3)]
        turned = [pltpu.roll(block, HD, 1) for block in blocks]
        groups = (
            (blocks[0], turned[0], blocks[1]),
            (turned[1], blocks[2], turned[2]),
        )
        for side, (query, key, value) in enumerate(groups):
            head = pair * 2 + side
            raw_gate = jnp.sum(key * scorer_ref[head : head + 1, :], axis=1, keepdims=True)
            gate = jnp.minimum(raw_gate, 0.0) - jnp.log1p(jnp.exp(-jnp.abs(raw_gate)))
            key_plain = jnp.where(real, key, 0.0)
            value_ones = jnp.where(real, value, ones)
            qa_ref[head] = jnp.where(real, query * 0.125, ones).astype(BF16)
            ka_ref[head] = put3(key_plain, lanes, HD, split3(gate)).astype(BF16)
            va_ref[head] = value_ones.astype(BF16)
            vt_ref[head] = value_ones.T[:VT, :].astype(BF16)
            kt_ref[head] = key_plain.T[:HD, :].astype(BF16)


def qkv_heads(norm_pieces, weight, bias, scorer):
    rows = ROWS * len(norm_pieces)
    heads = scorer.shape[0]
    cols = weight.shape[1]
    row_shape = jax.ShapeDtypeStruct((heads, rows, LANES), BF16)
    row_block = pl.BlockSpec((heads, ROWS, LANES), lambda i: (0, i, 0))
    bias = bias.reshape(1, cols)
    return pl.pallas_call(
        qkv_kernel,
        grid=(rows // ROWS,),
        in_specs=[whole_block(weight), whole_block(bias), whole_block(scorer)]
        + [chunk_spec(piece) for piece in norm_pieces],
        out_specs=[
            row_block,
            row_block,
            row_block,
            pl.BlockSpec((heads, VT, ROWS), lambda i: (0, 0, i)),
            pl.BlockSpec((heads, HD, ROWS), lambda i: (0, 0, i)),
        ],
        out_shape=[
            row_shape,
            row_shape,
            row_shape,
            jax.ShapeDtypeStruct((heads, VT, rows), BF16),
            jax.ShapeDtypeStruct((heads, HD, rows), BF16),
        ],
        compiler_params=pltpu.CompilerParams(vmem_limit_bytes=14 * MIB),
        cost_estimate=SMALL,
        name="qkv_heads",
    )(weight, bias, scorer, *norm_pieces)


def attend_block(
    place, q_block, k0, qa_ref, ka_ref, vt_ref, bits_ref, bias_ref, total_ref, peak_ref, corner
):
    heads = qa_ref.shape[0]
    depth, first = corner
    queries = slice(first, QB)
    bias = bias_ref.at[0:depth, queries]
    keys = pl.ds(k0, depth)
    fill_bias(bias, bits_ref, q_block * QB + first, place * KB + k0)

    def scores_of(head):
        return dot(ka_ref[head, keys, :], qa_ref[head, queries, :], NT)

    ahead = scores_of(0)
    for head in range(heads):
        scores = ahead
        if head + 1 < heads:
            ahead = scores_of(head + 1)
        scores = scores * LOG2E + bias[...]
        old = peak_ref[head, :, queries]
        new = jnp.maximum(old, jnp.max(scores, axis=0, keepdims=True))
        weights = jnp.exp2(scores - new[0:1])
        shrink = jnp.exp2(old - new)
        peak_ref[head, :, queries] = new
        part = dot(vt_ref[head, :, keys], weights.astype(BF16))
        total_ref[head, :, queries] = total_ref[head, :, queries] * shrink[0:1] + part


def attend_blocks(count, place, q_block, *refs):
    def step(j, carry):
        k0 = pl.multiple_of(j * KB, KB)
        attend_block(place, q_block, k0, *refs, (KB, 0))
        return carry

    lax.fori_loop(0, count, step, 0)


def attend_diagonal(n, place, q_block, *refs):
    half = KB // 2
    k0 = pl.multiple_of(n * KB, KB)
    attend_block(place, q_block, k0, *refs, (half, 0))
    attend_block(place, q_block, pl.multiple_of(k0 + half, half), *refs, (half, half))


def attend_open(total_ref, peak_ref):
    total_ref[...] = jnp.zeros_like(total_ref)
    peak_ref[...] = jnp.full_like(peak_ref, NEG)


def attend_end(total_ref, peak_ref, out_ref, log_ref):
    heads = total_ref.shape[0]
    for pair in range(heads // 2):
        sides = []
        for head in (2 * pair, 2 * pair + 1):
            mass = total_ref[head, HD : HD + 1, :]
            sides.append(total_ref[head, 0:HD, :] / mass)
            log_ref[head] = peak_ref[head] + jnp.log(mass) * LOG2E
        both = jnp.concatenate(sides, axis=0).T
        out_ref[:, pair * LANES : (pair + 1) * LANES] = both.astype(BF16)


def attend_start_kernel(
    places_ref, qa_ref, ka_ref, vt_ref, bits_ref, total_ref, peak_ref, bias_ref
):
    own = places_ref[0]
    n = pl.program_id(0)
    refs = (qa_ref, ka_ref, vt_ref, bits_ref, bias_ref, total_ref, peak_ref)
    attend_open(total_ref, peak_ref)
    attend_blocks(n, own, own + n, *refs)
    attend_diagonal(n, own, own + n, *refs)


def attend_finish_kernel(
    n,
    places_ref,
    qa_ref,
    ka_ref,
    vt_ref,
    bits_ref,
    total_in_ref,
    peak_in_ref,
    out_ref,
    log_ref,
    bias_ref,
    total_ref,
    peak_ref,
):
    own, peer, later = places_ref[0], places_ref[1], places_ref[2]
    refs = (qa_ref, ka_ref, vt_ref, bits_ref, bias_ref, total_ref, peak_ref)
    total_ref[...] = total_in_ref[...]
    peak_ref[...] = peak_in_ref[...]
    attend_blocks(later * (ka_ref.shape[1] // KB), peer, own + n, *refs)
    attend_end(total_ref, peak_ref, out_ref, log_ref)


def attend_other_kernel(
    n,
    places_ref,
    qa_ref,
    ka_ref,
    vt_ref,
    ka_own_ref,
    vt_own_ref,
    bits_ref,
    out_ref,
    log_ref,
    bias_ref,
    total_ref,
    peak_ref,
):
    own, peer, later = places_ref[0], places_ref[1], places_ref[2]
    block = peer + n
    tail = (bits_ref, bias_ref, total_ref, peak_ref)
    attend_open(total_ref, peak_ref)
    for at in range(n):
        attend_block(peer, block, at * KB, qa_ref, ka_ref, vt_ref, *tail, (KB, 0))
    attend_diagonal(n, peer, block, qa_ref, ka_ref, vt_ref, *tail)
    earlier = (1 - later) * (ka_own_ref.shape[1] // KB)
    attend_blocks(earlier, own, block, qa_ref, ka_own_ref, vt_own_ref, *tail)
    attend_end(total_ref, peak_ref, out_ref, log_ref)


def attend_call(kernel, name, places, qa, others, count, first, state=(), keep=False):
    heads = qa.shape[0]
    total_spec = pl.BlockSpec((heads, VT, QB), lambda i, _: (0, 0, first + i))
    peak_spec = pl.BlockSpec((heads, 8, QB), lambda i, _: (0, 0, first + i))
    log_spec = pl.BlockSpec((heads, 8, QB), lambda i, _: (0, 0, i))
    total_shape = jax.ShapeDtypeStruct((heads, VT, count * QB), F32)
    peak_shape = jax.ShapeDtypeStruct((heads, 8, count * QB), F32)
    scratch = [
        pltpu.VMEM((KB, QB), F32),
        pltpu.VMEM((heads, VT, QB), F32),
        pltpu.VMEM((heads, 8, QB), F32),
    ]
    if keep:
        out_specs, out_shape = [total_spec, peak_spec], [total_shape, peak_shape]
        scratch = scratch[:1]
    else:
        out_specs = [pl.BlockSpec((QB, heads * HD), lambda i, _: (i, 0)), log_spec]
        out_shape = [jax.ShapeDtypeStruct((count * QB, heads * HD), BF16), peak_shape]
    return pl.pallas_call(
        kernel,
        grid_spec=pltpu.PrefetchScalarGridSpec(
            num_scalar_prefetch=1,
            grid=(count,),
            in_specs=[pl.BlockSpec((heads, QB, LANES), lambda i, _: (0, first + i, 0))]
            + [whole_block(array) for array in others]
            + ([total_spec, peak_spec] if state else []),
            out_specs=out_specs,
            scratch_shapes=scratch,
        ),
        out_shape=out_shape,
        compiler_params=pltpu.CompilerParams(vmem_limit_bytes=16 * MIB),
        cost_estimate=SMALL,
        name=name,
    )(places, qa, *others, *state)


def in_vmem():
    return pl.BlockSpec(memory_space=pltpu.VMEM)


def attend_back_kernel(
    own_queries,
    places_ref,
    qa_ref,
    ka_refs,
    kt_refs,
    va_refs,
    grad_refs,
    att_refs,
    log_refs,
    bits_ref,
    dq_ref,
    dk_refs,
    dv_refs,
    bias_ref,
    ga_ref,
):
    heads, rows, _ = qa_ref.shape
    blocks = rows // QB
    lanes = lane_ids(ROWS)
    dq_ref[...] = jnp.zeros_like(dq_ref)
    if own_queries:
        for ref in tuple(dk_refs) + tuple(dv_refs):
            ref[...] = jnp.zeros_like(ref)

    for n in range(len(att_refs)):
        rows_n = slice(n * ROWS, (n + 1) * ROWS)
        grad_rows = grad_refs[n] if len(grad_refs) > 1 else grad_refs[0].at[rows_n, :]
        for pair in range(heads // 2):
            cols = slice(pair * LANES, (pair + 1) * LANES)
            grad = grad_rows[:, cols].astype(F32)
            prod = grad * att_refs[n][:, cols].astype(F32)
            turned = pltpu.roll(grad, HD, 1)
            for side, values in enumerate((grad, turned)):
                mine = (lanes < HD) if side == 0 else (lanes >= HD)
                inner = jnp.sum(jnp.where(mine, prod, 0.0), axis=1, keepdims=True)
                plain = jnp.where(lanes < HD, values, 0.0)
                filled = put3(plain, lanes, HD, split3(-inner))
                ga_ref[pair * 2 + side, rows_n, :] = filled.astype(BF16)

    q_place, k_places = places_ref[0], (places_ref[0], places_ref[1])
    later = places_ref[2]
    if not own_queries:
        q_place, k_places = k_places[1], (k_places[1], k_places[0])
        later = 1 - later

    def tile(piece, j, n, i, corner):
        depth, first = corner
        width = QB - first
        k1 = pl.multiple_of(j * KB + first, KB // 2)
        q1 = pl.multiple_of(i * QB + first, QB // 2)
        keys = pl.ds(k1, depth)
        queries = pl.ds(q1, width)
        bias = bias_ref.at[0:depth, 0:width]
        fill_bias(bias, bits_ref, q_place * QB + q1, k_places[piece] * KB + k1)
        ka_ref, kt_ref, va_ref = ka_refs[piece], kt_refs[piece], va_refs[piece]
        dk_ref, dv_ref = dk_refs[piece], dv_refs[piece]

        def first_of(head):
            qa = qa_ref[head, queries, :]
            ga = ga_ref[head, queries, :]
            return (
                qa,
                ga,
                dot(ka_ref[head, keys, :], qa, NT),
                dot(va_ref[head, keys, :], ga, NT),
            )

        ahead = first_of(0)
        for head in range(heads):
            qa, ga, scores, inner = ahead
            if head + 1 < heads:
                ahead = first_of(head + 1)
            scores = scores * LOG2E + bias[...]
            if isinstance(n, int):
                logs = log_refs[n][head, 0:1, first:QB]
            else:
                logs = jnp.where(n == 0, log_refs[0][head, 0:1, :], log_refs[1][head, 0:1, :])
            probs = jnp.exp2(scores - logs)
            slopes = (probs * inner).astype(BF16)
            dv_ref[head, keys, :] += dot(probs.astype(BF16), ga)
            dk_ref[head, keys, :] += dot(slopes, qa)
            dq_ref[head, :, queries] += dot(kt_ref[head, :, keys], slopes)

    half = KB // 2
    for n in range(blocks):
        tile(0, n, n, n, (half, 0))
        tile(0, n, n, n, (half, half))
        for j in range(n):
            tile(0, j, n, n, (KB, 0))

    def step(at, carry):
        i = at & (blocks - 1)
        tile(1, at // blocks, i, i, (KB, 0))
        return carry

    lax.fori_loop(0, later * (blocks * blocks), step, 0)


def join_piece(first, scorer_ref, dq_ref, dk_ref, dv_ref, ka_ref, joined_ref, bias_out_ref, scorer_out_ref):
    heads, rows, _ = dk_ref.shape
    span = 256
    lanes = lane_ids(span)
    real = lanes < HD

    def step(at, carry):
        here = pl.ds(pl.multiple_of(at * span, span), span)
        there = pl.ds(pl.multiple_of(at * span + first, span), span)
        for pair in range(heads // 2):
            dq = dq_ref[2 * pair : 2 * pair + 2, :, here].reshape(LANES, span).T * 0.125
            dks, dvs = [], []
            for head in (2 * pair, 2 * pair + 1):
                scorer = scorer_ref[head : head + 1, :]
                key = ka_ref[head, here, :].astype(F32)
                dk = dk_ref[head, here, :]
                raw_gate = jnp.sum(key * scorer, axis=1, keepdims=True)
                slope = dk[:, HD : HD + 1] / (1.0 + jnp.exp(raw_gate))
                scorer_out_ref[head : head + 1, :] += sum_rows(slope * key)
                dks.append(dk + slope * scorer)
                dvs.append(dv_ref[head, here, :])
            blocks = (
                jnp.where(real, dq, pltpu.roll(dks[0], HD, 1)),
                jnp.where(real, dvs[0], dq),
                jnp.where(real, dks[1], pltpu.roll(dvs[1], HD, 1)),
            )
            for n, block in enumerate(blocks):
                cols = slice((pair * 3 + n) * LANES, (pair * 3 + n + 1) * LANES)
                bias_out_ref[:, cols] += sum_rows(block)
                joined_ref[there, cols] = block.astype(BF16)
        return carry

    lax.fori_loop(0, rows // span, step, 0)


def attend_back(own_queries, places, qa, keys, grads, atts, logs, bits, sums=None):
    heads, rows, _ = qa.shape
    count = len(atts)
    inputs = [places, qa]
    for kind in range(3):
        inputs += [keys[0][kind], keys[1][kind]]
    inputs += list(grads) + list(atts) + list(logs) + [bits]
    given = len(inputs)
    aliases = {}
    dq_shape = jax.ShapeDtypeStruct((heads, HD, rows), F32)
    sum_shapes = [jax.ShapeDtypeStruct((heads, rows, LANES), F32)] * 4
    out_shape = [dq_shape] + sum_shapes
    scratch = [pltpu.VMEM((KB, QB), F32), pltpu.VMEM((heads, rows, LANES), BF16)]
    if not own_queries:
        aliases = {given + n: n for n in range(4)}
        inputs += list(sums)
        cols = 3 * HD * heads
        out_shape = sum_shapes + [
            jax.ShapeDtypeStruct((2 * rows, cols), BF16),
            jax.ShapeDtypeStruct((1, cols), F32),
            jax.ShapeDtypeStruct((heads, LANES), F32),
        ]
        scratch.append(pltpu.VMEM((heads, HD, rows), F32))

    def kernel(*refs):
        places_ref, qa_ref = refs[:2]
        pairs = [refs[2 + 2 * n : 4 + 2 * n] for n in range(3)]
        ends = [8, 8 + len(grads), 8 + len(grads) + count, 8 + len(grads) + 2 * count]
        lists = [refs[start:stop] for start, stop in zip(ends[:-1], ends[1:])]
        bits_ref = refs[ends[-1]]
        outs = refs[len(inputs) :]
        if own_queries:
            dq_ref, dk0, dk1, dv0, dv1, bias_ref, ga_ref = outs
        else:
            dk0, dk1, dv0, dv1, joined_ref, bias_out_ref, scorer_out_ref = outs[:7]
            bias_ref, ga_ref, dq_ref = outs[7:]
        attend_back_kernel(
            own_queries,
            places_ref,
            qa_ref,
            *pairs,
            *lists,
            bits_ref,
            dq_ref,
            (dk0, dk1),
            (dv0, dv1),
            bias_ref,
            ga_ref,
        )
        if not own_queries:
            dq_own_ref, scorer_ref = refs[given + 4 : given + 6]
            bias_out_ref[...] = jnp.zeros_like(bias_out_ref)
            scorer_out_ref[...] = jnp.zeros_like(scorer_out_ref)
            ends = (joined_ref, bias_out_ref, scorer_out_ref)
            join_piece(rows, scorer_ref, dq_ref, dk0, dv0, pairs[0][0], *ends)
            join_piece(0, scorer_ref, dq_own_ref, dk1, dv1, pairs[0][1], *ends)

    return pl.pallas_call(
        kernel,
        in_specs=[pl.BlockSpec(memory_space=pltpu.SMEM)] + [in_vmem()] * (len(inputs) - 1),
        out_specs=[in_vmem()] * len(out_shape),
        out_shape=out_shape,
        scratch_shapes=scratch,
        input_output_aliases=aliases,
        compiler_params=pltpu.CompilerParams(vmem_limit_bytes=16 * MIB),
        cost_estimate=SMALL,
        name="attend_back",
    )(*inputs)


def turned_product(parts, others, name, tile=256, chunks=1):
    across = parts[0].shape[1]
    width = others[0].shape[1]
    lengths = [part.shape[0] for part in parts]
    sizes = [other.shape[0] for other in others]
    cuts = sorted({sum(lengths[:n]) for n in range(len(lengths) + 1)} | {sum(sizes[:n]) for n in range(len(sizes) + 1)})

    def rows_of(refs, counts, start, stop):
        base = 0
        for ref, count in zip(refs, counts):
            if base <= start < base + count:
                return ref[start - base : stop - base, :]
            base += count

    def kernel(*refs):
        out_refs = refs[-chunks:]
        lefts, rights = refs[: len(parts)], refs[len(parts) : -chunks]
        total = None
        for start, stop in zip(cuts[:-1], cuts[1:]):
            left = rows_of(lefts, lengths, start, stop)
            part = dot(left, rows_of(rights, sizes, start, stop), TN)
            total = part if total is None else total + part
        value = total.astype(BF16)
        if chunks == 1:
            out_refs[0][...] = value
            return
        for n, ref in enumerate(out_refs):

            @pl.when(pl.program_id(0) == n)
            def _():
                ref[...] = value

    out = pl.pallas_call(
        kernel,
        grid=(across // tile,),
        in_specs=[pl.BlockSpec((n, tile), lambda i: (0, i)) for n in lengths]
        + [whole_block(other) for other in others],
        out_specs=[pl.BlockSpec((tile, width), lambda i: (i if chunks == 1 else 0, 0))] * chunks,
        out_shape=[jax.ShapeDtypeStruct((across // chunks, width), BF16)] * chunks,
        compiler_params=pltpu.CompilerParams(vmem_limit_bytes=20 * MIB),
        cost_estimate=SMALL,
        name=name,
    )(*parts, *others)
    return out[0] if chunks == 1 else out


def choose(refs, at):
    value = refs[0][...]
    for n in range(1, len(refs)):
        value = jnp.where(at == n, refs[n][...], value)
    return value


def chunk_spec(array):
    return pl.BlockSpec(array.shape, lambda i: (0, 0))


def product(rows, weight, dims, first, count, kind, name, chunks=1):
    depth = rows.shape[1]
    width = weight.shape[1] if dims == NN else weight.shape[0]
    span = count // max(chunks, 2)
    shape = (count // chunks, width)

    def kernel(rows_ref, weight_ref, *out_refs):
        value = dot(rows_ref[...], weight_ref[...], dims).astype(kind)
        if chunks == 1:
            out_refs[0][...] = value
            return
        for n, ref in enumerate(out_refs):

            @pl.when(pl.program_id(0) == n)
            def _():
                ref[...] = value

    return pl.pallas_call(
        kernel,
        grid=(count // span,),
        in_specs=[
            pl.BlockSpec((span, depth), lambda i: (first // span + i, 0)),
            whole_block(weight),
        ],
        out_specs=[pl.BlockSpec((span, width), lambda i: (i if chunks == 1 else 0, 0))] * chunks,
        out_shape=[jax.ShapeDtypeStruct(shape, kind)] * chunks,
        compiler_params=pltpu.CompilerParams(vmem_limit_bytes=16 * MIB),
        cost_estimate=SMALL,
        name=name,
    )(rows, weight)


def end_kernel(mixed_ref, active_ref, weight_ref, bias_ref, *refs):
    other = choose(refs[:-1], pl.program_id(0)).astype(F32)
    own = dot(active_ref[...], weight_ref[...])
    refs[-1][...] = mixed_ref[...] + (own + other) + bias_ref[...]


def layer_end(mixed, active, weight, bias, others, start, earlier):
    total, width = mixed.shape
    span, units = others[0].shape[0], weight.shape[0]
    bias = bias.reshape(1, width)
    (out,) = rows_call(
        end_kernel,
        "layer_end",
        span * len(others),
        (mixed, active, weight, bias, *others),
        [
            row_spec(width, span, start // span),
            row_spec(units, span, start // span),
            whole_block(weight),
            whole_block(bias),
        ]
        + [chunk_spec(other) for other in others],
        [(False, width, F32, total, start)],
        0,
        span=span,
        earlier=earlier,
    )
    return out


def pack_kernel(side_ref, weight_ref, joined_ref, bias_ref, scorer_ref, *refs):
    fulls, (fc_ref, out_ref) = refs[:-2], refs[-2:]
    width = fulls[0].shape[1]
    weight = weight_ref[...]
    ones = jnp.ones((8, weight.shape[1]), BF16)
    wide = weight.astype(F32) * joined_ref[...].astype(F32)
    times = sum(dot(ones, part.astype(BF16), NT) for part in split3(wide))
    rows = jnp.broadcast_to(bias_ref[...], (8, weight.shape[1]))
    plain = sum(dot(part.astype(BF16), weight, NT) for part in split3(rows))
    out_ref[...] = jnp.zeros_like(out_ref)
    at = 0
    for value in [times[0:1], plain[0:1]] + [ref[...] for ref in fulls]:
        out_ref[:, at : at + width] = value
        at += width
    heads = scorer_ref.shape[0]
    real = lane_ids(1) < HD
    pairs = []
    for pair in range(heads // 2):
        one, two = scorer_ref[2 * pair : 2 * pair + 1, :], scorer_ref[2 * pair + 1 : 2 * pair + 2, :]
        pairs.append(jnp.where(real, one, pltpu.roll(two, HD, 1)))
    halves = [bias_ref[...]] + pairs + [fc_ref[...]]
    total = sum(half.shape[1] for half in halves)
    for side in range(2):

        @pl.when(side_ref[2] == side)
        def _():
            start = at + side * total
            for half in halves:
                out_ref[:, start : start + half.shape[1]] = half
                start += half.shape[1]


def pack(places, weight, joined, bias, scorer, fulls, fc):
    inputs = (places, weight, joined, bias, scorer, *fulls, fc)
    heads = scorer.shape[0]
    total = (2 + len(fulls)) * weight.shape[0] + 2 * (
        bias.shape[1] + heads * HD + fc.shape[1]
    )
    return pl.pallas_call(
        pack_kernel,
        in_specs=[pl.BlockSpec(memory_space=pltpu.SMEM)] + [in_vmem()] * (len(inputs) - 1),
        out_specs=in_vmem(),
        out_shape=jax.ShapeDtypeStruct((1, total), F32),
        compiler_params=pltpu.CompilerParams(vmem_limit_bytes=16 * MIB),
        cost_estimate=SMALL,
        name="pack",
    )(*inputs)


SPAN = 256


def normalize(values):
    center = values - jnp.mean(values, axis=-1, keepdims=True)
    scale = lax.rsqrt(jnp.mean(center * center, axis=-1, keepdims=True) + 1e-05)
    return center * scale, scale


def norm_back(slope, hat, scale):
    means = jnp.mean(slope, axis=-1, keepdims=True)
    inner = jnp.mean(slope * hat, axis=-1, keepdims=True)
    return (slope - means - hat * inner) * scale


def row_spec(width, span=SPAN, skip=0):
    return pl.BlockSpec((span, width), lambda i, *_: (i + skip, 0))


def sum_rows(values):
    return jnp.sum(values, axis=0, keepdims=True)


def start_at_zero(*refs):
    @pl.when(pl.program_id(0) == 0)
    def _():
        for ref in refs:
            ref[...] = jnp.zeros_like(ref)


def rows_call(
    kernel, name, rows, inputs, in_specs, outs, flops, span=SPAN, earlier=(), limit=16
):
    aliases = {}
    body = kernel
    if earlier:
        first = len(inputs)
        aliases = {first + n: at for n, (at, _) in enumerate(earlier)}
        skip_from, skip_count = first, len(earlier)
        inputs = tuple(inputs) + tuple(array for _, array in earlier)
        in_specs = list(in_specs) + [pl.BlockSpec(memory_space=pl.ANY)] * len(earlier)

        def body(*refs):
            kernel(*refs[:skip_from], *refs[skip_from + skip_count :])

    return pl.pallas_call(
        body,
        grid=(rows // span,),
        in_specs=in_specs,
        out_specs=[
            pl.BlockSpec((1, width), lambda i, *_: (0, 0))
            if one
            else row_spec(width, span, start // span)
            for one, width, _, _, start in outs
        ],
        out_shape=[
            jax.ShapeDtypeStruct((1 if one else total, width), kind)
            for one, width, kind, total, _ in outs
        ],
        input_output_aliases=aliases,
        compiler_params=pltpu.CompilerParams(vmem_limit_bytes=limit * MIB),
        cost_estimate=SMALL,
        name=name,
    )(*inputs)


def norm_one_kernel(in_ref, gain_ref, shift_ref, out_ref):
    hat, _ = normalize(in_ref[...])
    gain = gain_ref[...].reshape(1, gain_ref.shape[0])
    shift = shift_ref[...].reshape(1, shift_ref.shape[0])
    out_ref[...] = (hat * gain + shift).astype(BF16)


def norm_one(layer_in, gain, shift, start, rows):
    width = layer_in.shape[1]
    (out,) = rows_call(
        norm_one_kernel,
        "norm_one",
        rows,
        (layer_in, gain, shift),
        [row_spec(width, skip=start // SPAN), in_vmem(), in_vmem()],
        [(False, width, BF16, rows, 0)],
        rows * width * 8,
        limit=60,
    )
    return out


def narrow_kernel(first_ref, second_ref, out_first_ref, out_second_ref):
    out_first_ref[...] = first_ref[...].astype(BF16)
    out_second_ref[...] = second_ref[...].astype(BF16)


def narrow_halves(values):
    rows, width = values.shape
    half = rows // 2
    return rows_call(
        narrow_kernel,
        "narrow",
        half,
        (values, values),
        [row_spec(width), row_spec(width, skip=half // SPAN)],
        [(False, width, BF16, half, 0)] * 2,
        rows * width,
        limit=60,
    )


def mix_kernel(
    in_ref, own_ref, peer_ref, w_own_ref, w_peer_ref, bias_ref, gain_ref, shift_ref, mixed_ref, norm_ref
):
    part = dot(own_ref[...], w_own_ref[...]) + dot(peer_ref[...], w_peer_ref[...])
    mixed = in_ref[...] + part + bias_ref[...]
    mixed_ref[...] = mixed
    hat, _ = normalize(mixed)
    norm_ref[...] = (hat * gain_ref[...] + shift_ref[...]).astype(BF16)


def mix(layer_in, own, peer, w_own, w_peer, bias, gain, shift, start, earlier):
    total, width = layer_in.shape
    rows, depth = peer.shape
    skip = start // SPAN
    vector = pl.BlockSpec((1, width), lambda i: (0, 0))
    return rows_call(
        mix_kernel,
        "mix",
        rows,
        (layer_in, own, peer, w_own, w_peer)
        + tuple(v.reshape(1, width) for v in (bias, gain, shift)),
        [
            row_spec(width, skip=skip),
            row_spec(depth),
            row_spec(depth),
            whole_block(w_own),
            whole_block(w_peer),
        ]
        + [vector] * 3,
        [(False, width, F32, total, start), (False, width, BF16, rows, 0)],
        rows * width * depth * 4,
        earlier=earlier,
        limit=60,
    )


def feed_kernel(
    norm_ref, grad_ref, fc_ref, bias_ref, proj_ref, active_ref, slope_ref, back_ref, sum_ref
):
    start_at_zero(sum_ref)
    units = fc_ref.shape[1]
    step = 512
    total = None
    for at in range(0, units, step):
        cols = slice(at, at + step)
        hidden = dot(norm_ref[...], fc_ref[:, cols]) + bias_ref[:, cols]
        grad = dot(grad_ref[...], proj_ref[cols, :], NT)
        square = hidden * hidden
        bend = jnp.tanh(hidden * (0.7978845608 + 0.7978845608 * 0.044715 * square))
        half = 0.5 + 0.5 * bend
        active_ref[:, cols] = (hidden * half).astype(BF16)
        inner = 0.7978845608 + 3.0 * 0.7978845608 * 0.044715 * square
        slope = grad * (half + 0.5 * hidden * (1.0 - bend * bend) * inner)
        low = slope.astype(BF16)
        slope_ref[:, cols] = low
        sum_ref[:, cols] += sum_rows(slope)
        part = dot(low, fc_ref[:, cols], NT)
        total = part if total is None else total + part
    back_ref[...] = total.astype(back_ref.dtype)


def feed(norm_rows, grad_rows, fc, bias, proj, back_kind, start, total, earlier):
    rows, width = norm_rows.shape
    units = fc.shape[1]
    bias = bias.reshape(1, units)
    return rows_call(
        feed_kernel,
        "feed",
        rows,
        (norm_rows, grad_rows, fc, bias, proj),
        [
            row_spec(width),
            row_spec(width),
            whole_block(fc),
            whole_block(bias),
            whole_block(proj),
        ],
        [
            (False, units, BF16, total, start),
            (False, units, BF16, total, start),
            (False, width, back_kind, rows, 0),
            (True, units, F32, 1, 0),
        ],
        rows * width * units * 6,
        earlier=earlier,
    )


def mix_back_kernel(
    mixed_ref,
    own_ref,
    other_ref,
    grad_ref,
    gain_ref,
    w_own_ref,
    w_peer_ref,
    out_ref,
    low_ref,
    att_own_ref,
    att_peer_ref,
    gain_out_ref,
    shift_out_ref,
    mixed_out_ref,
    grad_out_ref,
):
    start_at_zero(gain_out_ref, shift_out_ref, mixed_out_ref, grad_out_ref)
    hat, scale = normalize(mixed_ref[...])
    slope = own_ref[...] + other_ref[...].astype(F32)
    gain_out_ref[...] += sum_rows(slope * hat)
    shift_out_ref[...] += sum_rows(slope)
    grad = grad_ref[...]
    grad_out_ref[...] += sum_rows(grad)
    out = grad + norm_back(slope * gain_ref[...], hat, scale)
    mixed_out_ref[...] += sum_rows(out)
    out_ref[...] = out
    low = out.astype(BF16)
    low_ref[...] = low
    att_own_ref[...] = dot(low, w_own_ref[...], NT).astype(BF16)
    att_peer_ref[...] = dot(low, w_peer_ref[...], NT).astype(BF16)


def mix_back(mixed, own, other, grad, gain, w_own, w_peer, start, earlier):
    total, width = mixed.shape
    rows = other.shape[0]
    depth = w_own.shape[0]
    gain = gain.reshape(1, width)
    wide = row_spec(width)
    later = row_spec(width, skip=start // SPAN)
    return rows_call(
        mix_back_kernel,
        "mix_back",
        rows,
        (mixed, own, other, grad, gain, w_own, w_peer),
        [later, wide, wide, later, whole_block(gain), whole_block(w_own), whole_block(w_peer)],
        [
            (False, width, F32, total, start),
            (False, width, BF16, total, start),
            (False, depth, BF16, total, start),
            (False, depth, BF16, rows, 0),
            (True, width, F32, 1, 0),
            (True, width, F32, 1, 0),
            (True, width, F32, 1, 0),
            (True, width, F32, 1, 0),
        ],
        rows * width * depth * 4,
        earlier=earlier,
        limit=60,
    )


def norm_one_back_kernel(in_ref, own_ref, grad_ref, gain_ref, *refs):
    hat, scale = normalize(in_ref[...])
    other = choose(refs[:-1], pl.program_id(0)).astype(F32)
    slope = (own_ref[...] + other) * gain_ref[...]
    refs[-1][...] = grad_ref[...] + norm_back(slope, hat, scale)


def norm_one_back(layer_in, own, grad, gain, others):
    rows, width = layer_in.shape
    span = others[0].shape[0]
    gain = gain.reshape(1, width)
    return pl.pallas_call(
        norm_one_back_kernel,
        grid=(rows // span,),
        in_specs=[row_spec(width, span)] * 3
        + [whole_block(gain)]
        + [chunk_spec(other) for other in others],
        out_specs=row_spec(width, span),
        out_shape=jax.ShapeDtypeStruct((rows, width), F32),
        compiler_params=pltpu.CompilerParams(vmem_limit_bytes=16 * MIB),
        cost_estimate=SMALL,
        name="norm_one_back",
    )(layer_in, own, grad, gain, *others)


def flip_bit(values, bit):
    total = lax.axis_size("dp")
    return lax.ppermute(values, "dp", [(n, n ^ (1 << bit)) for n in range(total)])


def flip_core(values):
    return flip_bit(values, 0)


def flip_tensor(values):
    return lax.ppermute(values, "tensor", [(0, 1), (1, 0)])


def small_call(kernel, name, bits, inputs, outs):
    return pl.pallas_call(
        kernel,
        in_specs=[pl.BlockSpec(memory_space=pltpu.SMEM)] + [in_vmem()] * len(inputs),
        out_specs=[in_vmem()] * len(outs),
        out_shape=[jax.ShapeDtypeStruct(shape, kind) for shape, kind in outs],
        compiler_params=pltpu.CompilerParams(vmem_limit_bytes=16 * MIB),
        cost_estimate=SMALL,
        name=name,
    )(bits, *inputs)


def added(one_ref, two_ref, at, count):
    here = pl.ds(at, count)
    return (one_ref[here].astype(F32) + two_ref[here].astype(F32)).astype(BF16)


def stack_kernel(bits_ref, joined_ref, keep_ref, *refs):
    other_refs, (mine_ref, send_ref) = refs[:-2], refs[-2:]
    width = mine_ref.shape[1]
    rest = joined_ref.shape[1] - width
    step = other_refs[0].shape[0]

    def place(first, second):
        first[...] = joined_ref[:, 0:width]
        second[:, 0:rest] = joined_ref[:, width:]
        for n, other_ref in enumerate(other_refs):
            here = slice(n * step, (n + 1) * step)
            out = keep_ref[here, :].astype(F32) + other_ref[...].astype(F32)
            second[here, rest:] = out.astype(BF16)

    @pl.when(bits_ref[0] == 0)
    def _():
        place(mine_ref, send_ref)

    @pl.when(bits_ref[0] == 1)
    def _():
        place(send_ref, mine_ref)


def split_kernel(places, bits_ref, mine_ref, got_ref, *outs):
    step = mine_ref.shape[0] // (2 * len(places))
    for n, bit in enumerate(places):
        mine = bits_ref[bit]
        base = 2 * n * step
        outs[2 * n][...] = added(mine_ref, got_ref, base + mine * step, step)
        outs[2 * n + 1][...] = added(mine_ref, got_ref, base + (1 - mine) * step, step)


def split_sum(places, bits, mine, got):
    pieces, rows, cols = mine.shape
    shape = ((pieces // (2 * len(places)), rows, cols), BF16)
    return small_call(
        functools.partial(split_kernel, places), "split_sum", bits, (mine, got), [shape] * (2 * len(places))
    )


def add_kernel(bits_ref, mine_ref, got_ref, out_ref):
    out_ref[...] = added(mine_ref, got_ref, 0, mine_ref.shape[0])


def merge_kernel(places, bits_ref, *refs):
    out_ref = refs[-1]
    step = refs[0].shape[0]
    for n, bit in enumerate(places):
        mine = bits_ref[bit]
        base = 2 * n * step
        out_ref[pl.ds(base + mine * step, step)] = refs[2 * n][...]
        out_ref[pl.ds(base + (1 - mine) * step, step)] = refs[2 * n + 1][...]


def merge(places, bits, *inputs):
    pieces, rows, cols = inputs[0].shape
    shape = ((2 * len(places) * pieces, rows, cols), BF16)
    (out,) = small_call(
        functools.partial(merge_kernel, places), "merge", bits, inputs, [shape]
    )
    return out


def unstack_kernel(bits_ref, mine_ref, got_ref, joined_ref, out_ref):
    width = mine_ref.shape[1]
    rest = joined_ref.shape[1] - width

    def place(first, second):
        joined_ref[:, 0:width] = first[...].astype(F32)
        joined_ref[:, width:] = second[:, 0:rest].astype(F32)
        out_ref[...] = second[:, rest:].astype(F32).T

    @pl.when(bits_ref[0] == 0)
    def _():
        place(mine_ref, got_ref)

    @pl.when(bits_ref[0] == 1)
    def _():
        place(got_ref, mine_ref)


def ladder(joined, out_keep, out_others, small, sends, early):
    total = lax.axis_size("dp")
    count = total.bit_length() - 1
    bits = (lax.axis_index("dp") >> jnp.arange(count, dtype=jnp.int32)) & 1
    rows, cols = joined.shape
    width = (cols + out_keep.shape[1]) // 2
    rest = list(range(1, count))
    orders = (rest, rest[1:] + rest[:1])
    state = {"step": 0, "small": small, "sends": list(sends), "sent": [], "made": {}}
    flips = [functools.partial(flip_bit, bit=bit) for bit in range(count)] + [flip_tensor]
    first, first_chunk = 2, 1

    def together(values):
        at = state["step"]
        state["step"] += 1
        beside = []
        sums, chunk = first <= at < first + len(flips), first_chunk <= at < first_chunk + len(sends)
        if sums:
            beside.append(state["small"] + flips[at - first](state["small"]))
        if chunk:
            beside.append(flip_tensor(state["sends"][at - first_chunk]))
        if at in early:
            beside.append(early[at](state["made"], state["sent"]))
        values, beside = lax.optimization_barrier((values, beside))
        if sums:
            state["small"] = beside.pop(0)
        if chunk:
            state["sent"].append(beside.pop(0))
        if at in early:
            state["made"][at] = beside.pop(0)
        return values

    mine, send = small_call(
        stack_kernel, "stack", bits, (joined, out_keep, *out_others), [((rows, width), BF16)] * 2
    )
    cut = (total, rows // total, width)
    mine, got = together((mine.reshape(cut), flip_core(send.reshape(cut))))
    level = split_sum((orders[0][0], orders[1][0]), bits, mine, got)
    parts = [(level[0], level[1]), (level[2], level[3])]
    for n in range(len(rest)):
        both = together([(parts[p][0], flip_bit(parts[p][1], orders[p][n])) for p in range(2)])
        for p, (mine, got) in enumerate(both):
            if n + 1 < len(rest):
                parts[p] = split_sum((orders[p][n + 1],), bits, mine, got)
            else:
                (parts[p],) = small_call(add_kernel, "add_last", bits, (mine, got), [(mine.shape, BF16)])
    for n in reversed(range(len(rest))):
        both = together([(parts[p], flip_bit(parts[p], orders[p][n])) for p in range(2)])
        if n > 0:
            parts = [merge((orders[p][n],), bits, *both[p]) for p in range(2)]
    mine = merge((orders[0][0], orders[1][0]), bits, *both[0], *both[1])
    got = flip_core(mine)
    outs = [((rows, cols), F32), ((out_keep.shape[1], rows), F32)]
    grads = small_call(
        unstack_kernel, "unstack", bits, (mine.reshape(rows, width), got.reshape(rows, width)), outs
    )
    return grads, state["small"], state["made"]


def shards(
    layer_in,
    qkv_weight,
    qkv_bias,
    key_scorer,
    out_weight,
    out_bias,
    fc_weight,
    fc_bias,
    proj_weight,
    proj_bias,
    norm1_gain,
    norm1_shift,
    norm2_gain,
    norm2_shift,
    key_index,
    key_count,
    out_grad,
):
    side = lax.axis_index("tensor")
    own_rows, width = layer_in.shape
    seq = key_index.shape[0]
    half = own_rows // 2
    blocks = own_rows // QB
    places = jnp.stack([side * blocks, (1 - side) * blocks, side]).astype(jnp.int32)

    starts = (0, half)
    norm_own = [norm_one(layer_in, norm1_gain, norm1_shift, at, half) for at in starts]
    norm_peer = [flip_tensor(rows) for rows in norm_own]
    bits = allowed_bits(key_index, key_count)
    grad_lows = narrow_halves(out_grad)
    scorer = scorer_rows(key_scorer)
    core = lax.axis_index("dp") & 1
    out_half = out_weight.shape[0] // 2
    out_mine = lax.dynamic_slice_in_dim(out_weight, core * out_half, out_half, 0)
    bits, out_mine = lax.optimization_barrier((bits, out_mine))
    out_mine = flip_tensor(out_mine)

    own = qkv_heads(norm_own, qkv_weight, qkv_bias, scorer)
    own, *grad_laters = lax.optimization_barrier((own, *grad_lows))
    grad_peers = [flip_tensor(low) for low in grad_laters]
    qa_own, ka_own, va_own, vt_own, kt_own = own
    state = attend_call(
        attend_start_kernel, "attend_start", places, qa_own, (ka_own, vt_own, bits), blocks, 0, (), True
    )
    state, norm_peer = lax.optimization_barrier((state, norm_peer))
    peer = qkv_heads(norm_peer, qkv_weight, qkv_bias, scorer)
    qa_peer, ka_peer, va_peer, vt_peer, kt_peer = peer
    att_owns, logs_owns, att_sends, logs_sends, att_peers = [], [], [], [], []
    for n in range(blocks):
        att_send, logs_send = attend_call(
            functools.partial(attend_other_kernel, n),
            "attend_other",
            places,
            qa_peer,
            (ka_peer, vt_peer, ka_own, vt_own, bits),
            1,
            n,
        )
        att_own, logs_own = attend_call(
            functools.partial(attend_finish_kernel, n),
            "attend_finish",
            places,
            qa_own,
            (ka_peer, vt_peer, bits),
            1,
            n,
            state,
        )
        if n == 1:
            att_send, att_own, att_peers[0], out_mine = lax.optimization_barrier(
                (att_send, att_own, att_peers[0], out_mine)
            )
            out_other = flip_core(out_mine)
        att_send, att_own, qa_peer, qa_own = lax.optimization_barrier(
            (att_send, att_own, qa_peer, qa_own)
        )
        if n == 0:
            att_send, *grad_peers = lax.optimization_barrier((att_send, *grad_peers))
        att_owns.append(att_own)
        logs_owns.append(logs_own)
        att_sends.append(att_send)
        logs_sends.append(logs_send)
        att_peers.append(flip_tensor(att_send))

    out_peer = jnp.where(
        core == 0,
        jnp.concatenate([out_mine, out_other], axis=0),
        jnp.concatenate([out_other, out_mine], axis=0),
    )

    mixed = None
    normed, normed_peers = [], []
    grad_lows = list(grad_lows)
    for n, at in enumerate(starts):
        mixed, low = mix(
            layer_in,
            att_owns[n],
            att_peers[n],
            out_weight,
            out_peer,
            out_bias,
            norm2_gain,
            norm2_shift,
            at,
            () if mixed is None else ((0, mixed),),
        )
        normed.append(low)
        normed_peers.append(flip_tensor(low))
    active = slopes = None
    backs, back_others, fc_sums = [], [], []
    for n, rows in enumerate(normed + normed_peers):
        active, slopes, back, fc_sum = feed(
            rows,
            (grad_lows + grad_peers)[n],
            fc_weight,
            fc_bias,
            proj_weight,
            F32 if n < 2 else BF16,
            n * half,
            seq,
            () if active is None else ((0, active), (1, slopes)),
        )
        fc_sums.append(fc_sum)
        if n < 2:
            backs.append(back)
        else:
            back_others.append(flip_tensor(back))
    grad_fc_bias = sum(fc_sums[1:], fc_sums[0])
    grad_fc_weight = turned_product(normed + normed_peers, [slopes], "fc_slope")
    grad_proj_weight = turned_product([active], grad_lows + grad_peers, "proj_slope", 512)
    proj_sends = product(active, proj_weight, NN, own_rows, own_rows, BF16, "proj_send", 4)
    mixed, grad_fc_weight, grad_proj_weight = lax.optimization_barrier(
        (mixed, grad_fc_weight, grad_proj_weight)
    )
    grad_mixed = grad_mixed_low = grad_att_own = None
    grad_att_peers, row_sums = [], []
    for n, at in enumerate(starts):
        grad_mixed, grad_mixed_low, grad_att_own, grad_att_send, *some = mix_back(
            mixed,
            backs[n],
            back_others[n],
            out_grad,
            norm2_gain,
            out_weight,
            out_peer,
            at,
            ()
            if grad_mixed is None
            else ((0, grad_mixed), (1, grad_mixed_low), (2, grad_att_own)),
        )
        row_sums.append(some)
        grad_att_peers.append(flip_tensor(grad_att_send))
    grad_norm2_gain, grad_norm2_shift, grad_out_bias, grad_proj_bias = (
        one + two for one, two in zip(*row_sums)
    )

    out_sends = turned_product([grad_mixed_low], att_peers, "out_slope", width // 2, 2)
    out_keep = turned_product([grad_mixed_low], att_owns, "out_slope")
    grad_fc_weight, grad_proj_weight = lax.psum((grad_fc_weight, grad_proj_weight), "dp")
    own_keys, peer_keys = (ka_own, kt_own, va_own), (ka_peer, kt_peer, va_peer)
    out_others = [flip_tensor(rows) for rows in out_sends]
    qa_own, proj_sends, out_sends, out_keep = lax.optimization_barrier(
        (qa_own, proj_sends, out_sends, out_keep)
    )
    proj_others = [flip_tensor(rows) for rows in proj_sends]
    dq_own, *key_sums = attend_back(
        True, places, qa_own, (own_keys, peer_keys), [grad_att_own], att_owns, logs_owns, bits
    )
    swapped = (key_sums[1], key_sums[0], key_sums[3], key_sums[2])
    *_, joined, grad_qkv_bias, grad_key_scorer = attend_back(
        False,
        places,
        qa_peer,
        (peer_keys, own_keys),
        grad_att_peers,
        att_sends,
        logs_sends,
        bits,
        swapped + (dq_own, scorer),
    )
    joined, out_others, proj_others = lax.optimization_barrier((joined, out_others, proj_others))
    grad_qkv_weight = turned_product(norm_own + norm_peer, [joined], "qkv_slope")
    one_sends = product(joined, qkv_weight, NT, own_rows, own_rows, BF16, "one_send", 4)
    (one_own,) = product(joined, qkv_weight, NT, 0, own_rows, F32, "one_own")
    layer_half = layer_end(mixed, active, proj_weight, proj_bias, proj_others[:2], 0, ())
    packed = pack(
        places,
        qkv_weight,
        grad_qkv_weight,
        grad_qkv_bias,
        grad_key_scorer,
        (grad_norm2_gain, grad_norm2_shift, grad_out_bias, grad_proj_bias),
        grad_fc_bias,
    )

    grads, packed, made = ladder(
        grad_qkv_weight,
        out_keep,
        out_others,
        packed,
        one_sends,
        {
            0: lambda made, sent: (grad_fc_weight, grad_proj_weight),
            2: lambda made, sent: one_own,
            3: lambda made, sent: layer_half,
            4: lambda made, sent: (
                layer_end(
                    mixed, active, proj_weight, proj_bias, proj_others[2:], half, ((0, made[3]),)
                ),
                made[0][0].astype(F32),
            ),
            5: lambda made, sent: made[0][1].astype(F32),
            6: lambda made, sent: norm_one_back(
                layer_in, made[2], grad_mixed, norm1_gain, sent
            ),
        },
    )
    grad_qkv_weight, grad_out_weight = grads
    (layer_out, grad_fc_weight), grad_proj_weight, input_grad = made[4], made[5], made[6]
    joined_cols = qkv_weight.shape[1]

    full = [packed[0, n * width : (n + 1) * width] for n in range(6)]
    grad_norm1_gain = (full[0] - norm1_shift * full[1]) / norm1_gain
    sizes = (joined_cols, key_scorer.shape[0], fc_bias.shape[0])
    halves = lax.dynamic_slice_in_dim(packed[0], 6 * width + side * sum(sizes), sum(sizes), 0)
    ends = (sizes[0], sizes[0] + sizes[1])
    return (
        layer_out,
        input_grad,
        grad_qkv_weight,
        halves[: ends[0]],
        halves[ends[0] : ends[1]],
        grad_out_weight,
        full[4],
        grad_fc_weight,
        halves[ends[1] :],
        grad_proj_weight,
        full[5],
        grad_norm1_gain,
        full[1],
        full[2],
        full[3],
    )


def solution(mesh):
    rows = P(("dp", "tensor"), None)
    in_specs = (
        rows,
        P(None, "tensor"),
        P("tensor"),
        P("tensor"),
        P("tensor", None),
        P(),
        P(None, "tensor"),
        P("tensor"),
        P("tensor", None),
        P(),
        P(),
        P(),
        P(),
        P(),
        P("dp", None),
        P("dp"),
        rows,
    )
    out_specs = (
        rows,
        rows,
        P(None, "tensor"),
        P("tensor"),
        P("tensor"),
        P("tensor", None),
        P(),
        P(None, "tensor"),
        P("tensor"),
        P("tensor", None),
        P(),
        P(),
        P(),
        P(),
        P(),
    )
    return jax.shard_map(shards, mesh=mesh, in_specs=in_specs, out_specs=out_specs, check_vma=False)
```

```python
import functools
import math

import jax
import jax.numpy as jnp
from jax import lax
from jax.experimental import pallas as pl
from jax.experimental.pallas import tpu as pltpu
from jax.sharding import PartitionSpec as P

HD = 64
LANES = 128
WIN = 64
LOG2E = math.log2(math.e)
LN2 = math.log(2.0)
NEG = -1e30
QB = 512
KB = 512
ROWS = 512
VT = 80
NT = (((1,), (1,)), ((), ()))
NN = (((1,), (0,)), ((), ()))
TN = (((0,), (0,)), ((), ()))
F32 = jnp.float32
BF16 = jnp.bfloat16
MIB = 1024 * 1024
SMALL = pl.CostEstimate(flops=1000, bytes_accessed=1000, transcendentals=0)


def dot(a, b, dims=NN):
    return lax.dot_general(a, b, dims, preferred_element_type=F32)


def split3(x):
    hi = x.astype(BF16).astype(F32)
    rest = x - hi
    mid = rest.astype(BF16).astype(F32)
    low = (rest - mid).astype(BF16).astype(F32)
    return hi, mid, low


def lane_ids(rows):
    return lax.broadcasted_iota(jnp.int32, (rows, LANES), 1)


def put3(base, lanes, first, parts):
    out = base
    for n, part in enumerate(parts):
        out = jnp.where(lanes == first + n, part, out)
    return out


def whole_block(array):
    return pl.BlockSpec(memory_space=pltpu.VMEM)


def scorer_rows(key_scorer):
    return jnp.pad(key_scorer.reshape(-1, HD), ((0, 0), (0, LANES - HD)))


def bits_kernel(low_ref, flag_ref, bits_ref):
    width = bits_ref.shape[1]
    first = pl.program_id(0) * width
    lane = lax.broadcasted_iota(jnp.int32, (LANES, width), 0)
    pos = lax.broadcasted_iota(jnp.int32, (LANES, width), 1) + first
    back = (pos - lane) & (LANES - 1)
    at = pos - back
    bits = jnp.where((back < WIN) & (at >= 0), 1 << (jnp.maximum(at, 0) >> 7), 0)
    for slot in range(low_ref.shape[0]):
        hit = low_ref[slot : slot + 1, :] == lane
        bits = bits | jnp.where(hit, flag_ref[slot : slot + 1, :], 0)
    bits_ref[...] = bits


def allowed_bits(key_index, key_count):
    seq = key_index.shape[0]
    index = key_index.T
    slots = index.shape[0]
    slot = lax.broadcasted_iota(jnp.int32, index.shape, 0)
    used = (slot < key_count[None, :]) & (index >= 0)
    low = index & (LANES - 1)
    flag = jnp.where(used, 1 << (jnp.maximum(index, 0) >> 7), 0)
    width = 256
    spec = pl.BlockSpec((slots, width), lambda i: (0, i))
    return pl.pallas_call(
        bits_kernel,
        grid=(seq // width,),
        in_specs=[spec, spec],
        out_specs=pl.BlockSpec((LANES, width), lambda i: (0, i)),
        out_shape=jax.ShapeDtypeStruct((LANES, seq), jnp.int32),
        cost_estimate=SMALL,
        name="allowed_bits",
    )(low, flag)


def fill_bias(bias_ref, bits_ref, q0, k0):
    depth, width = bias_ref.shape
    bits = bits_ref[:, pl.ds(q0, width)]
    for part in range(depth // LANES):
        shift = k0 // LANES + part
        seen = ((bits >> shift) & 1) == 1
        bias_ref[part * LANES : (part + 1) * LANES, :] = jnp.where(seen, 0.0, NEG)


def qkv_kernel(weight_ref, bias_ref, scorer_ref, *refs):
    norm_refs, (qa_ref, ka_ref, va_ref, vt_ref, kt_ref) = refs[:-5], refs[-5:]
    norm = choose(norm_refs, pl.program_id(0))
    rows = norm.shape[0]
    heads = qa_ref.shape[0]
    lanes = lane_ids(rows)
    real = lanes < HD
    ones = jnp.where((lanes >= HD) & (lanes < HD + 3), 1.0, 0.0)
    for pair in range(heads // 2):
        cols = slice(pair * 6 * HD, (pair + 1) * 6 * HD)
        raw = dot(norm, weight_ref[:, cols]) + bias_ref[:, cols]
        raw = raw.astype(BF16).astype(F32)
        blocks = [raw[:, n * LANES : (n + 1) * LANES] for n in range(3)]
        turned = [pltpu.roll(block, HD, 1) for block in blocks]
        groups = (
            (blocks[0], turned[0], blocks[1]),
            (turned[1], blocks[2], turned[2]),
        )
        for side, (query, key, value) in enumerate(groups):
            head = pair * 2 + side
            raw_gate = jnp.sum(key * scorer_ref[head : head + 1, :], axis=1, keepdims=True)
            gate = jnp.minimum(raw_gate, 0.0) - jnp.log1p(jnp.exp(-jnp.abs(raw_gate)))
            key_plain = jnp.where(real, key, 0.0)
            value_ones = jnp.where(real, value, ones)
            qa_ref[head] = jnp.where(real, query * 0.125, ones).astype(BF16)
            ka_ref[head] = put3(key_plain, lanes, HD, split3(gate)).astype(BF16)
            va_ref[head] = value_ones.astype(BF16)
            vt_ref[head] = value_ones.T[:VT, :].astype(BF16)
            kt_ref[head] = key_plain.T[:HD, :].astype(BF16)


def qkv_heads(norm_pieces, weight, bias, scorer):
    rows = ROWS * len(norm_pieces)
    heads = scorer.shape[0]
    cols = weight.shape[1]
    row_shape = jax.ShapeDtypeStruct((heads, rows, LANES), BF16)
    row_block = pl.BlockSpec((heads, ROWS, LANES), lambda i: (0, i, 0))
    bias = bias.reshape(1, cols)
    return pl.pallas_call(
        qkv_kernel,
        grid=(rows // ROWS,),
        in_specs=[whole_block(weight), whole_block(bias), whole_block(scorer)]
        + [chunk_spec(piece) for piece in norm_pieces],
        out_specs=[
            row_block,
            row_block,
            row_block,
            pl.BlockSpec((heads, VT, ROWS), lambda i: (0, 0, i)),
            pl.BlockSpec((heads, HD, ROWS), lambda i: (0, 0, i)),
        ],
        out_shape=[
            row_shape,
            row_shape,
            row_shape,
            jax.ShapeDtypeStruct((heads, VT, rows), BF16),
            jax.ShapeDtypeStruct((heads, HD, rows), BF16),
        ],
        compiler_params=pltpu.CompilerParams(vmem_limit_bytes=14 * MIB),
        cost_estimate=SMALL,
        name="qkv_heads",
    )(weight, bias, scorer, *norm_pieces)


def attend_block(
    place, q_block, k0, qa_ref, ka_ref, vt_ref, bits_ref, bias_ref, total_ref, peak_ref, corner
):
    heads = qa_ref.shape[0]
    depth, first = corner
    queries = slice(first, QB)
    bias = bias_ref.at[0:depth, queries]
    keys = pl.ds(k0, depth)
    fill_bias(bias, bits_ref, q_block * QB + first, place * KB + k0)

    def scores_of(head):
        return dot(ka_ref[head, keys, :], qa_ref[head, queries, :], NT)

    ahead = scores_of(0)
    for head in range(heads):
        scores = ahead
        if head + 1 < heads:
            ahead = scores_of(head + 1)
        scores = scores * LOG2E + bias[...]
        old = peak_ref[head, :, queries]
        new = jnp.maximum(old, jnp.max(scores, axis=0, keepdims=True))
        weights = jnp.exp2(scores - new[0:1])
        shrink = jnp.exp2(old - new)
        peak_ref[head, :, queries] = new
        part = dot(vt_ref[head, :, keys], weights.astype(BF16))
        total_ref[head, :, queries] = total_ref[head, :, queries] * shrink[0:1] + part


def attend_blocks(count, place, q_block, *refs):
    def step(j, carry):
        k0 = pl.multiple_of(j * KB, KB)
        attend_block(place, q_block, k0, *refs, (KB, 0))
        return carry

    lax.fori_loop(0, count, step, 0)


def attend_diagonal(n, place, q_block, *refs):
    half = KB // 2
    k0 = pl.multiple_of(n * KB, KB)
    attend_block(place, q_block, k0, *refs, (half, 0))
    attend_block(place, q_block, pl.multiple_of(k0 + half, half), *refs, (half, half))


def attend_open(total_ref, peak_ref):
    total_ref[...] = jnp.zeros_like(total_ref)
    peak_ref[...] = jnp.full_like(peak_ref, NEG)


def attend_end(total_ref, peak_ref, out_ref, log_ref):
    heads = total_ref.shape[0]
    for pair in range(heads // 2):
        sides = []
        for head in (2 * pair, 2 * pair + 1):
            mass = total_ref[head, HD : HD + 1, :]
            sides.append(total_ref[head, 0:HD, :] / mass)
            log_ref[head] = peak_ref[head] + jnp.log(mass) * LOG2E
        both = jnp.concatenate(sides, axis=0).T
        out_ref[:, pair * LANES : (pair + 1) * LANES] = both.astype(BF16)


def attend_start_kernel(
    places_ref, qa_ref, ka_ref, vt_ref, bits_ref, total_ref, peak_ref, bias_ref
):
    own = places_ref[0]
    n = pl.program_id(0)
    refs = (qa_ref, ka_ref, vt_ref, bits_ref, bias_ref, total_ref, peak_ref)
    attend_open(total_ref, peak_ref)
    attend_blocks(n, own, own + n, *refs)
    attend_diagonal(n, own, own + n, *refs)


def attend_finish_kernel(
    n,
    places_ref,
    qa_ref,
    ka_ref,
    vt_ref,
    bits_ref,
    total_in_ref,
    peak_in_ref,
    out_ref,
    log_ref,
    bias_ref,
    total_ref,
    peak_ref,
):
    own, peer, later = places_ref[0], places_ref[1], places_ref[2]
    refs = (qa_ref, ka_ref, vt_ref, bits_ref, bias_ref, total_ref, peak_ref)
    total_ref[...] = total_in_ref[...]
    peak_ref[...] = peak_in_ref[...]
    attend_blocks(later * (ka_ref.shape[1] // KB), peer, own + n, *refs)
    attend_end(total_ref, peak_ref, out_ref, log_ref)


def attend_other_kernel(
    n,
    places_ref,
    qa_ref,
    ka_ref,
    vt_ref,
    ka_own_ref,
    vt_own_ref,
    bits_ref,
    out_ref,
    log_ref,
    bias_ref,
    total_ref,
    peak_ref,
):
    own, peer, later = places_ref[0], places_ref[1], places_ref[2]
    block = peer + n
    tail = (bits_ref, bias_ref, total_ref, peak_ref)
    attend_open(total_ref, peak_ref)
    for at in range(n):
        attend_block(peer, block, at * KB, qa_ref, ka_ref, vt_ref, *tail, (KB, 0))
    attend_diagonal(n, peer, block, qa_ref, ka_ref, vt_ref, *tail)
    earlier = (1 - later) * (ka_own_ref.shape[1] // KB)
    attend_blocks(earlier, own, block, qa_ref, ka_own_ref, vt_own_ref, *tail)
    attend_end(total_ref, peak_ref, out_ref, log_ref)


def attend_call(kernel, name, places, qa, others, count, first, state=(), keep=False):
    heads = qa.shape[0]
    total_spec = pl.BlockSpec((heads, VT, QB), lambda i, _: (0, 0, first + i))
    peak_spec = pl.BlockSpec((heads, 8, QB), lambda i, _: (0, 0, first + i))
    log_spec = pl.BlockSpec((heads, 8, QB), lambda i, _: (0, 0, i))
    total_shape = jax.ShapeDtypeStruct((heads, VT, count * QB), F32)
    peak_shape = jax.ShapeDtypeStruct((heads, 8, count * QB), F32)
    scratch = [
        pltpu.VMEM((KB, QB), F32),
        pltpu.VMEM((heads, VT, QB), F32),
        pltpu.VMEM((heads, 8, QB), F32),
    ]
    if keep:
        out_specs, out_shape = [total_spec, peak_spec], [total_shape, peak_shape]
        scratch = scratch[:1]
    else:
        out_specs = [pl.BlockSpec((QB, heads * HD), lambda i, _: (i, 0)), log_spec]
        out_shape = [jax.ShapeDtypeStruct((count * QB, heads * HD), BF16), peak_shape]
    return pl.pallas_call(
        kernel,
        grid_spec=pltpu.PrefetchScalarGridSpec(
            num_scalar_prefetch=1,
            grid=(count,),
            in_specs=[pl.BlockSpec((heads, QB, LANES), lambda i, _: (0, first + i, 0))]
            + [whole_block(array) for array in others]
            + ([total_spec, peak_spec] if state else []),
            out_specs=out_specs,
            scratch_shapes=scratch,
        ),
        out_shape=out_shape,
        compiler_params=pltpu.CompilerParams(vmem_limit_bytes=16 * MIB),
        cost_estimate=SMALL,
        name=name,
    )(places, qa, *others, *state)


def in_vmem():
    return pl.BlockSpec(memory_space=pltpu.VMEM)


def attend_back_kernel(
    own_queries,
    places_ref,
    qa_ref,
    ka_refs,
    kt_refs,
    va_refs,
    grad_refs,
    att_refs,
    log_refs,
    bits_ref,
    dq_ref,
    dk_refs,
    dv_refs,
    bias_ref,
    ga_ref,
):
    heads, rows, _ = qa_ref.shape
    blocks = rows // QB
    lanes = lane_ids(ROWS)
    dq_ref[...] = jnp.zeros_like(dq_ref)
    if own_queries:
        for ref in tuple(dk_refs) + tuple(dv_refs):
            ref[...] = jnp.zeros_like(ref)

    for n in range(len(att_refs)):
        rows_n = slice(n * ROWS, (n + 1) * ROWS)
        grad_rows = grad_refs[n] if len(grad_refs) > 1 else grad_refs[0].at[rows_n, :]
        for pair in range(heads // 2):
            cols = slice(pair * LANES, (pair + 1) * LANES)
            grad = grad_rows[:, cols].astype(F32)
            prod = grad * att_refs[n][:, cols].astype(F32)
            turned = pltpu.roll(grad, HD, 1)
            for side, values in enumerate((grad, turned)):
                mine = (lanes < HD) if side == 0 else (lanes >= HD)
                inner = jnp.sum(jnp.where(mine, prod, 0.0), axis=1, keepdims=True)
                plain = jnp.where(lanes < HD, values, 0.0)
                filled = put3(plain, lanes, HD, split3(-inner))
                ga_ref[pair * 2 + side, rows_n, :] = filled.astype(BF16)

    q_place, k_places = places_ref[0], (places_ref[0], places_ref[1])
    later = places_ref[2]
    if not own_queries:
        q_place, k_places = k_places[1], (k_places[1], k_places[0])
        later = 1 - later

    def tile(piece, j, n, i, corner):
        depth, first = corner
        width = QB - first
        k1 = pl.multiple_of(j * KB + first, KB // 2)
        q1 = pl.multiple_of(i * QB + first, QB // 2)
        keys = pl.ds(k1, depth)
        queries = pl.ds(q1, width)
        bias = bias_ref.at[0:depth, 0:width]
        fill_bias(bias, bits_ref, q_place * QB + q1, k_places[piece] * KB + k1)
        ka_ref, kt_ref, va_ref = ka_refs[piece], kt_refs[piece], va_refs[piece]
        dk_ref, dv_ref = dk_refs[piece], dv_refs[piece]

        def first_of(head):
            qa = qa_ref[head, queries, :]
            ga = ga_ref[head, queries, :]
            return (
                qa,
                ga,
                dot(ka_ref[head, keys, :], qa, NT),
                dot(va_ref[head, keys, :], ga, NT),
            )

        ahead = first_of(0)
        for head in range(heads):
            qa, ga, scores, inner = ahead
            if head + 1 < heads:
                ahead = first_of(head + 1)
            scores = scores * LOG2E + bias[...]
            if isinstance(n, int):
                logs = log_refs[n][head, 0:1, first:QB]
            else:
                logs = jnp.where(n == 0, log_refs[0][head, 0:1, :], log_refs[1][head, 0:1, :])
            probs = jnp.exp2(scores - logs)
            slopes = (probs * inner).astype(BF16)
            dv_ref[head, keys, :] += dot(probs.astype(BF16), ga)
            dk_ref[head, keys, :] += dot(slopes, qa)
            dq_ref[head, :, queries] += dot(kt_ref[head, :, keys], slopes)

    half = KB // 2
    for n in range(blocks):
        tile(0, n, n, n, (half, 0))
        tile(0, n, n, n, (half, half))
        for j in range(n):
            tile(0, j, n, n, (KB, 0))

    def step(at, carry):
        i = at & (blocks - 1)
        tile(1, at // blocks, i, i, (KB, 0))
        return carry

    lax.fori_loop(0, later * (blocks * blocks), step, 0)


def join_piece(first, scorer_ref, dq_ref, dk_ref, dv_ref, ka_ref, joined_ref, bias_out_ref, scorer_out_ref):
    heads, rows, _ = dk_ref.shape
    span = 256
    lanes = lane_ids(span)
    real = lanes < HD

    def step(at, carry):
        here = pl.ds(pl.multiple_of(at * span, span), span)
        there = pl.ds(pl.multiple_of(at * span + first, span), span)
        for pair in range(heads // 2):
            dq = dq_ref[2 * pair : 2 * pair + 2, :, here].reshape(LANES, span).T * 0.125
            dks, dvs = [], []
            for head in (2 * pair, 2 * pair + 1):
                scorer = scorer_ref[head : head + 1, :]
                key = ka_ref[head, here, :].astype(F32)
                dk = dk_ref[head, here, :]
                raw_gate = jnp.sum(key * scorer, axis=1, keepdims=True)
                slope = dk[:, HD : HD + 1] / (1.0 + jnp.exp(raw_gate))
                scorer_out_ref[head : head + 1, :] += sum_rows(slope * key)
                dks.append(dk + slope * scorer)
                dvs.append(dv_ref[head, here, :])
            blocks = (
                jnp.where(real, dq, pltpu.roll(dks[0], HD, 1)),
                jnp.where(real, dvs[0], dq),
                jnp.where(real, dks[1], pltpu.roll(dvs[1], HD, 1)),
            )
            for n, block in enumerate(blocks):
                cols = slice((pair * 3 + n) * LANES, (pair * 3 + n + 1) * LANES)
                bias_out_ref[:, cols] += sum_rows(block)
                joined_ref[there, cols] = block.astype(BF16)
        return carry

    lax.fori_loop(0, rows // span, step, 0)


def attend_back(own_queries, places, qa, keys, grads, atts, logs, bits, sums=None):
    heads, rows, _ = qa.shape
    count = len(atts)
    inputs = [places, qa]
    for kind in range(3):
        inputs += [keys[0][kind], keys[1][kind]]
    inputs += list(grads) + list(atts) + list(logs) + [bits]
    given = len(inputs)
    aliases = {}
    dq_shape = jax.ShapeDtypeStruct((heads, HD, rows), F32)
    sum_shapes = [jax.ShapeDtypeStruct((heads, rows, LANES), F32)] * 4
    out_shape = [dq_shape] + sum_shapes
    scratch = [pltpu.VMEM((KB, QB), F32), pltpu.VMEM((heads, rows, LANES), BF16)]
    if not own_queries:
        aliases = {given + n: n for n in range(4)}
        inputs += list(sums)
        cols = 3 * HD * heads
        out_shape = sum_shapes + [
            jax.ShapeDtypeStruct((2 * rows, cols), BF16),
            jax.ShapeDtypeStruct((1, cols), F32),
            jax.ShapeDtypeStruct((heads, LANES), F32),
        ]
        scratch.append(pltpu.VMEM((heads, HD, rows), F32))

    def kernel(*refs):
        places_ref, qa_ref = refs[:2]
        pairs = [refs[2 + 2 * n : 4 + 2 * n] for n in range(3)]
        ends = [8, 8 + len(grads), 8 + len(grads) + count, 8 + len(grads) + 2 * count]
        lists = [refs[start:stop] for start, stop in zip(ends[:-1], ends[1:])]
        bits_ref = refs[ends[-1]]
        outs = refs[len(inputs) :]
        if own_queries:
            dq_ref, dk0, dk1, dv0, dv1, bias_ref, ga_ref = outs
        else:
            dk0, dk1, dv0, dv1, joined_ref, bias_out_ref, scorer_out_ref = outs[:7]
            bias_ref, ga_ref, dq_ref = outs[7:]
        attend_back_kernel(
            own_queries,
            places_ref,
            qa_ref,
            *pairs,
            *lists,
            bits_ref,
            dq_ref,
            (dk0, dk1),
            (dv0, dv1),
            bias_ref,
            ga_ref,
        )
        if not own_queries:
            dq_own_ref, scorer_ref = refs[given + 4 : given + 6]
            bias_out_ref[...] = jnp.zeros_like(bias_out_ref)
            scorer_out_ref[...] = jnp.zeros_like(scorer_out_ref)
            ends = (joined_ref, bias_out_ref, scorer_out_ref)
            join_piece(rows, scorer_ref, dq_ref, dk0, dv0, pairs[0][0], *ends)
            join_piece(0, scorer_ref, dq_own_ref, dk1, dv1, pairs[0][1], *ends)

    return pl.pallas_call(
        kernel,
        in_specs=[pl.BlockSpec(memory_space=pltpu.SMEM)] + [in_vmem()] * (len(inputs) - 1),
        out_specs=[in_vmem()] * len(out_shape),
        out_shape=out_shape,
        scratch_shapes=scratch,
        input_output_aliases=aliases,
        compiler_params=pltpu.CompilerParams(vmem_limit_bytes=16 * MIB),
        cost_estimate=SMALL,
        name="attend_back",
    )(*inputs)


def turned_product(parts, others, name, tile=256, chunks=1):
    across = parts[0].shape[1]
    width = others[0].shape[1]
    lengths = [part.shape[0] for part in parts]
    sizes = [other.shape[0] for other in others]
    cuts = sorted({sum(lengths[:n]) for n in range(len(lengths) + 1)} | {sum(sizes[:n]) for n in range(len(sizes) + 1)})

    def rows_of(refs, counts, start, stop):
        base = 0
        for ref, count in zip(refs, counts):
            if base <= start < base + count:
                return ref[start - base : stop - base, :]
            base += count

    def kernel(*refs):
        out_refs = refs[-chunks:]
        lefts, rights = refs[: len(parts)], refs[len(parts) : -chunks]
        total = None
        for start, stop in zip(cuts[:-1], cuts[1:]):
            left = rows_of(lefts, lengths, start, stop)
            part = dot(left, rows_of(rights, sizes, start, stop), TN)
            total = part if total is None else total + part
        value = total.astype(BF16)
        if chunks == 1:
            out_refs[0][...] = value
            return
        for n, ref in enumerate(out_refs):

            @pl.when(pl.program_id(0) == n)
            def _():
                ref[...] = value

    out = pl.pallas_call(
        kernel,
        grid=(across // tile,),
        in_specs=[pl.BlockSpec((n, tile), lambda i: (0, i)) for n in lengths]
        + [whole_block(other) for other in others],
        out_specs=[pl.BlockSpec((tile, width), lambda i: (i if chunks == 1 else 0, 0))] * chunks,
        out_shape=[jax.ShapeDtypeStruct((across // chunks, width), BF16)] * chunks,
        compiler_params=pltpu.CompilerParams(vmem_limit_bytes=20 * MIB),
        cost_estimate=SMALL,
        name=name,
    )(*parts, *others)
    return out[0] if chunks == 1 else out


def choose(refs, at):
    value = refs[0][...]
    for n in range(1, len(refs)):
        value = jnp.where(at == n, refs[n][...], value)
    return value


def chunk_spec(array):
    return pl.BlockSpec(array.shape, lambda i: (0, 0))


def product(rows, weight, dims, first, count, kind, name, chunks=1):
    depth = rows.shape[1]
    width = weight.shape[1] if dims == NN else weight.shape[0]
    span = count // max(chunks, 2)
    shape = (count // chunks, width)

    def kernel(rows_ref, weight_ref, *out_refs):
        value = dot(rows_ref[...], weight_ref[...], dims).astype(kind)
        if chunks == 1:
            out_refs[0][...] = value
            return
        for n, ref in enumerate(out_refs):

            @pl.when(pl.program_id(0) == n)
            def _():
                ref[...] = value

    return pl.pallas_call(
        kernel,
        grid=(count // span,),
        in_specs=[
            pl.BlockSpec((span, depth), lambda i: (first // span + i, 0)),
            whole_block(weight),
        ],
        out_specs=[pl.BlockSpec((span, width), lambda i: (i if chunks == 1 else 0, 0))] * chunks,
        out_shape=[jax.ShapeDtypeStruct(shape, kind)] * chunks,
        compiler_params=pltpu.CompilerParams(vmem_limit_bytes=16 * MIB),
        cost_estimate=SMALL,
        name=name,
    )(rows, weight)


def end_kernel(mixed_ref, active_ref, weight_ref, bias_ref, *refs):
    other = choose(refs[:-1], pl.program_id(0)).astype(F32)
    own = dot(active_ref[...], weight_ref[...])
    refs[-1][...] = mixed_ref[...] + (own + other) + bias_ref[...]


def layer_end(mixed, active, weight, bias, others, start, earlier):
    total, width = mixed.shape
    span, units = others[0].shape[0], weight.shape[0]
    bias = bias.reshape(1, width)
    (out,) = rows_call(
        end_kernel,
        "layer_end",
        span * len(others),
        (mixed, active, weight, bias, *others),
        [
            row_spec(width, span, start // span),
            row_spec(units, span, start // span),
            whole_block(weight),
            whole_block(bias),
        ]
        + [chunk_spec(other) for other in others],
        [(False, width, F32, total, start)],
        0,
        span=span,
        earlier=earlier,
    )
    return out


def pack_kernel(side_ref, weight_ref, joined_ref, bias_ref, scorer_ref, *refs):
    fulls, (fc_ref, out_ref) = refs[:-2], refs[-2:]
    width = fulls[0].shape[1]
    weight = weight_ref[...]
    ones = jnp.ones((8, weight.shape[1]), BF16)
    wide = weight.astype(F32) * joined_ref[...].astype(F32)
    times = sum(dot(ones, part.astype(BF16), NT) for part in split3(wide))
    rows = jnp.broadcast_to(bias_ref[...], (8, weight.shape[1]))
    plain = sum(dot(part.astype(BF16), weight, NT) for part in split3(rows))
    out_ref[...] = jnp.zeros_like(out_ref)
    at = 0
    for value in [times[0:1], plain[0:1]] + [ref[...] for ref in fulls]:
        out_ref[:, at : at + width] = value
        at += width
    heads = scorer_ref.shape[0]
    real = lane_ids(1) < HD
    pairs = []
    for pair in range(heads // 2):
        one, two = scorer_ref[2 * pair : 2 * pair + 1, :], scorer_ref[2 * pair + 1 : 2 * pair + 2, :]
        pairs.append(jnp.where(real, one, pltpu.roll(two, HD, 1)))
    halves = [bias_ref[...]] + pairs + [fc_ref[...]]
    total = sum(half.shape[1] for half in halves)
    for side in range(2):

        @pl.when(side_ref[2] == side)
        def _():
            start = at + side * total
            for half in halves:
                out_ref[:, start : start + half.shape[1]] = half
                start += half.shape[1]


def pack(places, weight, joined, bias, scorer, fulls, fc):
    inputs = (places, weight, joined, bias, scorer, *fulls, fc)
    heads = scorer.shape[0]
    total = (2 + len(fulls)) * weight.shape[0] + 2 * (
        bias.shape[1] + heads * HD + fc.shape[1]
    )
    return pl.pallas_call(
        pack_kernel,
        in_specs=[pl.BlockSpec(memory_space=pltpu.SMEM)] + [in_vmem()] * (len(inputs) - 1),
        out_specs=in_vmem(),
        out_shape=jax.ShapeDtypeStruct((1, total), F32),
        compiler_params=pltpu.CompilerParams(vmem_limit_bytes=16 * MIB),
        cost_estimate=SMALL,
        name="pack",
    )(*inputs)


SPAN = 256


def normalize(values):
    center = values - jnp.mean(values, axis=-1, keepdims=True)
    scale = lax.rsqrt(jnp.mean(center * center, axis=-1, keepdims=True) + 1e-05)
    return center * scale, scale


def norm_back(slope, hat, scale):
    means = jnp.mean(slope, axis=-1, keepdims=True)
    inner = jnp.mean(slope * hat, axis=-1, keepdims=True)
    return (slope - means - hat * inner) * scale


def row_spec(width, span=SPAN, skip=0):
    return pl.BlockSpec((span, width), lambda i, *_: (i + skip, 0))


def sum_rows(values):
    return jnp.sum(values, axis=0, keepdims=True)


def start_at_zero(*refs):
    @pl.when(pl.program_id(0) == 0)
    def _():
        for ref in refs:
            ref[...] = jnp.zeros_like(ref)


def rows_call(
    kernel, name, rows, inputs, in_specs, outs, flops, span=SPAN, earlier=(), limit=16
):
    aliases = {}
    body = kernel
    if earlier:
        first = len(inputs)
        aliases = {first + n: at for n, (at, _) in enumerate(earlier)}
        skip_from, skip_count = first, len(earlier)
        inputs = tuple(inputs) + tuple(array for _, array in earlier)
        in_specs = list(in_specs) + [pl.BlockSpec(memory_space=pl.ANY)] * len(earlier)

        def body(*refs):
            kernel(*refs[:skip_from], *refs[skip_from + skip_count :])

    return pl.pallas_call(
        body,
        grid=(rows // span,),
        in_specs=in_specs,
        out_specs=[
            pl.BlockSpec((1, width), lambda i, *_: (0, 0))
            if one
            else row_spec(width, span, start // span)
            for one, width, _, _, start in outs
        ],
        out_shape=[
            jax.ShapeDtypeStruct((1 if one else total, width), kind)
            for one, width, kind, total, _ in outs
        ],
        input_output_aliases=aliases,
        compiler_params=pltpu.CompilerParams(vmem_limit_bytes=limit * MIB),
        cost_estimate=SMALL,
        name=name,
    )(*inputs)


def norm_one_kernel(in_ref, gain_ref, shift_ref, out_ref):
    hat, _ = normalize(in_ref[...])
    gain = gain_ref[...].reshape(1, gain_ref.shape[0])
    shift = shift_ref[...].reshape(1, shift_ref.shape[0])
    out_ref[...] = (hat * gain + shift).astype(BF16)


def norm_one(layer_in, gain, shift, start, rows):
    width = layer_in.shape[1]
    (out,) = rows_call(
        norm_one_kernel,
        "norm_one",
        rows,
        (layer_in, gain, shift),
        [row_spec(width, skip=start // SPAN), in_vmem(), in_vmem()],
        [(False, width, BF16, rows, 0)],
        rows * width * 8,
        limit=60,
    )
    return out


def narrow_kernel(first_ref, second_ref, out_first_ref, out_second_ref):
    out_first_ref[...] = first_ref[...].astype(BF16)
    out_second_ref[...] = second_ref[...].astype(BF16)


def narrow_halves(values):
    rows, width = values.shape
    half = rows // 2
    return rows_call(
        narrow_kernel,
        "narrow",
        half,
        (values, values),
        [row_spec(width), row_spec(width, skip=half // SPAN)],
        [(False, width, BF16, half, 0)] * 2,
        rows * width,
        limit=60,
    )


def mix_kernel(
    in_ref, own_ref, peer_ref, w_own_ref, w_peer_ref, bias_ref, gain_ref, shift_ref, mixed_ref, norm_ref
):
    part = dot(own_ref[...], w_own_ref[...]) + dot(peer_ref[...], w_peer_ref[...])
    mixed = in_ref[...] + part + bias_ref[...]
    mixed_ref[...] = mixed
    hat, _ = normalize(mixed)
    norm_ref[...] = (hat * gain_ref[...] + shift_ref[...]).astype(BF16)


def mix(layer_in, own, peer, w_own, w_peer, bias, gain, shift, start, earlier):
    total, width = layer_in.shape
    rows, depth = peer.shape
    skip = start // SPAN
    vector = pl.BlockSpec((1, width), lambda i: (0, 0))
    return rows_call(
        mix_kernel,
        "mix",
        rows,
        (layer_in, own, peer, w_own, w_peer)
        + tuple(v.reshape(1, width) for v in (bias, gain, shift)),
        [
            row_spec(width, skip=skip),
            row_spec(depth),
            row_spec(depth),
            whole_block(w_own),
            whole_block(w_peer),
        ]
        + [vector] * 3,
        [(False, width, F32, total, start), (False, width, BF16, rows, 0)],
        rows * width * depth * 4,
        earlier=earlier,
        limit=60,
    )


def feed_kernel(
    norm_ref, grad_ref, fc_ref, bias_ref, proj_ref, active_ref, slope_ref, back_ref, sum_ref
):
    start_at_zero(sum_ref)
    units = fc_ref.shape[1]
    step = 512
    total = None
    for at in range(0, units, step):
        cols = slice(at, at + step)
        hidden = dot(norm_ref[...], fc_ref[:, cols]) + bias_ref[:, cols]
        grad = dot(grad_ref[...], proj_ref[cols, :], NT)
        square = hidden * hidden
        bend = jnp.tanh(hidden * (0.7978845608 + 0.7978845608 * 0.044715 * square))
        half = 0.5 + 0.5 * bend
        active_ref[:, cols] = (hidden * half).astype(BF16)
        inner = 0.7978845608 + 3.0 * 0.7978845608 * 0.044715 * square
        slope = grad * (half + 0.5 * hidden * (1.0 - bend * bend) * inner)
        low = slope.astype(BF16)
        slope_ref[:, cols] = low
        sum_ref[:, cols] += sum_rows(slope)
        part = dot(low, fc_ref[:, cols], NT)
        total = part if total is None else total + part
    back_ref[...] = total.astype(back_ref.dtype)


def feed(norm_rows, grad_rows, fc, bias, proj, back_kind, start, total, earlier):
    rows, width = norm_rows.shape
    units = fc.shape[1]
    bias = bias.reshape(1, units)
    return rows_call(
        feed_kernel,
        "feed",
        rows,
        (norm_rows, grad_rows, fc, bias, proj),
        [
            row_spec(width),
            row_spec(width),
            whole_block(fc),
            whole_block(bias),
            whole_block(proj),
        ],
        [
            (False, units, BF16, total, start),
            (False, units, BF16, total, start),
            (False, width, back_kind, rows, 0),
            (True, units, F32, 1, 0),
        ],
        rows * width * units * 6,
        earlier=earlier,
    )


def mix_back_kernel(
    mixed_ref,
    own_ref,
    other_ref,
    grad_ref,
    gain_ref,
    w_own_ref,
    w_peer_ref,
    out_ref,
    low_ref,
    att_own_ref,
    att_peer_ref,
    gain_out_ref,
    shift_out_ref,
    mixed_out_ref,
    grad_out_ref,
):
    start_at_zero(gain_out_ref, shift_out_ref, mixed_out_ref, grad_out_ref)
    hat, scale = normalize(mixed_ref[...])
    slope = own_ref[...] + other_ref[...].astype(F32)
    gain_out_ref[...] += sum_rows(slope * hat)
    shift_out_ref[...] += sum_rows(slope)
    grad = grad_ref[...]
    grad_out_ref[...] += sum_rows(grad)
    out = grad + norm_back(slope * gain_ref[...], hat, scale)
    mixed_out_ref[...] += sum_rows(out)
    out_ref[...] = out
    low = out.astype(BF16)
    low_ref[...] = low
    att_own_ref[...] = dot(low, w_own_ref[...], NT).astype(BF16)
    att_peer_ref[...] = dot(low, w_peer_ref[...], NT).astype(BF16)


def mix_back(mixed, own, other, grad, gain, w_own, w_peer, start, earlier):
    total, width = mixed.shape
    rows = other.shape[0]
    depth = w_own.shape[0]
    gain = gain.reshape(1, width)
    wide = row_spec(width)
    later = row_spec(width, skip=start // SPAN)
    return rows_call(
        mix_back_kernel,
        "mix_back",
        rows,
        (mixed, own, other, grad, gain, w_own, w_peer),
        [later, wide, wide, later, whole_block(gain), whole_block(w_own), whole_block(w_peer)],
        [
            (False, width, F32, total, start),
            (False, width, BF16, total, start),
            (False, depth, BF16, total, start),
            (False, depth, BF16, rows, 0),
            (True, width, F32, 1, 0),
            (True, width, F32, 1, 0),
            (True, width, F32, 1, 0),
            (True, width, F32, 1, 0),
        ],
        rows * width * depth * 4,
        earlier=earlier,
        limit=60,
    )


def norm_one_back_kernel(in_ref, own_ref, grad_ref, gain_ref, *refs):
    hat, scale = normalize(in_ref[...])
    other = choose(refs[:-1], pl.program_id(0)).astype(F32)
    slope = (own_ref[...] + other) * gain_ref[...]
    refs[-1][...] = grad_ref[...] + norm_back(slope, hat, scale)


def norm_one_back(layer_in, own, grad, gain, others):
    rows, width = layer_in.shape
    span = others[0].shape[0]
    gain = gain.reshape(1, width)
    return pl.pallas_call(
        norm_one_back_kernel,
        grid=(rows // span,),
        in_specs=[row_spec(width, span)] * 3
        + [whole_block(gain)]
        + [chunk_spec(other) for other in others],
        out_specs=row_spec(width, span),
        out_shape=jax.ShapeDtypeStruct((rows, width), F32),
        compiler_params=pltpu.CompilerParams(vmem_limit_bytes=16 * MIB),
        cost_estimate=SMALL,
        name="norm_one_back",
    )(layer_in, own, grad, gain, *others)


def flip_bit(values, bit):
    total = lax.axis_size("dp")
    return lax.ppermute(values, "dp", [(n, n ^ (1 << bit)) for n in range(total)])


def flip_core(values):
    return flip_bit(values, 0)


def flip_tensor(values):
    return lax.ppermute(values, "tensor", [(0, 1), (1, 0)])


def small_call(kernel, name, bits, inputs, outs):
    return pl.pallas_call(
        kernel,
        in_specs=[pl.BlockSpec(memory_space=pltpu.SMEM)] + [in_vmem()] * len(inputs),
        out_specs=[in_vmem()] * len(outs),
        out_shape=[jax.ShapeDtypeStruct(shape, kind) for shape, kind in outs],
        compiler_params=pltpu.CompilerParams(vmem_limit_bytes=16 * MIB),
        cost_estimate=SMALL,
        name=name,
    )(bits, *inputs)


def added(one_ref, two_ref, at, count):
    here = pl.ds(at, count)
    return (one_ref[here].astype(F32) + two_ref[here].astype(F32)).astype(BF16)


def stack_kernel(bits_ref, joined_ref, keep_ref, *refs):
    other_refs, (mine_ref, send_ref) = refs[:-2], refs[-2:]
    width = mine_ref.shape[1]
    rest = joined_ref.shape[1] - width
    step = other_refs[0].shape[0]

    def place(first, second):
        first[...] = joined_ref[:, 0:width]
        second[:, 0:rest] = joined_ref[:, width:]
        for n, other_ref in enumerate(other_refs):
            here = slice(n * step, (n + 1) * step)
            out = keep_ref[here, :].astype(F32) + other_ref[...].astype(F32)
            second[here, rest:] = out.astype(BF16)

    @pl.when(bits_ref[0] == 0)
    def _():
        place(mine_ref, send_ref)

    @pl.when(bits_ref[0] == 1)
    def _():
        place(send_ref, mine_ref)


def split_kernel(places, bits_ref, mine_ref, got_ref, *outs):
    step = mine_ref.shape[0] // (2 * len(places))
    for n, bit in enumerate(places):
        mine = bits_ref[bit]
        base = 2 * n * step
        outs[2 * n][...] = added(mine_ref, got_ref, base + mine * step, step)
        outs[2 * n + 1][...] = added(mine_ref, got_ref, base + (1 - mine) * step, step)


def split_sum(places, bits, mine, got):
    pieces, rows, cols = mine.shape
    shape = ((pieces // (2 * len(places)), rows, cols), BF16)
    return small_call(
        functools.partial(split_kernel, places), "split_sum", bits, (mine, got), [shape] * (2 * len(places))
    )


def add_kernel(bits_ref, mine_ref, got_ref, out_ref):
    out_ref[...] = added(mine_ref, got_ref, 0, mine_ref.shape[0])


def merge_kernel(places, bits_ref, *refs):
    out_ref = refs[-1]
    step = refs[0].shape[0]
    for n, bit in enumerate(places):
        mine = bits_ref[bit]
        base = 2 * n * step
        out_ref[pl.ds(base + mine * step, step)] = refs[2 * n][...]
        out_ref[pl.ds(base + (1 - mine) * step, step)] = refs[2 * n + 1][...]


def merge(places, bits, *inputs):
    pieces, rows, cols = inputs[0].shape
    shape = ((2 * len(places) * pieces, rows, cols), BF16)
    (out,) = small_call(
        functools.partial(merge_kernel, places), "merge", bits, inputs, [shape]
    )
    return out


def unstack_kernel(bits_ref, mine_ref, got_ref, joined_ref, out_ref):
    width = mine_ref.shape[1]
    rest = joined_ref.shape[1] - width

    def place(first, second):
        joined_ref[:, 0:width] = first[...].astype(F32)
        joined_ref[:, width:] = second[:, 0:rest].astype(F32)
        out_ref[...] = second[:, rest:].astype(F32).T

    @pl.when(bits_ref[0] == 0)
    def _():
        place(mine_ref, got_ref)

    @pl.when(bits_ref[0] == 1)
    def _():
        place(got_ref, mine_ref)


def ladder(joined, out_keep, out_others, small, sends, early):
    total = lax.axis_size("dp")
    count = total.bit_length() - 1
    bits = (lax.axis_index("dp") >> jnp.arange(count, dtype=jnp.int32)) & 1
    rows, cols = joined.shape
    width = (cols + out_keep.shape[1]) // 2
    rest = list(range(1, count))
    orders = (rest, rest[1:] + rest[:1])
    state = {"step": 0, "small": small, "sends": list(sends), "sent": [], "made": {}}
    flips = [functools.partial(flip_bit, bit=bit) for bit in range(count)] + [flip_tensor]
    first, first_chunk = 2, 1

    def together(values):
        at = state["step"]
        state["step"] += 1
        beside = [state["small"]] if at == 0 else []
        sums, chunk = first <= at < first + len(flips), first_chunk <= at < first_chunk + len(sends)
        if sums:
            beside.append(state["small"] + flips[at - first](state["small"]))
        if chunk:
            beside.append(flip_tensor(state["sends"][at - first_chunk]))
        if at in early:
            beside.append(early[at](state["made"], state["sent"]))
        values, beside = lax.optimization_barrier((values, beside))
        if at == 0:
            state["small"] = beside.pop(0)
        if sums:
            state["small"] = beside.pop(0)
        if chunk:
            state["sent"].append(beside.pop(0))
        if at in early:
            state["made"][at] = beside.pop(0)
        return values

    mine, send = small_call(
        stack_kernel, "stack", bits, (joined, out_keep, *out_others), [((rows, width), BF16)] * 2
    )
    cut = (total, rows // total, width)
    mine, got = together((mine.reshape(cut), flip_core(send.reshape(cut))))
    level = split_sum((orders[0][0], orders[1][0]), bits, mine, got)
    parts = [(level[0], level[1]), (level[2], level[3])]
    for n in range(len(rest)):
        both = together([(parts[p][0], flip_bit(parts[p][1], orders[p][n])) for p in range(2)])
        for p, (mine, got) in enumerate(both):
            if n + 1 < len(rest):
                parts[p] = split_sum((orders[p][n + 1],), bits, mine, got)
            else:
                (parts[p],) = small_call(add_kernel, "add_last", bits, (mine, got), [(mine.shape, BF16)])
    for n in reversed(range(len(rest))):
        both = together([(parts[p], flip_bit(parts[p], orders[p][n])) for p in range(2)])
        if n > 0:
            parts = [merge((orders[p][n],), bits, *both[p]) for p in range(2)]
    mine = merge((orders[0][0], orders[1][0]), bits, *both[0], *both[1])
    got = flip_core(mine)
    outs = [((rows, cols), F32), ((out_keep.shape[1], rows), F32)]
    grads = small_call(
        unstack_kernel, "unstack", bits, (mine.reshape(rows, width), got.reshape(rows, width)), outs
    )
    return grads, state["small"], state["made"]


def shards(
    layer_in,
    qkv_weight,
    qkv_bias,
    key_scorer,
    out_weight,
    out_bias,
    fc_weight,
    fc_bias,
    proj_weight,
    proj_bias,
    norm1_gain,
    norm1_shift,
    norm2_gain,
    norm2_shift,
    key_index,
    key_count,
    out_grad,
):
    side = lax.axis_index("tensor")
    own_rows, width = layer_in.shape
    seq = key_index.shape[0]
    half = own_rows // 2
    blocks = own_rows // QB
    places = jnp.stack([side * blocks, (1 - side) * blocks, side]).astype(jnp.int32)

    starts = (0, half)
    norm_own = [norm_one(layer_in, norm1_gain, norm1_shift, at, half) for at in starts]
    norm_peer = [flip_tensor(rows) for rows in norm_own]
    bits = allowed_bits(key_index, key_count)
    grad_lows = narrow_halves(out_grad)
    scorer = scorer_rows(key_scorer)
    core = lax.axis_index("dp") & 1
    out_half = out_weight.shape[0] // 2
    out_mine = lax.dynamic_slice_in_dim(out_weight, core * out_half, out_half, 0)
    bits, out_mine = lax.optimization_barrier((bits, out_mine))
    out_mine = flip_tensor(out_mine)

    own = qkv_heads(norm_own, qkv_weight, qkv_bias, scorer)
    own, *grad_laters = lax.optimization_barrier((own, *grad_lows))
    grad_peers = [flip_tensor(low) for low in grad_laters]
    qa_own, ka_own, va_own, vt_own, kt_own = own
    state = attend_call(
        attend_start_kernel, "attend_start", places, qa_own, (ka_own, vt_own, bits), blocks, 0, (), True
    )
    state, norm_peer = lax.optimization_barrier((state, norm_peer))
    peer = qkv_heads(norm_peer, qkv_weight, qkv_bias, scorer)
    qa_peer, ka_peer, va_peer, vt_peer, kt_peer = peer
    att_owns, logs_owns, att_sends, logs_sends, att_peers = [], [], [], [], []
    for n in range(blocks):
        att_send, logs_send = attend_call(
            functools.partial(attend_other_kernel, n),
            "attend_other",
            places,
            qa_peer,
            (ka_peer, vt_peer, ka_own, vt_own, bits),
            1,
            n,
        )
        att_own, logs_own = attend_call(
            functools.partial(attend_finish_kernel, n),
            "attend_finish",
            places,
            qa_own,
            (ka_peer, vt_peer, bits),
            1,
            n,
            state,
        )
        if n == 1:
            att_send, att_own, att_peers[0], out_mine = lax.optimization_barrier(
                (att_send, att_own, att_peers[0], out_mine)
            )
            out_other = flip_core(out_mine)
        att_send, att_own, qa_peer, qa_own = lax.optimization_barrier(
            (att_send, att_own, qa_peer, qa_own)
        )
        if n == 0:
            att_send, *grad_peers = lax.optimization_barrier((att_send, *grad_peers))
        att_owns.append(att_own)
        logs_owns.append(logs_own)
        att_sends.append(att_send)
        logs_sends.append(logs_send)
        att_peers.append(flip_tensor(att_send))

    out_peer = jnp.where(
        core == 0,
        jnp.concatenate([out_mine, out_other], axis=0),
        jnp.concatenate([out_other, out_mine], axis=0),
    )

    mixed = None
    normed, normed_peers = [], []
    grad_lows = list(grad_lows)
    for n, at in enumerate(starts):
        mixed, low = mix(
            layer_in,
            att_owns[n],
            att_peers[n],
            out_weight,
            out_peer,
            out_bias,
            norm2_gain,
            norm2_shift,
            at,
            () if mixed is None else ((0, mixed),),
        )
        normed.append(low)
        normed_peers.append(flip_tensor(low))
    active = slopes = None
    backs, back_others, fc_sums = [], [], []
    for n, rows in enumerate(normed + normed_peers):
        active, slopes, back, fc_sum = feed(
            rows,
            (grad_lows + grad_peers)[n],
            fc_weight,
            fc_bias,
            proj_weight,
            F32 if n < 2 else BF16,
            n * half,
            seq,
            () if active is None else ((0, active), (1, slopes)),
        )
        fc_sums.append(fc_sum)
        if n < 2:
            backs.append(back)
        else:
            back_others.append(flip_tensor(back))
    grad_fc_bias = sum(fc_sums[1:], fc_sums[0])
    grad_fc_weight = turned_product(normed + normed_peers, [slopes], "fc_slope")
    grad_proj_weight = turned_product([active], grad_lows + grad_peers, "proj_slope", 512)
    proj_sends = product(active, proj_weight, NN, own_rows, own_rows, BF16, "proj_send", 4)
    mixed, grad_fc_weight, grad_proj_weight = lax.optimization_barrier(
        (mixed, grad_fc_weight, grad_proj_weight)
    )
    grad_mixed = grad_mixed_low = grad_att_own = None
    grad_att_peers, row_sums = [], []
    for n, at in enumerate(starts):
        grad_mixed, grad_mixed_low, grad_att_own, grad_att_send, *some = mix_back(
            mixed,
            backs[n],
            back_others[n],
            out_grad,
            norm2_gain,
            out_weight,
            out_peer,
            at,
            ()
            if grad_mixed is None
            else ((0, grad_mixed), (1, grad_mixed_low), (2, grad_att_own)),
        )
        row_sums.append(some)
        grad_att_peers.append(flip_tensor(grad_att_send))
    grad_norm2_gain, grad_norm2_shift, grad_out_bias, grad_proj_bias = (
        one + two for one, two in zip(*row_sums)
    )

    out_sends = turned_product([grad_mixed_low], att_peers, "out_slope", width // 2, 2)
    out_keep = turned_product([grad_mixed_low], att_owns, "out_slope")
    grad_fc_weight, grad_proj_weight = lax.psum((grad_fc_weight, grad_proj_weight), "dp")
    own_keys, peer_keys = (ka_own, kt_own, va_own), (ka_peer, kt_peer, va_peer)
    out_others = [flip_tensor(rows) for rows in out_sends]
    qa_own, proj_sends, out_sends, out_keep = lax.optimization_barrier(
        (qa_own, proj_sends, out_sends, out_keep)
    )
    proj_others = [flip_tensor(rows) for rows in proj_sends]
    dq_own, *key_sums = attend_back(
        True, places, qa_own, (own_keys, peer_keys), [grad_att_own], att_owns, logs_owns, bits
    )
    swapped = (key_sums[1], key_sums[0], key_sums[3], key_sums[2])
    *_, joined, grad_qkv_bias, grad_key_scorer = attend_back(
        False,
        places,
        qa_peer,
        (peer_keys, own_keys),
        grad_att_peers,
        att_sends,
        logs_sends,
        bits,
        swapped + (dq_own, scorer),
    )
    joined, out_others, proj_others = lax.optimization_barrier((joined, out_others, proj_others))
    grad_qkv_weight = turned_product(norm_own + norm_peer, [joined], "qkv_slope")
    one_sends = product(joined, qkv_weight, NT, own_rows, own_rows, BF16, "one_send", 4)
    (one_own,) = product(joined, qkv_weight, NT, 0, own_rows, F32, "one_own")
    layer_out = layer_end(mixed, active, proj_weight, proj_bias, proj_others, 0, ())
    packed = pack(
        places,
        qkv_weight,
        grad_qkv_weight,
        grad_qkv_bias,
        grad_key_scorer,
        (grad_norm2_gain, grad_norm2_shift, grad_out_bias, grad_proj_bias),
        grad_fc_bias,
    )

    grads, packed, made = ladder(
        grad_qkv_weight,
        out_keep,
        out_others,
        packed,
        one_sends,
        {
            0: lambda made, sent: (grad_fc_weight, grad_proj_weight, one_own, layer_out),
            4: lambda made, sent: made[0][0].astype(F32),
            5: lambda made, sent: made[0][1].astype(F32),
            6: lambda made, sent: norm_one_back(
                layer_in, made[0][2], grad_mixed, norm1_gain, sent
            ),
        },
    )
    grad_qkv_weight, grad_out_weight = grads
    layer_out = made[0][3]
    grad_fc_weight, grad_proj_weight, input_grad = made[4], made[5], made[6]
    joined_cols = qkv_weight.shape[1]

    full = [packed[0, n * width : (n + 1) * width] for n in range(6)]
    grad_norm1_gain = (full[0] - norm1_shift * full[1]) / norm1_gain
    sizes = (joined_cols, key_scorer.shape[0], fc_bias.shape[0])
    halves = lax.dynamic_slice_in_dim(packed[0], 6 * width + side * sum(sizes), sum(sizes), 0)
    ends = (sizes[0], sizes[0] + sizes[1])
    return (
        layer_out,
        input_grad,
        grad_qkv_weight,
        halves[: ends[0]],
        halves[ends[0] : ends[1]],
        grad_out_weight,
        full[4],
        grad_fc_weight,
        halves[ends[1] :],
        grad_proj_weight,
        full[5],
        grad_norm1_gain,
        full[1],
        full[2],
        full[3],
    )


def solution(mesh):
    rows = P(("dp", "tensor"), None)
    in_specs = (
        rows,
        P(None, "tensor"),
        P("tensor"),
        P("tensor"),
        P("tensor", None),
        P(),
        P(None, "tensor"),
        P("tensor"),
        P("tensor", None),
        P(),
        P(),
        P(),
        P(),
        P(),
        P("dp", None),
        P("dp"),
        rows,
    )
    out_specs = (
        rows,
        rows,
        P(None, "tensor"),
        P("tensor"),
        P("tensor"),
        P("tensor", None),
        P(),
        P(None, "tensor"),
        P("tensor"),
        P("tensor", None),
        P(),
        P(),
        P(),
        P(),
        P(),
    )
    return jax.shard_map(shards, mesh=mesh, in_specs=in_specs, out_specs=out_specs, check_vma=False)
```

```python
import functools
import math

import jax
import jax.numpy as jnp
from jax import lax
from jax.experimental import pallas as pl
from jax.experimental.pallas import tpu as pltpu
from jax.sharding import PartitionSpec as P

HD = 64
LANES = 128
WIN = 64
LOG2E = math.log2(math.e)
LN2 = math.log(2.0)
NEG = -1e30
QB = 512
KB = 512
ROWS = 512
VT = 80
NT = (((1,), (1,)), ((), ()))
NN = (((1,), (0,)), ((), ()))
TN = (((0,), (0,)), ((), ()))
F32 = jnp.float32
BF16 = jnp.bfloat16
MIB = 1024 * 1024
SMALL = pl.CostEstimate(flops=1000, bytes_accessed=1000, transcendentals=0)


def dot(a, b, dims=NN):
    return lax.dot_general(a, b, dims, preferred_element_type=F32)


def split3(x):
    hi = x.astype(BF16).astype(F32)
    rest = x - hi
    mid = rest.astype(BF16).astype(F32)
    low = (rest - mid).astype(BF16).astype(F32)
    return hi, mid, low


def lane_ids(rows):
    return lax.broadcasted_iota(jnp.int32, (rows, LANES), 1)


def put3(base, lanes, first, parts):
    out = base
    for n, part in enumerate(parts):
        out = jnp.where(lanes == first + n, part, out)
    return out


def whole_block(array):
    return pl.BlockSpec(memory_space=pltpu.VMEM)


def scorer_rows(key_scorer):
    return jnp.pad(key_scorer.reshape(-1, HD), ((0, 0), (0, LANES - HD)))


def bits_kernel(low_ref, flag_ref, bits_ref):
    width = bits_ref.shape[1]
    first = pl.program_id(0) * width
    lane = lax.broadcasted_iota(jnp.int32, (LANES, width), 0)
    pos = lax.broadcasted_iota(jnp.int32, (LANES, width), 1) + first
    back = (pos - lane) & (LANES - 1)
    at = pos - back
    bits = jnp.where((back < WIN) & (at >= 0), 1 << (jnp.maximum(at, 0) >> 7), 0)
    for slot in range(low_ref.shape[0]):
        hit = low_ref[slot : slot + 1, :] == lane
        bits = bits | jnp.where(hit, flag_ref[slot : slot + 1, :], 0)
    bits_ref[...] = bits


def allowed_bits(key_index, key_count):
    seq = key_index.shape[0]
    index = key_index.T
    slots = index.shape[0]
    slot = lax.broadcasted_iota(jnp.int32, index.shape, 0)
    used = (slot < key_count[None, :]) & (index >= 0)
    low = index & (LANES - 1)
    flag = jnp.where(used, 1 << (jnp.maximum(index, 0) >> 7), 0)
    width = 256
    spec = pl.BlockSpec((slots, width), lambda i: (0, i))
    return pl.pallas_call(
        bits_kernel,
        grid=(seq // width,),
        in_specs=[spec, spec],
        out_specs=pl.BlockSpec((LANES, width), lambda i: (0, i)),
        out_shape=jax.ShapeDtypeStruct((LANES, seq), jnp.int32),
        cost_estimate=SMALL,
        name="allowed_bits",
    )(low, flag)


def fill_bias(bias_ref, bits_ref, q0, k0):
    depth, width = bias_ref.shape
    bits = bits_ref[:, pl.ds(q0, width)]
    for part in range(depth // LANES):
        shift = k0 // LANES + part
        seen = ((bits >> shift) & 1) == 1
        bias_ref[part * LANES : (part + 1) * LANES, :] = jnp.where(seen, 0.0, NEG)


def qkv_kernel(weight_ref, bias_ref, scorer_ref, *refs):
    norm_refs, (qa_ref, ka_ref, va_ref, vt_ref, kt_ref) = refs[:-5], refs[-5:]
    norm = choose(norm_refs, pl.program_id(0))
    rows = norm.shape[0]
    heads = qa_ref.shape[0]
    lanes = lane_ids(rows)
    real = lanes < HD
    ones = jnp.where((lanes >= HD) & (lanes < HD + 3), 1.0, 0.0)
    for pair in range(heads // 2):
        cols = slice(pair * 6 * HD, (pair + 1) * 6 * HD)
        raw = dot(norm, weight_ref[:, cols]) + bias_ref[:, cols]
        raw = raw.astype(BF16).astype(F32)
        blocks = [raw[:, n * LANES : (n + 1) * LANES] for n in range(3)]
        turned = [pltpu.roll(block, HD, 1) for block in blocks]
        groups = (
            (blocks[0], turned[0], blocks[1]),
            (turned[1], blocks[2], turned[2]),
        )
        for side, (query, key, value) in enumerate(groups):
            head = pair * 2 + side
            raw_gate = jnp.sum(key * scorer_ref[head : head + 1, :], axis=1, keepdims=True)
            gate = jnp.minimum(raw_gate, 0.0) - jnp.log1p(jnp.exp(-jnp.abs(raw_gate)))
            key_plain = jnp.where(real, key, 0.0)
            value_ones = jnp.where(real, value, ones)
            qa_ref[head] = jnp.where(real, query * 0.125, ones).astype(BF16)
            ka_ref[head] = put3(key_plain, lanes, HD, split3(gate)).astype(BF16)
            va_ref[head] = value_ones.astype(BF16)
            vt_ref[head] = value_ones.T[:VT, :].astype(BF16)
            kt_ref[head] = key_plain.T[:HD, :].astype(BF16)


def qkv_heads(norm_pieces, weight, bias, scorer):
    rows = ROWS * len(norm_pieces)
    heads = scorer.shape[0]
    cols = weight.shape[1]
    row_shape = jax.ShapeDtypeStruct((heads, rows, LANES), BF16)
    row_block = pl.BlockSpec((heads, ROWS, LANES), lambda i: (0, i, 0))
    bias = bias.reshape(1, cols)
    return pl.pallas_call(
        qkv_kernel,
        grid=(rows // ROWS,),
        in_specs=[whole_block(weight), whole_block(bias), whole_block(scorer)]
        + [chunk_spec(piece) for piece in norm_pieces],
        out_specs=[
            row_block,
            row_block,
            row_block,
            pl.BlockSpec((heads, VT, ROWS), lambda i: (0, 0, i)),
            pl.BlockSpec((heads, HD, ROWS), lambda i: (0, 0, i)),
        ],
        out_shape=[
            row_shape,
            row_shape,
            row_shape,
            jax.ShapeDtypeStruct((heads, VT, rows), BF16),
            jax.ShapeDtypeStruct((heads, HD, rows), BF16),
        ],
        compiler_params=pltpu.CompilerParams(vmem_limit_bytes=14 * MIB),
        cost_estimate=SMALL,
        name="qkv_heads",
    )(weight, bias, scorer, *norm_pieces)


def attend_block(
    place, q_block, k0, qa_ref, ka_ref, vt_ref, bits_ref, bias_ref, total_ref, peak_ref, corner
):
    heads = qa_ref.shape[0]
    depth, first = corner
    queries = slice(first, QB)
    bias = bias_ref.at[0:depth, queries]
    keys = pl.ds(k0, depth)
    fill_bias(bias, bits_ref, q_block * QB + first, place * KB + k0)

    def scores_of(head):
        return dot(ka_ref[head, keys, :], qa_ref[head, queries, :], NT)

    ahead = scores_of(0)
    for head in range(heads):
        scores = ahead
        if head + 1 < heads:
            ahead = scores_of(head + 1)
        scores = scores * LOG2E + bias[...]
        old = peak_ref[head, :, queries]
        new = jnp.maximum(old, jnp.max(scores, axis=0, keepdims=True))
        weights = jnp.exp2(scores - new[0:1])
        shrink = jnp.exp2(old - new)
        peak_ref[head, :, queries] = new
        part = dot(vt_ref[head, :, keys], weights.astype(BF16))
        total_ref[head, :, queries] = total_ref[head, :, queries] * shrink[0:1] + part


def attend_blocks(count, place, q_block, *refs):
    def step(j, carry):
        k0 = pl.multiple_of(j * KB, KB)
        attend_block(place, q_block, k0, *refs, (KB, 0))
        return carry

    lax.fori_loop(0, count, step, 0)


def attend_diagonal(n, place, q_block, *refs):
    half = KB // 2
    k0 = pl.multiple_of(n * KB, KB)
    attend_block(place, q_block, k0, *refs, (half, 0))
    attend_block(place, q_block, pl.multiple_of(k0 + half, half), *refs, (half, half))


def attend_open(total_ref, peak_ref):
    total_ref[...] = jnp.zeros_like(total_ref)
    peak_ref[...] = jnp.full_like(peak_ref, NEG)


def attend_end(total_ref, peak_ref, out_ref, log_ref):
    heads = total_ref.shape[0]
    for pair in range(heads // 2):
        sides = []
        for head in (2 * pair, 2 * pair + 1):
            mass = total_ref[head, HD : HD + 1, :]
            sides.append(total_ref[head, 0:HD, :] / mass)
            log_ref[head] = peak_ref[head] + jnp.log(mass) * LOG2E
        both = jnp.concatenate(sides, axis=0).T
        out_ref[:, pair * LANES : (pair + 1) * LANES] = both.astype(BF16)


def attend_start_kernel(
    places_ref, qa_ref, ka_ref, vt_ref, bits_ref, total_ref, peak_ref, bias_ref
):
    own = places_ref[0]
    n = pl.program_id(0)
    refs = (qa_ref, ka_ref, vt_ref, bits_ref, bias_ref, total_ref, peak_ref)
    attend_open(total_ref, peak_ref)
    attend_blocks(n, own, own + n, *refs)
    attend_diagonal(n, own, own + n, *refs)


def attend_finish_kernel(
    n,
    places_ref,
    qa_ref,
    ka_ref,
    vt_ref,
    bits_ref,
    total_in_ref,
    peak_in_ref,
    out_ref,
    log_ref,
    bias_ref,
    total_ref,
    peak_ref,
):
    own, peer, later = places_ref[0], places_ref[1], places_ref[2]
    refs = (qa_ref, ka_ref, vt_ref, bits_ref, bias_ref, total_ref, peak_ref)
    total_ref[...] = total_in_ref[...]
    peak_ref[...] = peak_in_ref[...]
    attend_blocks(later * (ka_ref.shape[1] // KB), peer, own + n, *refs)
    attend_end(total_ref, peak_ref, out_ref, log_ref)


def attend_other_kernel(
    n,
    places_ref,
    qa_ref,
    ka_ref,
    vt_ref,
    ka_own_ref,
    vt_own_ref,
    bits_ref,
    out_ref,
    log_ref,
    bias_ref,
    total_ref,
    peak_ref,
):
    own, peer, later = places_ref[0], places_ref[1], places_ref[2]
    block = peer + n
    tail = (bits_ref, bias_ref, total_ref, peak_ref)
    attend_open(total_ref, peak_ref)
    for at in range(n):
        attend_block(peer, block, at * KB, qa_ref, ka_ref, vt_ref, *tail, (KB, 0))
    attend_diagonal(n, peer, block, qa_ref, ka_ref, vt_ref, *tail)
    earlier = (1 - later) * (ka_own_ref.shape[1] // KB)
    attend_blocks(earlier, own, block, qa_ref, ka_own_ref, vt_own_ref, *tail)
    attend_end(total_ref, peak_ref, out_ref, log_ref)


def attend_call(kernel, name, places, qa, others, count, first, state=(), keep=False):
    heads = qa.shape[0]
    total_spec = pl.BlockSpec((heads, VT, QB), lambda i, _: (0, 0, first + i))
    peak_spec = pl.BlockSpec((heads, 8, QB), lambda i, _: (0, 0, first + i))
    log_spec = pl.BlockSpec((heads, 8, QB), lambda i, _: (0, 0, i))
    total_shape = jax.ShapeDtypeStruct((heads, VT, count * QB), F32)
    peak_shape = jax.ShapeDtypeStruct((heads, 8, count * QB), F32)
    scratch = [
        pltpu.VMEM((KB, QB), F32),
        pltpu.VMEM((heads, VT, QB), F32),
        pltpu.VMEM((heads, 8, QB), F32),
    ]
    if keep:
        out_specs, out_shape = [total_spec, peak_spec], [total_shape, peak_shape]
        scratch = scratch[:1]
    else:
        out_specs = [pl.BlockSpec((QB, heads * HD), lambda i, _: (i, 0)), log_spec]
        out_shape = [jax.ShapeDtypeStruct((count * QB, heads * HD), BF16), peak_shape]
    return pl.pallas_call(
        kernel,
        grid_spec=pltpu.PrefetchScalarGridSpec(
            num_scalar_prefetch=1,
            grid=(count,),
            in_specs=[pl.BlockSpec((heads, QB, LANES), lambda i, _: (0, first + i, 0))]
            + [whole_block(array) for array in others]
            + ([total_spec, peak_spec] if state else []),
            out_specs=out_specs,
            scratch_shapes=scratch,
        ),
        out_shape=out_shape,
        compiler_params=pltpu.CompilerParams(vmem_limit_bytes=16 * MIB),
        cost_estimate=SMALL,
        name=name,
    )(places, qa, *others, *state)


def in_vmem():
    return pl.BlockSpec(memory_space=pltpu.VMEM)


def attend_back_kernel(
    own_queries,
    places_ref,
    qa_ref,
    ka_refs,
    kt_refs,
    va_refs,
    grad_refs,
    att_refs,
    log_refs,
    bits_ref,
    dq_ref,
    dk_refs,
    dv_refs,
    bias_ref,
    ga_ref,
):
    heads, rows, _ = qa_ref.shape
    blocks = rows // QB
    lanes = lane_ids(ROWS)
    dq_ref[...] = jnp.zeros_like(dq_ref)
    if own_queries:
        for ref in tuple(dk_refs) + tuple(dv_refs):
            ref[...] = jnp.zeros_like(ref)

    for n in range(len(att_refs)):
        rows_n = slice(n * ROWS, (n + 1) * ROWS)
        grad_rows = grad_refs[n] if len(grad_refs) > 1 else grad_refs[0].at[rows_n, :]
        for pair in range(heads // 2):
            cols = slice(pair * LANES, (pair + 1) * LANES)
            grad = grad_rows[:, cols].astype(F32)
            prod = grad * att_refs[n][:, cols].astype(F32)
            turned = pltpu.roll(grad, HD, 1)
            for side, values in enumerate((grad, turned)):
                mine = (lanes < HD) if side == 0 else (lanes >= HD)
                inner = jnp.sum(jnp.where(mine, prod, 0.0), axis=1, keepdims=True)
                plain = jnp.where(lanes < HD, values, 0.0)
                filled = put3(plain, lanes, HD, split3(-inner))
                ga_ref[pair * 2 + side, rows_n, :] = filled.astype(BF16)

    q_place, k_places = places_ref[0], (places_ref[0], places_ref[1])
    later = places_ref[2]
    if not own_queries:
        q_place, k_places = k_places[1], (k_places[1], k_places[0])
        later = 1 - later

    def tile(piece, j, n, i, corner):
        depth, first = corner
        width = QB - first
        k1 = pl.multiple_of(j * KB + first, KB // 2)
        q1 = pl.multiple_of(i * QB + first, QB // 2)
        keys = pl.ds(k1, depth)
        queries = pl.ds(q1, width)
        bias = bias_ref.at[0:depth, 0:width]
        fill_bias(bias, bits_ref, q_place * QB + q1, k_places[piece] * KB + k1)
        ka_ref, kt_ref, va_ref = ka_refs[piece], kt_refs[piece], va_refs[piece]
        dk_ref, dv_ref = dk_refs[piece], dv_refs[piece]

        def first_of(head):
            qa = qa_ref[head, queries, :]
            ga = ga_ref[head, queries, :]
            return (
                qa,
                ga,
                dot(ka_ref[head, keys, :], qa, NT),
                dot(va_ref[head, keys, :], ga, NT),
            )

        ahead = first_of(0)
        for head in range(heads):
            qa, ga, scores, inner = ahead
            if head + 1 < heads:
                ahead = first_of(head + 1)
            scores = scores * LOG2E + bias[...]
            if isinstance(n, int):
                logs = log_refs[n][head, 0:1, first:QB]
            else:
                logs = jnp.where(n == 0, log_refs[0][head, 0:1, :], log_refs[1][head, 0:1, :])
            probs = jnp.exp2(scores - logs)
            slopes = (probs * inner).astype(BF16)
            dv_ref[head, keys, :] += dot(probs.astype(BF16), ga)
            dk_ref[head, keys, :] += dot(slopes, qa)
            dq_ref[head, :, queries] += dot(kt_ref[head, :, keys], slopes)

    half = KB // 2
    for n in range(blocks):
        tile(0, n, n, n, (half, 0))
        tile(0, n, n, n, (half, half))
        for j in range(n):
            tile(0, j, n, n, (KB, 0))

    def step(at, carry):
        i = at & (blocks - 1)
        tile(1, at // blocks, i, i, (KB, 0))
        return carry

    lax.fori_loop(0, later * (blocks * blocks), step, 0)


def join_piece(first, scorer_ref, dq_ref, dk_ref, dv_ref, ka_ref, joined_ref, bias_out_ref, scorer_out_ref):
    heads, rows, _ = dk_ref.shape
    span = 256
    lanes = lane_ids(span)
    real = lanes < HD

    def step(at, carry):
        here = pl.ds(pl.multiple_of(at * span, span), span)
        there = pl.ds(pl.multiple_of(at * span + first, span), span)
        for pair in range(heads // 2):
            dq = dq_ref[2 * pair : 2 * pair + 2, :, here].reshape(LANES, span).T * 0.125
            dks, dvs = [], []
            for head in (2 * pair, 2 * pair + 1):
                scorer = scorer_ref[head : head + 1, :]
                key = ka_ref[head, here, :].astype(F32)
                dk = dk_ref[head, here, :]
                raw_gate = jnp.sum(key * scorer, axis=1, keepdims=True)
                slope = dk[:, HD : HD + 1] / (1.0 + jnp.exp(raw_gate))
                scorer_out_ref[head : head + 1, :] += sum_rows(slope * key)
                dks.append(dk + slope * scorer)
                dvs.append(dv_ref[head, here, :])
            blocks = (
                jnp.where(real, dq, pltpu.roll(dks[0], HD, 1)),
                jnp.where(real, dvs[0], dq),
                jnp.where(real, dks[1], pltpu.roll(dvs[1], HD, 1)),
            )
            for n, block in enumerate(blocks):
                cols = slice((pair * 3 + n) * LANES, (pair * 3 + n + 1) * LANES)
                bias_out_ref[:, cols] += sum_rows(block)
                joined_ref[there, cols] = block.astype(BF16)
        return carry

    lax.fori_loop(0, rows // span, step, 0)


def attend_back(own_queries, places, qa, keys, grads, atts, logs, bits, sums=None):
    heads, rows, _ = qa.shape
    count = len(atts)
    inputs = [places, qa]
    for kind in range(3):
        inputs += [keys[0][kind], keys[1][kind]]
    inputs += list(grads) + list(atts) + list(logs) + [bits]
    given = len(inputs)
    aliases = {}
    dq_shape = jax.ShapeDtypeStruct((heads, HD, rows), F32)
    sum_shapes = [jax.ShapeDtypeStruct((heads, rows, LANES), F32)] * 4
    out_shape = [dq_shape] + sum_shapes
    scratch = [pltpu.VMEM((KB, QB), F32), pltpu.VMEM((heads, rows, LANES), BF16)]
    if not own_queries:
        aliases = {given + n: n for n in range(4)}
        inputs += list(sums)
        cols = 3 * HD * heads
        out_shape = sum_shapes + [
            jax.ShapeDtypeStruct((2 * rows, cols), BF16),
            jax.ShapeDtypeStruct((1, cols), F32),
            jax.ShapeDtypeStruct((heads, LANES), F32),
        ]
        scratch.append(pltpu.VMEM((heads, HD, rows), F32))

    def kernel(*refs):
        places_ref, qa_ref = refs[:2]
        pairs = [refs[2 + 2 * n : 4 + 2 * n] for n in range(3)]
        ends = [8, 8 + len(grads), 8 + len(grads) + count, 8 + len(grads) + 2 * count]
        lists = [refs[start:stop] for start, stop in zip(ends[:-1], ends[1:])]
        bits_ref = refs[ends[-1]]
        outs = refs[len(inputs) :]
        if own_queries:
            dq_ref, dk0, dk1, dv0, dv1, bias_ref, ga_ref = outs
        else:
            dk0, dk1, dv0, dv1, joined_ref, bias_out_ref, scorer_out_ref = outs[:7]
            bias_ref, ga_ref, dq_ref = outs[7:]
        attend_back_kernel(
            own_queries,
            places_ref,
            qa_ref,
            *pairs,
            *lists,
            bits_ref,
            dq_ref,
            (dk0, dk1),
            (dv0, dv1),
            bias_ref,
            ga_ref,
        )
        if not own_queries:
            dq_own_ref, scorer_ref = refs[given + 4 : given + 6]
            bias_out_ref[...] = jnp.zeros_like(bias_out_ref)
            scorer_out_ref[...] = jnp.zeros_like(scorer_out_ref)
            ends = (joined_ref, bias_out_ref, scorer_out_ref)
            join_piece(rows, scorer_ref, dq_ref, dk0, dv0, pairs[0][0], *ends)
            join_piece(0, scorer_ref, dq_own_ref, dk1, dv1, pairs[0][1], *ends)

    return pl.pallas_call(
        kernel,
        in_specs=[pl.BlockSpec(memory_space=pltpu.SMEM)] + [in_vmem()] * (len(inputs) - 1),
        out_specs=[in_vmem()] * len(out_shape),
        out_shape=out_shape,
        scratch_shapes=scratch,
        input_output_aliases=aliases,
        compiler_params=pltpu.CompilerParams(vmem_limit_bytes=16 * MIB),
        cost_estimate=SMALL,
        name="attend_back",
    )(*inputs)


def turned_product(parts, others, name, tile=256, chunks=1):
    across = parts[0].shape[1]
    width = others[0].shape[1]
    lengths = [part.shape[0] for part in parts]
    sizes = [other.shape[0] for other in others]
    cuts = sorted({sum(lengths[:n]) for n in range(len(lengths) + 1)} | {sum(sizes[:n]) for n in range(len(sizes) + 1)})

    def rows_of(refs, counts, start, stop):
        base = 0
        for ref, count in zip(refs, counts):
            if base <= start < base + count:
                return ref[start - base : stop - base, :]
            base += count

    def kernel(*refs):
        out_refs = refs[-chunks:]
        lefts, rights = refs[: len(parts)], refs[len(parts) : -chunks]
        total = None
        for start, stop in zip(cuts[:-1], cuts[1:]):
            left = rows_of(lefts, lengths, start, stop)
            part = dot(left, rows_of(rights, sizes, start, stop), TN)
            total = part if total is None else total + part
        value = total.astype(BF16)
        if chunks == 1:
            out_refs[0][...] = value
            return
        for n, ref in enumerate(out_refs):

            @pl.when(pl.program_id(0) == n)
            def _():
                ref[...] = value

    out = pl.pallas_call(
        kernel,
        grid=(across // tile,),
        in_specs=[pl.BlockSpec((n, tile), lambda i: (0, i)) for n in lengths]
        + [whole_block(other) for other in others],
        out_specs=[pl.BlockSpec((tile, width), lambda i: (i if chunks == 1 else 0, 0))] * chunks,
        out_shape=[jax.ShapeDtypeStruct((across // chunks, width), BF16)] * chunks,
        compiler_params=pltpu.CompilerParams(vmem_limit_bytes=20 * MIB),
        cost_estimate=SMALL,
        name=name,
    )(*parts, *others)
    return out[0] if chunks == 1 else out


def choose(refs, at):
    value = refs[0][...]
    for n in range(1, len(refs)):
        value = jnp.where(at == n, refs[n][...], value)
    return value


def chunk_spec(array):
    return pl.BlockSpec(array.shape, lambda i: (0, 0))


def product(rows, weight, dims, first, count, kind, name, chunks=1):
    depth = rows.shape[1]
    width = weight.shape[1] if dims == NN else weight.shape[0]
    span = count // max(chunks, 2)
    shape = (count // chunks, width)

    def kernel(rows_ref, weight_ref, *out_refs):
        value = dot(rows_ref[...], weight_ref[...], dims).astype(kind)
        if chunks == 1:
            out_refs[0][...] = value
            return
        for n, ref in enumerate(out_refs):

            @pl.when(pl.program_id(0) == n)
            def _():
                ref[...] = value

    return pl.pallas_call(
        kernel,
        grid=(count // span,),
        in_specs=[
            pl.BlockSpec((span, depth), lambda i: (first // span + i, 0)),
            whole_block(weight),
        ],
        out_specs=[pl.BlockSpec((span, width), lambda i: (i if chunks == 1 else 0, 0))] * chunks,
        out_shape=[jax.ShapeDtypeStruct(shape, kind)] * chunks,
        compiler_params=pltpu.CompilerParams(vmem_limit_bytes=16 * MIB),
        cost_estimate=SMALL,
        name=name,
    )(rows, weight)


def end_kernel(mixed_ref, active_ref, weight_ref, bias_ref, *refs):
    other = choose(refs[:-1], pl.program_id(0)).astype(F32)
    own = dot(active_ref[...], weight_ref[...])
    refs[-1][...] = mixed_ref[...] + (own + other) + bias_ref[...]


def layer_end(mixed, active, weight, bias, others, start, earlier):
    total, width = mixed.shape
    span, units = others[0].shape[0], weight.shape[0]
    bias = bias.reshape(1, width)
    (out,) = rows_call(
        end_kernel,
        "layer_end",
        span * len(others),
        (mixed, active, weight, bias, *others),
        [
            row_spec(width, span, start // span),
            row_spec(units, span, start // span),
            whole_block(weight),
            whole_block(bias),
        ]
        + [chunk_spec(other) for other in others],
        [(False, width, F32, total, start)],
        0,
        span=span,
        earlier=earlier,
    )
    return out


def pack_kernel(side_ref, weight_ref, joined_ref, bias_ref, scorer_ref, *refs):
    fulls, (fc_ref, out_ref) = refs[:-2], refs[-2:]
    width = fulls[0].shape[1]
    weight = weight_ref[...]
    ones = jnp.ones((8, weight.shape[1]), BF16)
    wide = weight.astype(F32) * joined_ref[...].astype(F32)
    times = sum(dot(ones, part.astype(BF16), NT) for part in split3(wide))
    rows = jnp.broadcast_to(bias_ref[...], (8, weight.shape[1]))
    plain = sum(dot(part.astype(BF16), weight, NT) for part in split3(rows))
    out_ref[...] = jnp.zeros_like(out_ref)
    at = 0
    for value in [times[0:1], plain[0:1]] + [ref[...] for ref in fulls]:
        out_ref[:, at : at + width] = value
        at += width
    heads = scorer_ref.shape[0]
    real = lane_ids(1) < HD
    pairs = []
    for pair in range(heads // 2):
        one, two = scorer_ref[2 * pair : 2 * pair + 1, :], scorer_ref[2 * pair + 1 : 2 * pair + 2, :]
        pairs.append(jnp.where(real, one, pltpu.roll(two, HD, 1)))
    halves = [bias_ref[...]] + pairs + [fc_ref[...]]
    total = sum(half.shape[1] for half in halves)
    for side in range(2):

        @pl.when(side_ref[2] == side)
        def _():
            start = at + side * total
            for half in halves:
                out_ref[:, start : start + half.shape[1]] = half
                start += half.shape[1]


def pack(places, weight, joined, bias, scorer, fulls, fc):
    inputs = (places, weight, joined, bias, scorer, *fulls, fc)
    heads = scorer.shape[0]
    total = (2 + len(fulls)) * weight.shape[0] + 2 * (
        bias.shape[1] + heads * HD + fc.shape[1]
    )
    return pl.pallas_call(
        pack_kernel,
        in_specs=[pl.BlockSpec(memory_space=pltpu.SMEM)] + [in_vmem()] * (len(inputs) - 1),
        out_specs=in_vmem(),
        out_shape=jax.ShapeDtypeStruct((1, total), F32),
        compiler_params=pltpu.CompilerParams(vmem_limit_bytes=16 * MIB),
        cost_estimate=SMALL,
        name="pack",
    )(*inputs)


SPAN = 256


def normalize(values):
    center = values - jnp.mean(values, axis=-1, keepdims=True)
    scale = lax.rsqrt(jnp.mean(center * center, axis=-1, keepdims=True) + 1e-05)
    return center * scale, scale


def norm_back(slope, hat, scale):
    means = jnp.mean(slope, axis=-1, keepdims=True)
    inner = jnp.mean(slope * hat, axis=-1, keepdims=True)
    return (slope - means - hat * inner) * scale


def row_spec(width, span=SPAN, skip=0):
    return pl.BlockSpec((span, width), lambda i, *_: (i + skip, 0))


def sum_rows(values):
    return jnp.sum(values, axis=0, keepdims=True)


def start_at_zero(*refs):
    @pl.when(pl.program_id(0) == 0)
    def _():
        for ref in refs:
            ref[...] = jnp.zeros_like(ref)


def rows_call(
    kernel, name, rows, inputs, in_specs, outs, flops, span=SPAN, earlier=(), limit=16
):
    aliases = {}
    body = kernel
    if earlier:
        first = len(inputs)
        aliases = {first + n: at for n, (at, _) in enumerate(earlier)}
        skip_from, skip_count = first, len(earlier)
        inputs = tuple(inputs) + tuple(array for _, array in earlier)
        in_specs = list(in_specs) + [pl.BlockSpec(memory_space=pl.ANY)] * len(earlier)

        def body(*refs):
            kernel(*refs[:skip_from], *refs[skip_from + skip_count :])

    return pl.pallas_call(
        body,
        grid=(rows // span,),
        in_specs=in_specs,
        out_specs=[
            pl.BlockSpec((1, width), lambda i, *_: (0, 0))
            if one
            else row_spec(width, span, start // span)
            for one, width, _, _, start in outs
        ],
        out_shape=[
            jax.ShapeDtypeStruct((1 if one else total, width), kind)
            for one, width, kind, total, _ in outs
        ],
        input_output_aliases=aliases,
        compiler_params=pltpu.CompilerParams(vmem_limit_bytes=limit * MIB),
        cost_estimate=SMALL,
        name=name,
    )(*inputs)


def norm_one_kernel(in_ref, gain_ref, shift_ref, out_ref):
    hat, _ = normalize(in_ref[...])
    gain = gain_ref[...].reshape(1, gain_ref.shape[0])
    shift = shift_ref[...].reshape(1, shift_ref.shape[0])
    out_ref[...] = (hat * gain + shift).astype(BF16)


def norm_one(layer_in, gain, shift, start, rows):
    width = layer_in.shape[1]
    (out,) = rows_call(
        norm_one_kernel,
        "norm_one",
        rows,
        (layer_in, gain, shift),
        [row_spec(width, skip=start // SPAN), in_vmem(), in_vmem()],
        [(False, width, BF16, rows, 0)],
        rows * width * 8,
        limit=60,
    )
    return out


def narrow_kernel(first_ref, second_ref, out_first_ref, out_second_ref):
    out_first_ref[...] = first_ref[...].astype(BF16)
    out_second_ref[...] = second_ref[...].astype(BF16)


def narrow_halves(values):
    rows, width = values.shape
    half = rows // 2
    return rows_call(
        narrow_kernel,
        "narrow",
        half,
        (values, values),
        [row_spec(width), row_spec(width, skip=half // SPAN)],
        [(False, width, BF16, half, 0)] * 2,
        rows * width,
        limit=60,
    )


def mix_kernel(
    in_ref, own_ref, peer_ref, w_own_ref, w_peer_ref, bias_ref, gain_ref, shift_ref, mixed_ref, norm_ref
):
    part = dot(own_ref[...], w_own_ref[...]) + dot(peer_ref[...], w_peer_ref[...])
    mixed = in_ref[...] + part + bias_ref[...]
    mixed_ref[...] = mixed
    hat, _ = normalize(mixed)
    norm_ref[...] = (hat * gain_ref[...] + shift_ref[...]).astype(BF16)


def mix(layer_in, own, peer, w_own, w_peer, bias, gain, shift, start, earlier):
    total, width = layer_in.shape
    rows, depth = peer.shape
    skip = start // SPAN
    vector = pl.BlockSpec((1, width), lambda i: (0, 0))
    return rows_call(
        mix_kernel,
        "mix",
        rows,
        (layer_in, own, peer, w_own, w_peer)
        + tuple(v.reshape(1, width) for v in (bias, gain, shift)),
        [
            row_spec(width, skip=skip),
            row_spec(depth),
            row_spec(depth),
            whole_block(w_own),
            whole_block(w_peer),
        ]
        + [vector] * 3,
        [(False, width, F32, total, start), (False, width, BF16, rows, 0)],
        rows * width * depth * 4,
        earlier=earlier,
        limit=60,
    )


def feed_kernel(
    norm_ref, grad_ref, fc_ref, bias_ref, proj_ref, active_ref, slope_ref, back_ref, sum_ref
):
    start_at_zero(sum_ref)
    units = fc_ref.shape[1]
    step = 512
    total = None
    for at in range(0, units, step):
        cols = slice(at, at + step)
        hidden = dot(norm_ref[...], fc_ref[:, cols]) + bias_ref[:, cols]
        grad = dot(grad_ref[...], proj_ref[cols, :], NT)
        square = hidden * hidden
        bend = jnp.tanh(hidden * (0.7978845608 + 0.7978845608 * 0.044715 * square))
        half = 0.5 + 0.5 * bend
        active_ref[:, cols] = (hidden * half).astype(BF16)
        inner = 0.7978845608 + 3.0 * 0.7978845608 * 0.044715 * square
        slope = grad * (half + 0.5 * hidden * (1.0 - bend * bend) * inner)
        low = slope.astype(BF16)
        slope_ref[:, cols] = low
        sum_ref[:, cols] += sum_rows(slope)
        part = dot(low, fc_ref[:, cols], NT)
        total = part if total is None else total + part
    back_ref[...] = total.astype(back_ref.dtype)


def feed(norm_rows, grad_rows, fc, bias, proj, back_kind, start, total, earlier):
    rows, width = norm_rows.shape
    units = fc.shape[1]
    bias = bias.reshape(1, units)
    return rows_call(
        feed_kernel,
        "feed",
        rows,
        (norm_rows, grad_rows, fc, bias, proj),
        [
            row_spec(width),
            row_spec(width),
            whole_block(fc),
            whole_block(bias),
            whole_block(proj),
        ],
        [
            (False, units, BF16, total, start),
            (False, units, BF16, total, start),
            (False, width, back_kind, rows, 0),
            (True, units, F32, 1, 0),
        ],
        rows * width * units * 6,
        earlier=earlier,
    )


def mix_back_kernel(
    mixed_ref,
    own_ref,
    other_ref,
    grad_ref,
    gain_ref,
    w_own_ref,
    w_peer_ref,
    out_ref,
    low_ref,
    att_own_ref,
    att_peer_ref,
    gain_out_ref,
    shift_out_ref,
    mixed_out_ref,
    grad_out_ref,
):
    start_at_zero(gain_out_ref, shift_out_ref, mixed_out_ref, grad_out_ref)
    hat, scale = normalize(mixed_ref[...])
    slope = own_ref[...] + other_ref[...].astype(F32)
    gain_out_ref[...] += sum_rows(slope * hat)
    shift_out_ref[...] += sum_rows(slope)
    grad = grad_ref[...]
    grad_out_ref[...] += sum_rows(grad)
    out = grad + norm_back(slope * gain_ref[...], hat, scale)
    mixed_out_ref[...] += sum_rows(out)
    out_ref[...] = out
    low = out.astype(BF16)
    low_ref[...] = low
    att_own_ref[...] = dot(low, w_own_ref[...], NT).astype(BF16)
    att_peer_ref[...] = dot(low, w_peer_ref[...], NT).astype(BF16)


def mix_back(mixed, own, other, grad, gain, w_own, w_peer, start, earlier):
    total, width = mixed.shape
    rows = other.shape[0]
    depth = w_own.shape[0]
    gain = gain.reshape(1, width)
    wide = row_spec(width)
    later = row_spec(width, skip=start // SPAN)
    return rows_call(
        mix_back_kernel,
        "mix_back",
        rows,
        (mixed, own, other, grad, gain, w_own, w_peer),
        [later, wide, wide, later, whole_block(gain), whole_block(w_own), whole_block(w_peer)],
        [
            (False, width, F32, total, start),
            (False, width, BF16, total, start),
            (False, depth, BF16, total, start),
            (False, depth, BF16, rows, 0),
            (True, width, F32, 1, 0),
            (True, width, F32, 1, 0),
            (True, width, F32, 1, 0),
            (True, width, F32, 1, 0),
        ],
        rows * width * depth * 4,
        earlier=earlier,
        limit=60,
    )


def norm_one_back_kernel(in_ref, own_ref, grad_ref, gain_ref, *refs):
    hat, scale = normalize(in_ref[...])
    other = choose(refs[:-1], pl.program_id(0)).astype(F32)
    slope = (own_ref[...] + other) * gain_ref[...]
    refs[-1][...] = grad_ref[...] + norm_back(slope, hat, scale)


def norm_one_back(layer_in, own, grad, gain, others):
    rows, width = layer_in.shape
    span = others[0].shape[0]
    gain = gain.reshape(1, width)
    return pl.pallas_call(
        norm_one_back_kernel,
        grid=(rows // span,),
        in_specs=[row_spec(width, span)] * 3
        + [whole_block(gain)]
        + [chunk_spec(other) for other in others],
        out_specs=row_spec(width, span),
        out_shape=jax.ShapeDtypeStruct((rows, width), F32),
        compiler_params=pltpu.CompilerParams(vmem_limit_bytes=16 * MIB),
        cost_estimate=SMALL,
        name="norm_one_back",
    )(layer_in, own, grad, gain, *others)


def flip_bit(values, bit):
    total = lax.axis_size("dp")
    return lax.ppermute(values, "dp", [(n, n ^ (1 << bit)) for n in range(total)])


def flip_core(values):
    return flip_bit(values, 0)


def flip_tensor(values):
    return lax.ppermute(values, "tensor", [(0, 1), (1, 0)])


def small_call(kernel, name, bits, inputs, outs):
    return pl.pallas_call(
        kernel,
        in_specs=[pl.BlockSpec(memory_space=pltpu.SMEM)] + [in_vmem()] * len(inputs),
        out_specs=[in_vmem()] * len(outs),
        out_shape=[jax.ShapeDtypeStruct(shape, kind) for shape, kind in outs],
        compiler_params=pltpu.CompilerParams(vmem_limit_bytes=16 * MIB),
        cost_estimate=SMALL,
        name=name,
    )(bits, *inputs)


def added(one_ref, two_ref, at, count):
    here = pl.ds(at, count)
    return (one_ref[here].astype(F32) + two_ref[here].astype(F32)).astype(BF16)


def stack_kernel(bits_ref, joined_ref, keep_ref, *refs):
    other_refs, (mine_ref, send_ref) = refs[:-2], refs[-2:]
    width = mine_ref.shape[1]
    rest = joined_ref.shape[1] - width
    step = other_refs[0].shape[0]

    def place(first, second):
        first[...] = joined_ref[:, 0:width]
        second[:, 0:rest] = joined_ref[:, width:]
        for n, other_ref in enumerate(other_refs):
            here = slice(n * step, (n + 1) * step)
            out = keep_ref[here, :].astype(F32) + other_ref[...].astype(F32)
            second[here, rest:] = out.astype(BF16)

    @pl.when(bits_ref[0] == 0)
    def _():
        place(mine_ref, send_ref)

    @pl.when(bits_ref[0] == 1)
    def _():
        place(send_ref, mine_ref)


def split_kernel(places, bits_ref, mine_ref, got_ref, *outs):
    step = mine_ref.shape[0] // (2 * len(places))
    for n, bit in enumerate(places):
        mine = bits_ref[bit]
        base = 2 * n * step
        outs[2 * n][...] = added(mine_ref, got_ref, base + mine * step, step)
        outs[2 * n + 1][...] = added(mine_ref, got_ref, base + (1 - mine) * step, step)


def split_sum(places, bits, mine, got):
    pieces, rows, cols = mine.shape
    shape = ((pieces // (2 * len(places)), rows, cols), BF16)
    return small_call(
        functools.partial(split_kernel, places), "split_sum", bits, (mine, got), [shape] * (2 * len(places))
    )


def add_kernel(bits_ref, mine_ref, got_ref, out_ref):
    out_ref[...] = added(mine_ref, got_ref, 0, mine_ref.shape[0])


def merge_kernel(places, bits_ref, *refs):
    out_ref = refs[-1]
    step = refs[0].shape[0]
    for n, bit in enumerate(places):
        mine = bits_ref[bit]
        base = 2 * n * step
        out_ref[pl.ds(base + mine * step, step)] = refs[2 * n][...]
        out_ref[pl.ds(base + (1 - mine) * step, step)] = refs[2 * n + 1][...]


def merge(places, bits, *inputs):
    pieces, rows, cols = inputs[0].shape
    shape = ((2 * len(places) * pieces, rows, cols), BF16)
    (out,) = small_call(
        functools.partial(merge_kernel, places), "merge", bits, inputs, [shape]
    )
    return out


def unstack_kernel(bits_ref, mine_ref, got_ref, joined_ref, out_ref):
    width = mine_ref.shape[1]
    rest = joined_ref.shape[1] - width

    def place(first, second):
        joined_ref[:, 0:width] = first[...].astype(F32)
        joined_ref[:, width:] = second[:, 0:rest].astype(F32)
        out_ref[...] = second[:, rest:].astype(F32).T

    @pl.when(bits_ref[0] == 0)
    def _():
        place(mine_ref, got_ref)

    @pl.when(bits_ref[0] == 1)
    def _():
        place(got_ref, mine_ref)


def ladder(joined, out_keep, out_others, small, sends, early):
    total = lax.axis_size("dp")
    count = total.bit_length() - 1
    bits = (lax.axis_index("dp") >> jnp.arange(count, dtype=jnp.int32)) & 1
    rows, cols = joined.shape
    width = (cols + out_keep.shape[1]) // 2
    rest = list(range(1, count))
    orders = (rest, rest[1:] + rest[:1])
    state = {"step": 0, "small": small, "sends": list(sends), "sent": [], "made": {}}
    flips = [functools.partial(flip_bit, bit=bit) for bit in range(count)] + [flip_tensor]
    first, first_chunk = 1, 1

    def together(values):
        at = state["step"]
        state["step"] += 1
        beside = [state["small"]] if at == 0 else []
        sums, chunk = first <= at < first + len(flips), first_chunk <= at < first_chunk + len(sends)
        if sums:
            beside.append(state["small"] + flips[at - first](state["small"]))
        if chunk:
            beside.append(flip_tensor(state["sends"][at - first_chunk]))
        if at in early:
            beside.append(early[at](state["made"], state["sent"]))
        values, beside = lax.optimization_barrier((values, beside))
        if at == 0:
            state["small"] = beside.pop(0)
        if sums:
            state["small"] = beside.pop(0)
        if chunk:
            state["sent"].append(beside.pop(0))
        if at in early:
            state["made"][at] = beside.pop(0)
        return values

    mine, send = small_call(
        stack_kernel, "stack", bits, (joined, out_keep, *out_others), [((rows, width), BF16)] * 2
    )
    cut = (total, rows // total, width)
    mine, got = together((mine.reshape(cut), flip_core(send.reshape(cut))))
    level = split_sum((orders[0][0], orders[1][0]), bits, mine, got)
    parts = [(level[0], level[1]), (level[2], level[3])]
    for n in range(len(rest)):
        both = together([(parts[p][0], flip_bit(parts[p][1], orders[p][n])) for p in range(2)])
        for p, (mine, got) in enumerate(both):
            if n + 1 < len(rest):
                parts[p] = split_sum((orders[p][n + 1],), bits, mine, got)
            else:
                (parts[p],) = small_call(add_kernel, "add_last", bits, (mine, got), [(mine.shape, BF16)])
    for n in reversed(range(len(rest))):
        both = together([(parts[p], flip_bit(parts[p], orders[p][n])) for p in range(2)])
        if n > 0:
            parts = [merge((orders[p][n],), bits, *both[p]) for p in range(2)]
    mine = merge((orders[0][0], orders[1][0]), bits, *both[0], *both[1])
    got = flip_core(mine)
    outs = [((rows, cols), F32), ((out_keep.shape[1], rows), F32)]
    grads = small_call(
        unstack_kernel, "unstack", bits, (mine.reshape(rows, width), got.reshape(rows, width)), outs
    )
    return grads, state["small"], state["made"]


def shards(
    layer_in,
    qkv_weight,
    qkv_bias,
    key_scorer,
    out_weight,
    out_bias,
    fc_weight,
    fc_bias,
    proj_weight,
    proj_bias,
    norm1_gain,
    norm1_shift,
    norm2_gain,
    norm2_shift,
    key_index,
    key_count,
    out_grad,
):
    side = lax.axis_index("tensor")
    own_rows, width = layer_in.shape
    seq = key_index.shape[0]
    half = own_rows // 2
    blocks = own_rows // QB
    places = jnp.stack([side * blocks, (1 - side) * blocks, side]).astype(jnp.int32)

    starts = (0, half)
    norm_own = [norm_one(layer_in, norm1_gain, norm1_shift, at, half) for at in starts]
    norm_peer = [flip_tensor(rows) for rows in norm_own]
    bits = allowed_bits(key_index, key_count)
    grad_lows = narrow_halves(out_grad)
    scorer = scorer_rows(key_scorer)
    core = lax.axis_index("dp") & 1
    out_half = out_weight.shape[0] // 2
    out_mine = lax.dynamic_slice_in_dim(out_weight, core * out_half, out_half, 0)
    bits, out_mine = lax.optimization_barrier((bits, out_mine))
    out_mine = flip_tensor(out_mine)

    own = qkv_heads(norm_own, qkv_weight, qkv_bias, scorer)
    own, *grad_laters = lax.optimization_barrier((own, *grad_lows))
    grad_peers = [flip_tensor(low) for low in grad_laters]
    qa_own, ka_own, va_own, vt_own, kt_own = own
    state = attend_call(
        attend_start_kernel, "attend_start", places, qa_own, (ka_own, vt_own, bits), blocks, 0, (), True
    )
    state, norm_peer = lax.optimization_barrier((state, norm_peer))
    peer = qkv_heads(norm_peer, qkv_weight, qkv_bias, scorer)
    qa_peer, ka_peer, va_peer, vt_peer, kt_peer = peer
    att_owns, logs_owns, att_sends, logs_sends, att_peers = [], [], [], [], []
    for n in range(blocks):
        att_send, logs_send = attend_call(
            functools.partial(attend_other_kernel, n),
            "attend_other",
            places,
            qa_peer,
            (ka_peer, vt_peer, ka_own, vt_own, bits),
            1,
            n,
        )
        att_own, logs_own = attend_call(
            functools.partial(attend_finish_kernel, n),
            "attend_finish",
            places,
            qa_own,
            (ka_peer, vt_peer, bits),
            1,
            n,
            state,
        )
        if n == 1:
            att_send, att_own, att_peers[0], out_mine = lax.optimization_barrier(
                (att_send, att_own, att_peers[0], out_mine)
            )
            out_other = flip_core(out_mine)
        att_send, att_own, qa_peer, qa_own = lax.optimization_barrier(
            (att_send, att_own, qa_peer, qa_own)
        )
        if n == 0:
            att_send, *grad_peers = lax.optimization_barrier((att_send, *grad_peers))
        att_owns.append(att_own)
        logs_owns.append(logs_own)
        att_sends.append(att_send)
        logs_sends.append(logs_send)
        att_peers.append(flip_tensor(att_send))

    out_peer = jnp.where(
        core == 0,
        jnp.concatenate([out_mine, out_other], axis=0),
        jnp.concatenate([out_other, out_mine], axis=0),
    )

    mixed = None
    normed, normed_peers = [], []
    grad_lows = list(grad_lows)
    for n, at in enumerate(starts):
        mixed, low = mix(
            layer_in,
            att_owns[n],
            att_peers[n],
            out_weight,
            out_peer,
            out_bias,
            norm2_gain,
            norm2_shift,
            at,
            () if mixed is None else ((0, mixed),),
        )
        normed.append(low)
        normed_peers.append(flip_tensor(low))
    active = slopes = None
    backs, back_others, fc_sums = [], [], []
    for n, rows in enumerate(normed + normed_peers):
        active, slopes, back, fc_sum = feed(
            rows,
            (grad_lows + grad_peers)[n],
            fc_weight,
            fc_bias,
            proj_weight,
            F32 if n < 2 else BF16,
            n * half,
            seq,
            () if active is None else ((0, active), (1, slopes)),
        )
        fc_sums.append(fc_sum)
        if n < 2:
            backs.append(back)
        else:
            back_others.append(flip_tensor(back))
    grad_fc_bias = sum(fc_sums[1:], fc_sums[0])
    grad_fc_weight = turned_product(normed + normed_peers, [slopes], "fc_slope")
    grad_proj_weight = turned_product([active], grad_lows + grad_peers, "proj_slope", 512)
    proj_sends = product(active, proj_weight, NN, own_rows, own_rows, BF16, "proj_send", 4)
    mixed, grad_fc_weight, grad_proj_weight = lax.optimization_barrier(
        (mixed, grad_fc_weight, grad_proj_weight)
    )
    grad_mixed = grad_mixed_low = grad_att_own = None
    grad_att_peers, row_sums = [], []
    for n, at in enumerate(starts):
        grad_mixed, grad_mixed_low, grad_att_own, grad_att_send, *some = mix_back(
            mixed,
            backs[n],
            back_others[n],
            out_grad,
            norm2_gain,
            out_weight,
            out_peer,
            at,
            ()
            if grad_mixed is None
            else ((0, grad_mixed), (1, grad_mixed_low), (2, grad_att_own)),
        )
        row_sums.append(some)
        grad_att_peers.append(flip_tensor(grad_att_send))
    grad_norm2_gain, grad_norm2_shift, grad_out_bias, grad_proj_bias = (
        one + two for one, two in zip(*row_sums)
    )

    out_sends = turned_product([grad_mixed_low], att_peers, "out_slope", width // 2, 2)
    out_keep = turned_product([grad_mixed_low], att_owns, "out_slope")
    grad_fc_weight, grad_proj_weight = lax.psum((grad_fc_weight, grad_proj_weight), "dp")
    own_keys, peer_keys = (ka_own, kt_own, va_own), (ka_peer, kt_peer, va_peer)
    out_others = [flip_tensor(rows) for rows in out_sends]
    qa_own, proj_sends, out_sends, out_keep = lax.optimization_barrier(
        (qa_own, proj_sends, out_sends, out_keep)
    )
    proj_others = [flip_tensor(rows) for rows in proj_sends]
    dq_own, *key_sums = attend_back(
        True, places, qa_own, (own_keys, peer_keys), [grad_att_own], att_owns, logs_owns, bits
    )
    swapped = (key_sums[1], key_sums[0], key_sums[3], key_sums[2])
    *_, joined, grad_qkv_bias, grad_key_scorer = attend_back(
        False,
        places,
        qa_peer,
        (peer_keys, own_keys),
        grad_att_peers,
        att_sends,
        logs_sends,
        bits,
        swapped + (dq_own, scorer),
    )
    joined, out_others, proj_others = lax.optimization_barrier((joined, out_others, proj_others))
    grad_qkv_weight = turned_product(norm_own + norm_peer, [joined], "qkv_slope")
    one_sends = product(joined, qkv_weight, NT, own_rows, own_rows, BF16, "one_send", 4)
    (one_own,) = product(joined, qkv_weight, NT, 0, own_rows, F32, "one_own")
    layer_out = layer_end(mixed, active, proj_weight, proj_bias, proj_others, 0, ())
    packed = pack(
        places,
        qkv_weight,
        grad_qkv_weight,
        grad_qkv_bias,
        grad_key_scorer,
        (grad_norm2_gain, grad_norm2_shift, grad_out_bias, grad_proj_bias),
        grad_fc_bias,
    )

    grads, packed, made = ladder(
        grad_qkv_weight,
        out_keep,
        out_others,
        packed,
        one_sends,
        {
            0: lambda made, sent: (grad_fc_weight, grad_proj_weight, one_own, layer_out),
            4: lambda made, sent: made[0][0].astype(F32),
            5: lambda made, sent: made[0][1].astype(F32),
            6: lambda made, sent: norm_one_back(
                layer_in, made[0][2], grad_mixed, norm1_gain, sent
            ),
        },
    )
    grad_qkv_weight, grad_out_weight = grads
    layer_out = made[0][3]
    grad_fc_weight, grad_proj_weight, input_grad = made[4], made[5], made[6]
    joined_cols = qkv_weight.shape[1]

    full = [packed[0, n * width : (n + 1) * width] for n in range(6)]
    grad_norm1_gain = (full[0] - norm1_shift * full[1]) / norm1_gain
    sizes = (joined_cols, key_scorer.shape[0], fc_bias.shape[0])
    halves = lax.dynamic_slice_in_dim(packed[0], 6 * width + side * sum(sizes), sum(sizes), 0)
    ends = (sizes[0], sizes[0] + sizes[1])
    return (
        layer_out,
        input_grad,
        grad_qkv_weight,
        halves[: ends[0]],
        halves[ends[0] : ends[1]],
        grad_out_weight,
        full[4],
        grad_fc_weight,
        halves[ends[1] :],
        grad_proj_weight,
        full[5],
        grad_norm1_gain,
        full[1],
        full[2],
        full[3],
    )


def solution(mesh):
    rows = P(("dp", "tensor"), None)
    in_specs = (
        rows,
        P(None, "tensor"),
        P("tensor"),
        P("tensor"),
        P("tensor", None),
        P(),
        P(None, "tensor"),
        P("tensor"),
        P("tensor", None),
        P(),
        P(),
        P(),
        P(),
        P(),
        P("dp", None),
        P("dp"),
        rows,
    )
    out_specs = (
        rows,
        rows,
        P(None, "tensor"),
        P("tensor"),
        P("tensor"),
        P("tensor", None),
        P(),
        P(None, "tensor"),
        P("tensor"),
        P("tensor", None),
        P(),
        P(),
        P(),
        P(),
        P(),
    )
    return jax.shard_map(shards, mesh=mesh, in_specs=in_specs, out_specs=out_specs, check_vma=False)
```
